128 devices in a mesh: dp: 32 (over z_hi, y, x), head: 2 (over core), tensor: 2 (over z_lo).
Axes of the slice: x: 4, y: 4, z: 4 (z_hi: 2, z_lo: 2; z = z_hi * 2 + z_lo), core: 2. Of those that a mesh axis runs over, the one named last changes fastest.
Arguments:
- tokens: bfloat16 [4096, 2048], P('dp'), may hold values from -6 to 6
- gain_attn: bfloat16 [2048], P('dp'), may hold values from 0.5 to 1.5
- w_query: bfloat16 [2048, 2048], P('dp', 'head'), may hold values from -0.125 to 0.125
- w_key: bfloat16 [2048, 512], P('dp', 'head'), may hold values from -0.125 to 0.125
- w_value: bfloat16 [2048, 512], P('dp', 'head'), may hold values from -0.125 to 0.125
- gain_query: bfloat16 [64], replicated, may hold values from 0.5 to 1.5
- gain_key: bfloat16 [64], replicated, may hold values from 0.5 to 1.5
- w_out: bfloat16 [2048, 2048], P('dp', 'head'), may hold values from -0.75 to 0.75
- gain_ffn: bfloat16 [2048], P('dp'), may hold values from 0.5 to 1.5
- w_gate: bfloat16 [2048, 8192], P('dp', 'tensor'), may hold values from -0.125 to 0.125
- w_up: bfloat16 [2048, 8192], P('dp', 'tensor'), may hold values from -0.125 to 0.125
- w_down: bfloat16 [2048, 8192], P('dp', 'tensor'), may hold values from -0.0625 to 0.0625
- cotangent: bfloat16 [4096, 2048], P('dp'), may hold values from -6 to 6
Outputs:
- output: bfloat16 [4096, 2048], P('dp')
- token_input_gradient: float32 [4096, 2048], P('dp')
- attention_gain_gradient: float32 [2048], P('dp')
- grad_query: float32 [2048, 2048], P('dp', 'head')
- grad_key: float32 [2048, 512], P('dp', 'head')
- grad_value: float32 [2048, 512], P('dp', 'head')
- grad_gain_query: float32 [64], replicated
- grad_gain_key: float32 [64], replicated
- grad_out: float32 [2048, 2048], P('dp', 'head')
- feedforward_gain_gradient: float32 [2048], P('dp')
- grad_gate: float32 [2048, 8192], P('dp', 'tensor')
- grad_up: float32 [2048, 8192], P('dp', 'tensor')
- grad_down: float32 [2048, 8192], P('dp', 'tensor')
The draws below stay inside these ranges and needn't reach their ends.
All inputs are finite; a program needn't handle non-finite values.
Results may differ from the reference program's by a relative error of at most 0.028.
Values may be sent and summed in bfloat16 or wider, within the bound.
A program may use at most 192 MiB of HBM per device.

```python
import jax
import jax.numpy as jnp
from jax import lax

D = 2048
H = 32
KV = 8
HD = 64
FF = 8192
TOK_DEV = 128
TOKENS = 4096
N_DP = 32


def level_of(own_key, shape, cuts, least, largest):
    factor_of, own = 1.0, jax.random.fold_in(own_key, 6)
    for axis_at, parts in cuts:
        draws = jnp.exp(jax.random.uniform(jax.random.fold_in(own, axis_at), (parts,), jnp.float32, least / len(cuts), largest / len(cuts)))
        factor_of = factor_of * jnp.repeat(draws, shape[axis_at] // parts).reshape([-1 if axis == axis_at else 1 for axis in range(len(shape))])
    return factor_of


def noise(rng, shape, spread, reach, cuts=(), kind=jnp.bfloat16):
    gain = level_of(rng, shape, cuts, -0.22, 0.18) if cuts else 1.0
    values = jax.random.normal(rng, shape, jnp.float32) * spread * gain
    return jnp.minimum(jnp.maximum(values, -reach), reach).astype(kind)


def setup_inputs(seed: int = 0) -> dict:
    arg_keys = jax.random.split(jax.random.key(seed), 14)
    return {
        "tokens": noise(arg_keys[0], (TOKENS, D), 1.0, 6.0, ((0, 32),)),
        "gain_attn": jnp.clip(1.0 + 0.1 * jax.random.normal(arg_keys[1], (D,), jnp.float32), 0.5, 1.5).astype(jnp.bfloat16),
        "w_query": noise(arg_keys[2], (D, H * HD), D ** -0.5, 0.125, ((0, 32), (1, 2))),
        "w_key": noise(arg_keys[3], (D, KV * HD), D ** -0.5, 0.125, ((0, 32), (1, 2))),
        "w_value": noise(arg_keys[4], (D, KV * HD), D ** -0.5, 0.125, ((0, 32), (1, 2))),
        "gain_query": jnp.clip(1.0 + 0.1 * jax.random.normal(arg_keys[5], (HD,), jnp.float32), 0.5, 1.5).astype(jnp.bfloat16),
        "gain_key": jnp.clip(1.0 + 0.1 * jax.random.normal(arg_keys[6], (HD,), jnp.float32), 0.5, 1.5).astype(jnp.bfloat16),
        "w_out": noise(arg_keys[7], (D, H * HD), (H * HD // 32) ** -0.5, 0.75, ((0, 32), (1, 2))),
        "gain_ffn": jnp.clip(1.0 + 0.1 * jax.random.normal(arg_keys[8], (D,), jnp.float32), 0.5, 1.5).astype(jnp.bfloat16),
        "w_gate": noise(arg_keys[9], (D, FF), D ** -0.5, 0.125, ((0, 32), (1, 2))),
        "w_up": noise(arg_keys[10], (D, FF), D ** -0.5, 0.125, ((0, 32), (1, 2))),
        "w_down": noise(arg_keys[11], (D, FF), FF ** -0.5, 0.0625, ((0, 32), (1, 2))),
        "cotangent": noise(arg_keys[12], (TOKENS, D), 1.0, 6.0, ((0, 32),)),
    }


@jax.custom_vjp
def low(v):
    return lax.optimization_barrier(v.astype(jnp.bfloat16)).astype(jnp.float32)

@jax.custom_vjp
def low_back(v):
    return v

def low_keep(v):
    return (low(v), None)

def low_pass(kept, grad):
    return (grad,)

def back_keep(v):
    return (v, None)

def back_low(kept, grad):
    return (low(grad),)
low.defvjp(low_keep, low_pass)
low_back.defvjp(back_keep, back_low)
eps = 1e-05
theta_base = 1000000.0

def mult(left, right):
    return jnp.dot(left, right, precision=lax.Precision.HIGHEST, preferred_element_type=jnp.float32)

def mult_rows(left, right):
    return jnp.dot(left, right.T, precision=lax.Precision.HIGHEST, preferred_element_type=jnp.float32)

def rms_scale(value, norm_gain):
    return value * lax.rsqrt(lax.optimization_barrier(jnp.mean(value * value, axis=-1, keepdims=True)) + eps) * norm_gain

def tables(seq, depth):
    half = depth // 2
    position = jnp.arange(seq, dtype=jnp.float32)
    inverse = theta_base ** (-(jnp.arange(half, dtype=jnp.float32) * 2.0) / depth)
    angles = position[:, None] * inverse[None, :]
    return (jnp.cos(angles)[:, None, :], jnp.sin(angles)[:, None, :])

def rotate(value, cosine, sine):
    half = value.shape[-1] // 2
    first = value[..., :half]
    second = value[..., half:]
    return jnp.concatenate([first * cosine - second * sine, second * cosine + first * sine], axis=-1)

def block(x, gain_attn, w_query, w_key, w_value, gain_query, gain_key, w_out, gain_ffn, w_gate, w_up, w_down):
    seq = x.shape[0]
    scale = HD ** (-0.5)
    cosine, sine = tables(seq, HD)
    first_normed_rows = low(rms_scale(x, gain_attn))
    q_raw = low_back(mult(first_normed_rows, w_query)).reshape(seq, H, HD)
    k_raw = low_back(mult(first_normed_rows, w_key)).reshape(seq, KV, HD)
    values = low(low_back(mult(first_normed_rows, w_value))).reshape(seq, KV, HD)
    queries = low(rotate(rms_scale(q_raw, gain_query), cosine, sine)).reshape(seq, KV, H // KV, HD)
    keys = low(rotate(rms_scale(k_raw, gain_key), cosine, sine))
    scores = low_back(jnp.einsum('skgd,tkd->kgst', queries, keys, precision=lax.Precision.HIGHEST) * scale)
    causal = jnp.arange(seq)[:, None] >= jnp.arange(seq)[None, :]
    scores = jnp.where(causal, scores, -1e+30)
    top = lax.optimization_barrier(jnp.max(scores, axis=-1, keepdims=True))
    expo = jnp.exp(scores - top)
    probs = low(expo / lax.optimization_barrier(jnp.sum(expo, axis=-1, keepdims=True)))
    attn = jnp.einsum('kgst,tkd->skgd', probs, values, precision=lax.Precision.HIGHEST).reshape(seq, H * HD)
    attn = low(low_back(attn))
    hidden_state = x + low_back(mult_rows(attn, w_out))
    second_normed_rows = low(rms_scale(hidden_state, gain_ffn))
    gate = low_back(mult(second_normed_rows, w_gate))
    up_proj = low_back(mult(second_normed_rows, w_up))
    active = low(gate * jax.nn.sigmoid(gate) * up_proj)
    return hidden_state + mult_rows(active, w_down)

def reference(tokens, gain_attn, w_query, w_key, w_value, gain_query, gain_key, w_out, gain_ffn, w_gate, w_up, w_down, cotangent):
    weights = tuple((w.astype(jnp.float32) for w in (gain_attn, w_query, w_key, w_value, gain_query, gain_key, w_out, gain_ffn, w_gate, w_up, w_down)))
    input_rows = tokens.astype(jnp.float32).reshape(N_DP, TOK_DEV, D)
    cotans = cotangent.astype(jnp.float32).reshape(N_DP, TOK_DEV, D)

    def one_sequence(carry, pair):
        seq_in, seq_cot = pair
        result, pull = jax.vjp(block, seq_in, *weights)
        grads = pull(seq_cot)
        summed = tuple((c + g for c, g in zip(carry, grads[1:])))
        return (summed, (result.astype(jnp.bfloat16), grads[0]))
    start = tuple((jnp.zeros(w.shape, jnp.float32) for w in weights))
    sums, (outputs, grad_in) = lax.scan(one_sequence, start, (input_rows, cotans))
    return (outputs.reshape(TOKENS, D), grad_in.reshape(TOKENS, D), sums[0], sums[1], sums[2], sums[3], sums[4], sums[5], sums[6], sums[7], sums[8], sums[9], sums[10])
```

```python
import functools

import jax
import jax.numpy as jnp
import numpy as np
from jax import lax
from jax.experimental import pallas as pl
from jax.experimental.pallas import tpu as pltpu
from jax.sharding import PartitionSpec as P

BF = jnp.bfloat16
F32 = jnp.float32
MESH = pl.DeviceIdType.MESH
EPS = 1e-05
THETA = 1000000.0
VMEM_BYTES = 60 << 20
ATT_SPLIT = 640


def nn(a, b):
    return lax.dot_general(a, b, (((1,), (0,)), ((), ())), preferred_element_type=F32)


def nt(a, b):
    return lax.dot_general(a, b, (((1,), (1,)), ((), ())), preferred_element_type=F32)


def tn(a, b):
    return lax.dot_general(a, b, (((0,), (0,)), ((), ())), preferred_element_type=F32)


class Place:
    def __init__(self):
        dp = lax.axis_index("dp")
        self.c = lax.axis_index("head")
        self.zl = lax.axis_index("tensor")
        self.zh = lax.div(dp, 16)
        self.y = lax.rem(lax.div(dp, 4), 4)
        self.x = lax.rem(dp, 4)
        self.z = self.zh * 2 + self.zl

    def at(self, zh=None, y=None, x=None, c=None, zl=None):
        zh = self.zh if zh is None else zh
        y = self.y if y is None else y
        x = self.x if x is None else x
        return (zh * 16 + y * 4 + x, self.c if c is None else c, self.zl if zl is None else zl)

    def step(self, axis, by):
        if axis == "x":
            return self.at(x=lax.rem(self.x + by + 4, 4))
        if axis == "y":
            return self.at(y=lax.rem(self.y + by + 4, 4))
        z = lax.rem(self.z + by + 4, 4)
        return self.at(zh=lax.div(z, 2), zl=lax.rem(z, 2))

    def core(self):
        return self.at(c=1 - self.c)

    def zl_pair(self):
        return self.at(zl=1 - self.zl)

    def zh_pair(self):
        return self.at(zh=1 - self.zh)

    def ring(self, axis):
        return {"x": self.x, "y": self.y, "z": self.z}[axis]


class Net:
    def __init__(self, send_sems, recv_sems):
        self.send_sems = send_sems
        self.recv_sems = recv_sems
        self.count = 0
        self.left = []

    def send(self, src, dst, device):
        k = self.count
        assert k < self.send_sems.shape[0]
        self.count += 1
        copy = pltpu.make_async_remote_copy(
            src_ref=src,
            dst_ref=dst,
            send_sem=self.send_sems.at[k],
            recv_sem=self.recv_sems.at[k],
            device_id=device,
            device_id_type=MESH,
        )
        copy.start()
        self.left.append(copy)
        return copy

    def wait_send(self, copy):
        copy.wait_send()
        self.left = [other for other in self.left if other is not copy]

    def drain(self):
        for copy in self.left:
            copy.wait_send()


def greet(devices):
    barrier = pltpu.get_barrier_semaphore()
    for device in devices:
        pl.semaphore_signal(barrier, inc=1, device_id=device, device_id_type=MESH)
    pl.semaphore_wait(barrier, len(devices))


def together(*pipelines):
    live = list(pipelines)
    while live:
        for pipe in list(live):
            try:
                next(pipe)
            except StopIteration:
                live.remove(pipe)
        yield


def interleave(*pipelines):
    for _ in together(*pipelines):
        pass


def local(pairs, sems):
    copies = [pltpu.make_async_copy(s, d, sems.at[i]) for i, (s, d) in enumerate(pairs)]
    for copy in copies:
        copy.start()
    for copy in copies:
        copy.wait()


def add_refs(dst, srcs, rows=32):
    lead, height = dst.shape[:-2], dst.shape[-2]
    rows = min(rows, height)
    per = height // rows
    count = int(np.prod(lead, dtype=np.int64)) * per

    def body(t, carry):
        r = lax.rem(t, per)
        rest = lax.div(t, per)
        index = []
        for size in reversed(lead):
            index.insert(0, lax.rem(rest, size))
            rest = lax.div(rest, size)
        at = tuple(index) + (pl.ds(r * rows, rows), slice(None))
        total = srcs[0][at].astype(F32)
        for src in srcs[1:]:
            total = total + src[at].astype(F32)
        dst[at] = total.astype(dst.dtype)
        return carry

    lax.fori_loop(0, count, body, 0)


def ring_gather(net, place, axis, view):
    i = place.ring(axis)
    before, after = lax.rem(i + 3, 4), lax.rem(i + 1, 4)
    up, down = place.step(axis, 1), place.step(axis, -1)
    u0 = net.send(view(i, 0), view(i, 0), up)
    d1 = net.send(view(i, 1), view(i, 1), down)
    u1 = net.send(view(i, 1), view(i, 1), up)
    d0 = net.send(view(i, 0), view(i, 0), down)
    yield
    u0.wait_recv()
    f0 = net.send(view(before, 0), view(before, 0), up)
    d1.wait_recv()
    f1 = net.send(view(after, 1), view(after, 1), down)
    yield
    for copy in (u1, d0, f0, f1):
        copy.wait_recv()


def ring_reduce(net, place, axis, view, far, near, out):
    i = place.ring(axis)
    before, after, across = lax.rem(i + 3, 4), lax.rem(i + 1, 4), lax.rem(i + 2, 4)
    up, down = place.step(axis, 1), place.step(axis, -1)
    f0 = net.send(view(across, 0), far.at[0], up)
    f1 = net.send(view(across, 1), far.at[1], down)
    u1 = net.send(view(after, 1), near.at[1], up)
    d0 = net.send(view(before, 0), near.at[2], down)
    yield
    f0.wait_recv()
    add_refs(far.at[0], [far.at[0], view(after, 0)])
    u0 = net.send(far.at[0], near.at[0], up)
    f1.wait_recv()
    add_refs(far.at[1], [far.at[1], view(before, 1)])
    d1 = net.send(far.at[1], near.at[3], down)
    yield
    u1.wait_recv()
    d0.wait_recv()
    u0.wait_recv()
    d1.wait_recv()
    add_refs(out(0), [view(i, 0), near.at[0], near.at[2]])
    add_refs(out(1), [view(i, 1), near.at[1], near.at[3]])


def halves(ref, part):
    return ref.at[..., pl.ds(part * 1024, 1024)]


def torus_gather(net, place, buf):
    x, z, c = place.x, place.z, place.c

    def first():
        yield from ring_gather(
            net, place, "x", lambda i, p: buf.at[z, i, c, pl.ds(0, 16), pl.ds(p * 1024, 1024)]
        )
        yield
        yield from ring_gather(
            net, place, "z", lambda i, p: buf.at[i, :, c, pl.ds(0, 16), pl.ds(p * 1024, 1024)]
        )

    def second():
        yield from ring_gather(
            net, place, "z", lambda i, p: buf.at[i, x, c, pl.ds(16, 16), pl.ds(p * 1024, 1024)]
        )
        yield
        yield from ring_gather(
            net, place, "x", lambda i, p: buf.at[:, i, c, pl.ds(16, 16), pl.ds(p * 1024, 1024)]
        )

    yield from together(first(), second())
    swap = net.send(buf.at[:, :, c], buf.at[:, :, c], place.core())
    yield
    swap.wait_recv()


TORUS_SCRATCH = [
    pltpu.VMEM((4, 4, 32, 2048), BF),
    pltpu.VMEM((2, 4, 16, 1024), BF),
    pltpu.VMEM((4, 4, 16, 1024), BF),
    pltpu.VMEM((2, 4, 16, 1024), BF),
    pltpu.VMEM((2, 16, 1024), BF),
    pltpu.VMEM((4, 16, 1024), BF),
    pltpu.VMEM((2, 4, 16, 1024), BF),
    pltpu.VMEM((4, 4, 16, 1024), BF),
    pltpu.VMEM((2, 4, 16, 1024), BF),
    pltpu.VMEM((2, 16, 1024), BF),
    pltpu.VMEM((4, 16, 1024), BF),
]


def torus_reduce(net, place, src, scratch, out):
    both, far_a, near_a, mid_a, far_a2, near_a2, far_b, near_b, mid_b, far_b2, near_b2 = scratch
    x, z, c = place.x, place.z, place.c
    swap = net.send(src.at[:, :, 1 - c], both, place.core())
    yield
    swap.wait_recv()
    add_refs(both, [both, src.at[:, :, c]])

    def first():
        yield from ring_reduce(
            net, place, "z",
            lambda i, p: both.at[i, :, pl.ds(0, 16), pl.ds(p * 1024, 1024)],
            far_a, near_a, lambda p: mid_a.at[p],
        )
        yield
        yield from ring_reduce(
            net, place, "x",
            lambda i, p: mid_a.at[p, i],
            far_a2, near_a2, lambda p: out.at[pl.ds(0, 16), pl.ds(p * 1024, 1024)],
        )

    def second():
        yield from ring_reduce(
            net, place, "x",
            lambda i, p: both.at[:, i, pl.ds(16, 16), pl.ds(p * 1024, 1024)],
            far_b, near_b, lambda p: mid_b.at[p],
        )
        yield
        yield from ring_reduce(
            net, place, "z",
            lambda i, p: mid_b.at[p, i],
            far_b2, near_b2, lambda p: out.at[pl.ds(16, 16), pl.ds(p * 1024, 1024)],
        )

    yield from together(first(), second())


def quad_gather(net, place, buf):
    c, zl = place.c, place.zl
    own = buf.at[pl.ds(c * 64 + zl * 32, 32)]
    one = net.send(own, own, place.zl_pair())
    yield
    one.wait_recv()
    half = buf.at[pl.ds(c * 64, 64)]
    two = net.send(half, half, place.core())
    yield
    two.wait_recv()


def quad_reduce(net, place, src, from_core, from_zl, tmp):
    c, zl = place.c, place.zl
    one = net.send(src.at[pl.ds((1 - c) * 64, 64)], from_core, place.core())
    yield
    one.wait_recv()
    theirs = src[pl.ds(c * 64 + (1 - zl) * 32, 32), :].astype(F32)
    tmp[...] = (theirs + from_core[pl.ds((1 - zl) * 32, 32), :].astype(F32)).astype(BF)
    two = net.send(tmp, from_zl, place.zl_pair())
    yield
    two.wait_recv()


def quad_total(place, src, from_core, from_zl):
    c, zl = place.c, place.zl
    mine = src[pl.ds(c * 64 + zl * 32, 32), :].astype(F32)
    mine = mine + from_core[pl.ds(zl * 32, 32), :].astype(F32)
    return mine + from_zl[...].astype(F32)


def sem_scratch(n):
    return [pltpu.SemaphoreType.DMA((n,)), pltpu.SemaphoreType.DMA((n,))]


def params(collective_id=None):
    if collective_id is None:
        return pltpu.CompilerParams(vmem_limit_bytes=VMEM_BYTES)
    return pltpu.CompilerParams(
        vmem_limit_bytes=VMEM_BYTES, collective_id=collective_id, has_side_effects=True
    )


ANY = pl.BlockSpec(memory_space=pl.ANY)
VM = pl.BlockSpec(memory_space=pltpu.VMEM)


def gather_kernel(
    wq, wk, wv, wo, wg, wu, wd, cot, gains,
    att, ffn, cots, all_gains,
    send_sems, recv_sems, sems,
):
    me = Place()
    zh, y, x, c, zl, z = me.zh, me.y, me.x, me.c, me.zl, me.z
    greet(
        [me.step("x", 1), me.step("x", 2), me.step("x", -1)]
        + [me.step("y", 1), me.step("y", 2), me.step("y", -1)]
        + [me.step("z", 1), me.step("z", 2), me.step("z", -1)]
        + [me.core()]
        + [me.at(zh=1 - zh, x=lax.rem(x + k, 4)) for k in (1, 2, 3)]
    )
    net = Net(send_sems, recv_sems)

    def piece(k):
        return pl.ds(pl.multiple_of(k * 512 + c * 256, 256), 256)

    own = att.at[zh, y, x]
    local(
        [
            (wq.at[:, pl.ds(pl.multiple_of(zl * 512, 512), 512)], own.at[:, pl.ds(0, 512)]),
            (wk.at[:, pl.ds(pl.multiple_of(zl * 128, 128), 128)], own.at[:, pl.ds(512, 128)]),
            (wv.at[:, pl.ds(pl.multiple_of(zl * 128, 128), 128)], own.at[:, pl.ds(640, 128)]),
            (wo.at[:, pl.ds(pl.multiple_of(zl * 512, 512), 512)], own.at[:, pl.ds(768, 512)]),
            (gains, all_gains.at[zh, y, x]),
            (cot.at[pl.ds(c * 64 + zl * 32, 32)], cots.at[z, x, c]),
            (wg.at[:, piece(zh * 4 + x)], ffn.at[0, zh, y, x]),
            (wu.at[:, piece(zh * 4 + x)], ffn.at[1, zh, y, x]),
            (wd.at[:, piece(zh * 4 + x)], ffn.at[2, zh, y, x]),
        ],
        sems,
    )

    def attention():
        swap = net.send(own, own, me.zh_pair())
        yield
        swap.wait_recv()
        a, b = pl.ds(0, ATT_SPLIT), pl.ds(ATT_SPLIT, 1280 - ATT_SPLIT)

        def first():
            yield from ring_gather(net, me, "x", lambda i, p: att.at[p, y, i, :, a])
            yield
            yield from ring_gather(net, me, "y", lambda i, p: att.at[p, i, :, :, a])

        def second():
            yield from ring_gather(net, me, "y", lambda i, p: att.at[p, i, x, :, b])
            yield
            yield from ring_gather(net, me, "x", lambda i, p: att.at[p, :, i, :, b])

        yield from together(first(), second())

    def feed_forward():
        arrivals = []
        for dz in (0, 1):
            for dx in range(4):
                if dz == 0 and dx == 0:
                    continue
                tx = lax.rem(x + dx, 4)
                tz = 1 - zh if dz else zh
                for m, w in enumerate((wg, wu, wd)):
                    arrivals.append(
                        net.send(
                            w.at[:, piece(tz * 4 + tx)],
                            ffn.at[m, zh, y, x],
                            me.at(zh=tz, x=tx),
                        )
                    )
        yield
        for copy in arrivals:
            copy.wait_recv()
        yield from ring_gather(net, me, "y", lambda i, p: ffn.at[:, p, i])

    def small():
        steps = [
            (all_gains.at[zh, y, x], me.zh_pair()),
            (all_gains.at[:, y, x], me.at(x=x + 1 - 2 * lax.rem(x, 2))),
            (all_gains.at[:, y, pl.ds(2 * lax.div(x, 2), 2)], me.step("x", 2)),
            (all_gains.at[:, y], me.at(y=y + 1 - 2 * lax.rem(y, 2))),
            (all_gains.at[:, pl.ds(2 * lax.div(y, 2), 2)], me.step("y", 2)),
        ]
        for block, device in steps:
            copy = net.send(block, block, device)
            yield
            copy.wait_recv()

    interleave(attention(), small(), feed_forward(), torus_gather(net, me, cots))
    net.drain()


def gather_all(wq, wk, wv, wo, wg, wu, wd, cot, gains):
    return pl.pallas_call(
        gather_kernel,
        out_shape=(
            jax.ShapeDtypeStruct((2, 4, 4, 64, 1280), BF),
            jax.ShapeDtypeStruct((3, 2, 4, 4, 64, 256), BF),
            jax.ShapeDtypeStruct((4, 4, 2, 32, 2048), BF),
            jax.ShapeDtypeStruct((2, 4, 4, 16, 128), BF),
        ),
        in_specs=[ANY] * 9,
        out_specs=[ANY] * 4,
        scratch_shapes=sem_scratch(96) + [pltpu.SemaphoreType.DMA((9,))],
        compiler_params=params(1),
        name="gather_all",
    )(wq, wk, wv, wo, wg, wu, wd, cot, gains)


def lanes(shape):
    return lax.broadcasted_iota(jnp.int32, shape, len(shape) - 1)


def partner(v):
    n = v.shape[-1]
    low = lax.rem(lanes(v.shape), 64) < 32
    return jnp.where(low, pltpu.roll(v, n - 32, 1), pltpu.roll(v, 32, 1))


def head_mean(v):
    n = v.shape[-1]
    r = lax.broadcasted_iota(jnp.int32, (n, n), 0)
    same = lax.div(r, 64) == lax.div(lanes((n, n)), 64)
    return lax.dot_general(
        v, jnp.where(same, 1.0 / 64.0, 0.0), (((1,), (0,)), ((), ())),
        precision=lax.Precision.HIGHEST, preferred_element_type=F32,
    )


def half_of(v, which):
    upper = lanes(v.shape) >= 64
    keep = upper if which else jnp.logical_not(upper)
    return jnp.where(keep, v, jnp.zeros_like(v))


def swap_halves(v):
    return pltpu.roll(v.astype(F32), 64, 1).astype(v.dtype)


def attention_forward_kernel(
    x_ref, gain_ref, w_ref, head_gain_ref, cos_ref, sin_ref,
    xn_ref, z_ref, qk_ref, v_ref, p_ref, o_ref, branch_ref,
):
    x = x_ref[...].astype(F32)
    r = lax.rsqrt(jnp.mean(x * x, axis=-1, keepdims=True) + EPS)
    xn = (x * r * gain_ref[...]).astype(BF)
    xn_ref[...] = xn
    raw = nn(xn, w_ref[:, 0:768])
    z = raw[:, 0:640]
    z_ref[...] = z
    v = raw[:, 640:768].astype(BF)
    v_ref[...] = v
    n = z * lax.rsqrt(head_mean(z * z) + EPS) * head_gain_ref[...]
    cos = jnp.concatenate([cos_ref[...]] * 5, axis=1)
    sin = jnp.concatenate([sin_ref[...]] * 5, axis=1)
    qk = (n * cos + partner(n) * sin).astype(BF)
    qk_ref[...] = qk
    k = qk[:, 512:640]
    k_at = {True: k, False: swap_halves(k)}
    v_at = {True: v, False: swap_halves(v)}
    rows = lax.broadcasted_iota(jnp.int32, (128, 128), 0)
    causal = rows >= lanes((128, 128))
    for block in range(4):
        out = None
        for side in range(2):
            h = 2 * block + side
            same = side == h // 4
            q = half_of(qk[:, block * 128:(block + 1) * 128], side)
            s = jnp.where(causal, nt(q, k_at[same]) * 0.125, -1e30)
            e = jnp.exp(s - jnp.max(s, axis=-1, keepdims=True))
            p = e / jnp.sum(e, axis=-1, keepdims=True)
            p_ref[h] = p
            part = nn(p.astype(BF), half_of(v_at[same], side))
            out = part if out is None else out + part
        o_ref[:, block * 128:(block + 1) * 128] = out.astype(BF)
    branch_ref[...] = nt(o_ref[...], w_ref[:, 768:1280]).astype(BF)


def attention_forward(x, gain, w, head_gain, cos, sin):
    return pl.pallas_call(
        attention_forward_kernel,
        out_shape=(
            jax.ShapeDtypeStruct((128, 2048), BF),
            jax.ShapeDtypeStruct((128, 640), F32),
            jax.ShapeDtypeStruct((128, 640), BF),
            jax.ShapeDtypeStruct((128, 128), BF),
            jax.ShapeDtypeStruct((8, 128, 128), F32),
            jax.ShapeDtypeStruct((128, 512), BF),
            jax.ShapeDtypeStruct((128, 2048), BF),
        ),
        in_specs=[VM] * 6,
        out_specs=[VM] * 7,
        compiler_params=params(),
        name="attention_forward",
    )(x, gain, w, head_gain, cos, sin)


def attention_backward_kernel(
    dh_ref, w_ref, head_gain_ref, cos_ref, sin_ref,
    xn_ref, z_ref, qk_ref, v_ref, p_ref, o_ref,
    grad_ref, dxn_ref, dgain_ref, d_ref,
):
    dh = dh_ref[...]
    grad_ref[:, 768:1280] = tn(dh, o_ref[...]).astype(BF)
    do = nn(dh, w_ref[:, 768:1280]).astype(BF)
    qk = qk_ref[...]
    v = v_ref[...]
    k = qk[:, 512:640]
    k_at = {True: k, False: swap_halves(k)}
    v_at = {True: v, False: swap_halves(v)}
    dk = {True: jnp.zeros((128, 128), F32), False: jnp.zeros((128, 128), F32)}
    dv = {True: jnp.zeros((128, 128), F32), False: jnp.zeros((128, 128), F32)}
    for block in range(4):
        dq = None
        for side in range(2):
            h = 2 * block + side
            same = side == h // 4
            p = p_ref[h]
            dob = half_of(do[:, block * 128:(block + 1) * 128], side)
            q = half_of(qk[:, block * 128:(block + 1) * 128], side)
            dp = nt(dob, v_at[same])
            dv[same] = dv[same] + tn(p.astype(BF), dob)
            ds = (p * (dp - jnp.sum(p * dp, axis=-1, keepdims=True))).astype(BF)
            part = nn(ds, half_of(k_at[same], side))
            dq = part if dq is None else dq + part
            dk[same] = dk[same] + tn(ds, q)
        d_ref[:, block * 128:(block + 1) * 128] = dq * 0.125
    d_ref[:, 512:640] = (dk[True] + pltpu.roll(dk[False], 64, 1)) * 0.125
    dvb = (dv[True] + pltpu.roll(dv[False], 64, 1)).astype(BF)
    cos = jnp.concatenate([cos_ref[...]] * 5, axis=1)
    sin = jnp.concatenate([sin_ref[...]] * 5, axis=1)
    dout = d_ref[...]
    dn = dout * cos - partner(dout) * sin
    z = z_ref[...]
    r = lax.rsqrt(head_mean(z * z) + EPS)
    zhat = z * r
    dgain = jnp.sum(dn * zhat, axis=0, keepdims=True)
    pairs = dgain[:, 0:128] + dgain[:, 128:256] + dgain[:, 256:384] + dgain[:, 384:512]
    both = jnp.concatenate([pairs, dgain[:, 512:640]], axis=0)
    both = both + pltpu.roll(both, 64, 1)
    q_row = half_of(both[0:1], 0) + half_of(both[1:2], 1)
    dgain_ref[...] = jnp.concatenate([q_row, jnp.zeros((7, 128), F32)], axis=0)
    dz = dn * head_gain_ref[...]
    dz = r * (dz - zhat * head_mean(dz * zhat))
    low = jnp.concatenate([dz.astype(BF), dvb], axis=1)
    grad_ref[:, 0:768] = tn(xn_ref[...], low).astype(BF)
    dxn_ref[...] = nt(low, w_ref[:, 0:768]).astype(BF)


def attention_backward(dh, w, head_gain, cos, sin, xn, z, qk, v, p, o):
    return pl.pallas_call(
        attention_backward_kernel,
        out_shape=(
            jax.ShapeDtypeStruct((2048, 1280), BF),
            jax.ShapeDtypeStruct((128, 2048), BF),
            jax.ShapeDtypeStruct((8, 128), F32),
        ),
        in_specs=[VM] * 11,
        out_specs=[VM] * 3,
        scratch_shapes=[pltpu.VMEM((128, 640), F32)],
        compiler_params=params(),
        name="attention_backward",
    )(dh, w, head_gain, cos, sin, xn, z, qk, v, p, o)


def hidden_kernel(
    branch, tokens, gain, xn, hidden, from_core, from_zl, tmp, send_sems, recv_sems
):
    me = Place()
    x, z, c, zl = me.x, me.z, me.c, me.zl
    greet(
        [me.step("x", 1), me.step("x", -1), me.step("z", 1), me.step("z", -1), me.core()]
    )
    net = Net(send_sems, recv_sems)
    interleave(quad_reduce(net, me, branch, from_core, from_zl, tmp))
    h = tokens[pl.ds(c * 64 + zl * 32, 32), :].astype(F32)
    h = h + quad_total(me, branch, from_core, from_zl)
    hidden[...] = h
    r = lax.rsqrt(jnp.mean(h * h, axis=-1, keepdims=True) + EPS)
    xn[z, x, c] = (h * r * gain[...]).astype(BF)
    interleave(torus_gather(net, me, xn))
    net.drain()


def hidden_state(branch, tokens, gain):
    return pl.pallas_call(
        hidden_kernel,
        out_shape=(
            jax.ShapeDtypeStruct((4, 4, 2, 32, 2048), BF),
            jax.ShapeDtypeStruct((32, 2048), F32),
        ),
        in_specs=[VM] * 3,
        out_specs=[VM] * 2,
        scratch_shapes=[
            pltpu.VMEM((64, 2048), BF),
            pltpu.VMEM((32, 2048), BF),
            pltpu.VMEM((32, 2048), BF),
        ]
        + sem_scratch(32),
        compiler_params=params(2),
        name="hidden_state",
    )(branch, tokens, gain)


def feed_forward_kernel(x_ref, dy_ref, w_ref, out_ref, dx_ref, grad_ref, acc):
    step = pl.program_id(0)
    x, dy = x_ref[...], dy_ref[...]
    wg, wu, wd = w_ref[0], w_ref[1], w_ref[2]
    g, u, da = nn(x, wg), nn(x, wu), nn(dy, wd)
    sigma = jax.nn.sigmoid(g)
    swish = g * sigma
    ab = (swish * u).astype(BF)
    dg = (da * u * sigma * (1.0 + g * (1.0 - sigma))).astype(BF)
    du = (da * swish).astype(BF)
    out_ref[...] = nt(ab, wd).astype(BF)
    dx_ref[...] = (nt(dg, wg) + nt(du, wu)).astype(BF)
    grads = [tn(x, dg), tn(x, du), tn(dy, ab)]

    @pl.when(step == 0)
    def _():
        for m in range(3):
            acc[m] = grads[m]

    @pl.when(step > 0)
    def _():
        for m in range(3):
            acc[m] += grads[m]

    @pl.when(step == pl.num_programs(0) - 1)
    def _():
        for m in range(3):
            grad_ref[m] = acc[m].astype(BF)


def feed_forward(x, dy, w):
    rows = 512
    block = pl.BlockSpec((rows, 2048), lambda t: (t, 0))
    whole = pl.BlockSpec((3, 2048, 256), lambda t: (0, 0, 0))
    return pl.pallas_call(
        feed_forward_kernel,
        grid=(1024 // rows,),
        out_shape=(
            jax.ShapeDtypeStruct((1024, 2048), BF),
            jax.ShapeDtypeStruct((1024, 2048), BF),
            jax.ShapeDtypeStruct((3, 2048, 256), BF),
        ),
        in_specs=[block, block, whole],
        out_specs=[block, block, whole],
        scratch_shapes=[pltpu.VMEM((3, 2048, 256), F32)],
        compiler_params=params(),
        name="feed_forward",
    )(x, dy, w)


def hidden_grad_kernel(
    part, hidden, cot, gain, dh, dhb, gain_grad, dxn, *rest
):
    scratch, (send_sems, recv_sems) = rest[:-2], rest[-2:]
    me = Place()
    c, zl = me.c, me.zl
    greet(
        [me.step("x", 1), me.step("x", -1), me.step("z", 1), me.step("z", -1), me.core()]
    )
    net = Net(send_sems, recv_sems)
    interleave(torus_reduce(net, me, part, scratch, dxn))
    rows = pl.ds(c * 64 + zl * 32, 32)
    h = hidden[...]
    r = lax.rsqrt(jnp.mean(h * h, axis=-1, keepdims=True) + EPS)
    hat = h * r
    d = dxn[...]
    gain_grad[...] = jnp.sum(d * hat, axis=0, keepdims=True)
    s = d * gain[...]
    total = cot[rows, :].astype(F32) + r * (s - hat * jnp.mean(s * hat, axis=-1, keepdims=True))
    dh[...] = total
    dhb[rows, :] = total.astype(BF)
    interleave(quad_gather(net, me, dhb))
    net.drain()


def hidden_grad(part, hidden, cot, gain):
    return pl.pallas_call(
        hidden_grad_kernel,
        out_shape=(
            jax.ShapeDtypeStruct((32, 2048), F32),
            jax.ShapeDtypeStruct((128, 2048), BF),
            jax.ShapeDtypeStruct((1, 2048), F32),
        ),
        in_specs=[VM] * 4,
        out_specs=[VM] * 3,
        scratch_shapes=[pltpu.VMEM((32, 2048), F32)] + TORUS_SCRATCH + sem_scratch(32),
        compiler_params=params(3),
        name="hidden_grad",
    )(part, hidden, cot, gain)


ATT_A, ATT_B = ATT_SPLIT, 1280 - ATT_SPLIT
FINAL_SCRATCH = [
    pltpu.VMEM((2, 4, 64, ATT_A), BF),
    pltpu.VMEM((4, 4, 64, ATT_A), BF),
    pltpu.VMEM((2, 4, 64, ATT_A), BF),
    pltpu.VMEM((2, 64, ATT_A), BF),
    pltpu.VMEM((4, 64, ATT_A), BF),
    pltpu.VMEM((2, 4, 64, ATT_B), BF),
    pltpu.VMEM((4, 4, 64, ATT_B), BF),
    pltpu.VMEM((2, 4, 64, ATT_B), BF),
    pltpu.VMEM((2, 64, ATT_B), BF),
    pltpu.VMEM((4, 64, ATT_B), BF),
    pltpu.VMEM((2, 64, 1280), BF),
    pltpu.VMEM((64, 1280), BF),
    pltpu.VMEM((2, 3, 4, 64, 256), BF),
    pltpu.VMEM((4, 3, 4, 64, 256), BF),
    pltpu.VMEM((2, 3, 4, 64, 256), BF),
    pltpu.VMEM((64, 2048), BF),
    pltpu.VMEM((32, 2048), BF),
    pltpu.VMEM((32, 2048), BF),
    pltpu.VMEM((7, 8, 640), F32),
    pltpu.VMEM((32, 2048), F32),
]


def final_kernel(
    out_part, grads, ffn_grads, dxn_part, hidden, dh, tokens, gain, ffn_gain_grad, head_gain_grad,
    out, dx, att_grads, gate_grads, gain_sums,
    *rest,
):
    (
        far_a, near_a, mid_a, far_a2, near_a2,
        far_b, near_b, mid_b, far_b2, near_b2,
        both_z, other_z,
        far_f, near_f, mid_f,
        from_core, from_zl, tmp,
        small, total,
    ) = rest[: len(FINAL_SCRATCH)]
    torus = rest[len(FINAL_SCRATCH): len(FINAL_SCRATCH) + len(TORUS_SCRATCH)]
    send_sems, recv_sems, sems = rest[-3:]
    me = Place()
    zh, y, x, c, zl = me.zh, me.y, me.x, me.c, me.zl
    greet(
        [me.step("x", 1), me.step("x", 2), me.step("x", -1)]
        + [me.step("y", 1), me.step("y", 2), me.step("y", -1)]
        + [me.step("z", 1), me.step("z", 2), me.step("z", -1)]
        + [me.core()]
        + [me.at(zh=1 - zh, x=lax.rem(x + k, 4)) for k in (1, 2, 3)]
    )
    net = Net(send_sems, recv_sems)
    rows = pl.ds(c * 64 + zl * 32, 32)

    def tokens_and_gains():
        yield from quad_reduce(net, me, dxn_part, from_core, from_zl, tmp)
        d = quad_total(me, dxn_part, from_core, from_zl)
        t = tokens[rows, :].astype(F32)
        r = lax.rsqrt(jnp.mean(t * t, axis=-1, keepdims=True) + EPS)
        hat = t * r
        s = d * gain[...]
        grad = dh[...] + r * (s - hat * jnp.mean(s * hat, axis=-1, keepdims=True))
        dx[rows, :] = grad.astype(BF)
        gain_grad = jnp.sum(d * hat, axis=0, keepdims=True)
        gain_sums[...] = jnp.zeros((8, 640), F32)
        for k in range(8):
            gain_sums[k:k + 1, 0:256] = gain_grad[:, k * 256:(k + 1) * 256]
            gain_sums[k:k + 1, 256:512] = ffn_gain_grad[:, k * 256:(k + 1) * 256]
        gain_sums[:, 512:640] = head_gain_grad[...]
        spread = quad_gather(net, me, dx)
        next(spread)
        devices = [
            me.core(),
            me.zl_pair(),
            me.zh_pair(),
            me.at(x=x + 1 - 2 * lax.rem(x, 2)),
            me.step("x", 2),
            me.at(y=y + 1 - 2 * lax.rem(y, 2)),
            me.step("y", 2),
        ]
        for k, device in enumerate(devices):
            copy = net.send(gain_sums, small.at[k], device)
            yield
            copy.wait_recv()
            net.wait_send(copy)
            gain_sums[...] = gain_sums[...] + small[k]
            next(spread, None)

    def output():
        yield from torus_reduce(net, me, out_part, torus, total)
        out[rows, :] = (hidden[...] + total[...]).astype(BF)
        yield from quad_gather(net, me, out)

    def attention():
        a, b = pl.ds(0, ATT_A), pl.ds(ATT_A, ATT_B)

        def first():
            yield from ring_reduce(
                net, me, "y", lambda i, p: grads.at[p, i, :, :, a],
                far_a, near_a, lambda p: mid_a.at[p],
            )
            yield
            yield from ring_reduce(
                net, me, "x", lambda i, p: mid_a.at[p, i],
                far_a2, near_a2, lambda p: both_z.at[p, :, a],
            )

        def second():
            yield from ring_reduce(
                net, me, "x", lambda i, p: grads.at[p, :, i, :, b],
                far_b, near_b, lambda p: mid_b.at[p],
            )
            yield
            yield from ring_reduce(
                net, me, "y", lambda i, p: mid_b.at[p, i],
                far_b2, near_b2, lambda p: both_z.at[p, :, b],
            )

        yield from together(first(), second())
        swap = net.send(both_z.at[1 - zh], other_z, me.zh_pair())
        yield
        swap.wait_recv()
        own = att_grads.at[zl]
        add_refs(own, [both_z.at[zh], other_z])
        swap = net.send(own, own, me.zl_pair())
        yield
        swap.wait_recv()

    def feed_forward_grads():
        yield from ring_reduce(
            net, me, "y", lambda i, p: ffn_grads.at[:, p, i],
            far_f, near_f, lambda p: mid_f.at[p],
        )
        mine = zh * 4 + x
        arrivals = []
        for dz in (0, 1):
            for dxx in range(4):
                if dz == 0 and dxx == 0:
                    continue
                tx = lax.rem(x + dxx, 4)
                tz = 1 - zh if dz else zh
                arrivals.append(
                    net.send(
                        mid_f.at[tz, :, tx], gate_grads.at[:, mine, c], me.at(zh=tz, x=tx)
                    )
                )
        keep = pltpu.make_async_copy(mid_f.at[zh, :, x], gate_grads.at[:, mine, c], sems.at[0])
        keep.start()
        yield
        keep.wait()
        for copy in arrivals:
            copy.wait_recv()
        swap = net.send(gate_grads.at[:, :, c], gate_grads.at[:, :, c], me.core())
        yield
        swap.wait_recv()

    interleave(attention(), feed_forward_grads(), output(), tokens_and_gains())
    net.drain()


def final_sums(*args):
    return pl.pallas_call(
        final_kernel,
        out_shape=(
            jax.ShapeDtypeStruct((128, 2048), BF),
            jax.ShapeDtypeStruct((128, 2048), BF),
            jax.ShapeDtypeStruct((2, 64, 1280), BF),
            jax.ShapeDtypeStruct((3, 8, 2, 64, 256), BF),
            jax.ShapeDtypeStruct((8, 640), F32),
        ),
        in_specs=[VM] * 10,
        out_specs=[VM] * 5,
        scratch_shapes=FINAL_SCRATCH
        + TORUS_SCRATCH
        + sem_scratch(96)
        + [pltpu.SemaphoreType.DMA((1,))],
        compiler_params=params(4),
        name="final_sums",
    )(*args)


def rotary_tables():
    position = np.arange(128, dtype=np.float64)[:, None]
    lane = np.arange(128)
    angle = position * THETA ** (-2.0 * (lane % 32) / 64.0)[None, :]
    sign = np.where(lane % 64 < 32, -1.0, 1.0)
    return np.cos(angle).astype(np.float32), (np.sin(angle) * sign).astype(np.float32)


def on_device(
    tokens, gain_attn, w_query, w_key, w_value, gain_query, gain_key, w_out, gain_ffn,
    w_gate, w_up, w_down, cotangent,
):
    cos, sin = (jnp.asarray(t) for t in rotary_tables())
    gains = jnp.zeros((16, 128), BF)
    gains = gains.at[0, 0:64].set(gain_attn).at[0, 64:128].set(gain_ffn)
    att, ffn, cots, all_gains = gather_all(
        w_query, w_key, w_value, w_out, w_gate, w_up, w_down, cotangent, gains
    )
    gain_rows = all_gains[:, :, :, 0, :].reshape(32, 128).astype(F32)
    attn_gain = gain_rows[:, 0:64].reshape(1, 2048)
    ffn_gain = gain_rows[:, 64:128].reshape(1, 2048)
    head_gain = jnp.concatenate([jnp.tile(gain_query, 8), jnp.tile(gain_key, 2)])
    head_gain = head_gain.astype(F32).reshape(1, 640)
    att = att.reshape(2048, 1280)
    xn, z, qk, v, p, o, branch = attention_forward(tokens, attn_gain, att, head_gain, cos, sin)
    xn2, hidden = hidden_state(branch, tokens, ffn_gain)
    out_part, dxn2_part, ffn_grads = feed_forward(
        xn2.reshape(1024, 2048), cots.reshape(1024, 2048), ffn.reshape(3, 2048, 256)
    )
    dh, dhb, ffn_gain_grad = hidden_grad(
        dxn2_part.reshape(4, 4, 2, 32, 2048), hidden, cotangent, ffn_gain
    )
    grads, dxn_part, head_gain_grad = attention_backward(
        dhb, att, head_gain, cos, sin, xn, z, qk, v, p, o
    )
    out, dx, att_grads, gate_grads, gain_sums = final_sums(
        out_part.reshape(4, 4, 2, 32, 2048),
        grads.reshape(2, 4, 4, 64, 1280),
        ffn_grads.reshape(3, 2, 4, 4, 64, 256),
        dxn_part, hidden, dh, tokens, attn_gain, ffn_gain_grad, head_gain_grad,
    )
    dp = lax.axis_index("dp")

    def side_by_side(lo, hi):
        return jnp.concatenate([att_grads[0, :, lo:hi], att_grads[1, :, lo:hi]], axis=1).astype(F32)

    wide = gate_grads.transpose(0, 3, 1, 2, 4).reshape(3, 64, 4096)
    gq = gain_sums[0, 512:576]
    gk = gain_sums[0, 576:640]
    att_gain_grad = lax.dynamic_slice(gain_sums[:, 0:256].reshape(2048), (dp * 64,), (64,))
    ffn_gain_grad = lax.dynamic_slice(gain_sums[:, 256:512].reshape(2048), (dp * 64,), (64,))
    return (
        out,
        dx.astype(F32),
        att_gain_grad,
        side_by_side(0, 512),
        side_by_side(512, 640),
        side_by_side(640, 768),
        gq,
        gk,
        side_by_side(768, 1280),
        ffn_gain_grad,
        wide[0].astype(F32),
        wide[1].astype(F32),
        wide[2].astype(F32),
    )


def solution(mesh):
    return jax.shard_map(
        on_device,
        mesh=mesh,
        in_specs=(
            P("dp", None), P("dp"), P("dp", "head"), P("dp", "head"), P("dp", "head"),
            P(), P(), P("dp", "head"), P("dp"),
            P("dp", "tensor"), P("dp", "tensor"), P("dp", "tensor"), P("dp", None),
        ),
        out_specs=(
            P("dp", None), P("dp", None), P("dp"),
            P("dp", "head"), P("dp", "head"), P("dp", "head"),
            P(), P(), P("dp", "head"), P("dp"),
            P("dp", "tensor"), P("dp", "tensor"), P("dp", "tensor"),
        ),
        check_vma=False,
    )
```

```python
import types

import jax
import jax.numpy as jnp
import numpy as np
from jax import lax
from jax.experimental import pallas as pl
from jax.experimental.pallas import tpu as pltpu
from jax.sharding import PartitionSpec as P

BF = jnp.bfloat16
F32 = jnp.float32
MESH = pl.DeviceIdType.MESH
EPS = 1e-05
THETA = 1000000.0
VMEM_BYTES = 62 << 20
ATT_GATHER_SPLIT = 768
ATT_SLICES = ((0, 384, "yx"), (384, 384, "xy"), (768, 256, "yx"), (1024, 256, "xy"))


def nn(a, b):
    return lax.dot_general(a, b, (((1,), (0,)), ((), ())), preferred_element_type=F32)


def nt(a, b):
    return lax.dot_general(a, b, (((1,), (1,)), ((), ())), preferred_element_type=F32)


def tn(a, b):
    return lax.dot_general(a, b, (((0,), (0,)), ((), ())), preferred_element_type=F32)


class Place:
    def __init__(self):
        dp = lax.axis_index("dp")
        self.c = lax.axis_index("head")
        self.zl = lax.axis_index("tensor")
        self.zh = lax.div(dp, 16)
        self.y = lax.rem(lax.div(dp, 4), 4)
        self.x = lax.rem(dp, 4)
        self.z = self.zh * 2 + self.zl

    def at(self, zh=None, y=None, x=None, c=None, zl=None):
        zh = self.zh if zh is None else zh
        y = self.y if y is None else y
        x = self.x if x is None else x
        return (zh * 16 + y * 4 + x, self.c if c is None else c, self.zl if zl is None else zl)

    def step(self, axis, by):
        if axis == "x":
            return self.at(x=lax.rem(self.x + by + 4, 4))
        if axis == "y":
            return self.at(y=lax.rem(self.y + by + 4, 4))
        z = lax.rem(self.z + by + 4, 4)
        return self.at(zh=lax.div(z, 2), zl=lax.rem(z, 2))

    def core(self):
        return self.at(c=1 - self.c)

    def zl_pair(self):
        return self.at(zl=1 - self.zl)

    def zh_pair(self):
        return self.at(zh=1 - self.zh)

    def ring(self, axis):
        return {"x": self.x, "y": self.y, "z": self.z}[axis]


class Net:
    def __init__(self, send_sems, recv_sems):
        self.send_sems = send_sems
        self.recv_sems = recv_sems
        self.count = 0
        self.left = []

    def send(self, src, dst, device):
        k = self.count
        assert k < self.send_sems.shape[0]
        self.count += 1
        copy = pltpu.make_async_remote_copy(
            src_ref=src,
            dst_ref=dst,
            send_sem=self.send_sems.at[k],
            recv_sem=self.recv_sems.at[k],
            device_id=device,
            device_id_type=MESH,
        )
        copy.start()
        self.left.append(copy)
        return copy

    def wait_send(self, copy):
        copy.wait_send()
        self.left = [other for other in self.left if other is not copy]

    def drain(self):
        for copy in self.left:
            copy.wait_send()


class Tagged:
    def __init__(self, net):
        self.net = net
        self.copies = []

    def send(self, src, dst, device):
        self.copies.append(self.net.send(src, dst, device))
        return self.copies[-1]

    def drain(self):
        for copy in self.copies:
            self.net.wait_send(copy)


def greet(devices):
    barrier = pltpu.get_barrier_semaphore()
    for device in devices:
        pl.semaphore_signal(barrier, inc=1, device_id=device, device_id_type=MESH)
    pl.semaphore_wait(barrier, len(devices))


def together(*pipelines):
    live = list(pipelines)
    while live:
        for pipe in list(live):
            try:
                next(pipe)
            except StopIteration:
                live.remove(pipe)
        yield


def step(*pipelines):
    for pipe in pipelines:
        next(pipe, None)


def finish(*pipelines):
    for _ in together(*pipelines):
        pass


def local(pairs, sems):
    copies = [pltpu.make_async_copy(s, d, sems.at[i]) for i, (s, d) in enumerate(pairs)]
    for copy in copies:
        copy.start()
    for copy in copies:
        copy.wait()


def add_refs(dst, srcs, rows=32):
    lead, height = dst.shape[:-2], dst.shape[-2]
    rows = min(rows, height)
    per = height // rows
    count = int(np.prod(lead, dtype=np.int64)) * per

    def body(t, carry):
        r = lax.rem(t, per)
        rest = lax.div(t, per)
        index = []
        for size in reversed(lead):
            index.insert(0, lax.rem(rest, size))
            rest = lax.div(rest, size)
        at = tuple(index) + (pl.ds(r * rows, rows), slice(None))
        total = srcs[0][at].astype(F32)
        for src in srcs[1:]:
            total = total + src[at].astype(F32)
        dst[at] = total.astype(dst.dtype)
        return carry

    lax.fori_loop(0, count, body, 0)


def ring_gather(net, place, axis, view, also=None):
    i = place.ring(axis)
    before, after, across = lax.rem(i + 3, 4), lax.rem(i + 1, 4), lax.rem(i + 2, 4)
    up, down = place.step(axis, 1), place.step(axis, -1)
    u0 = net.send(view(i, 0), view(i, 0), up)
    d1 = net.send(view(i, 1), view(i, 1), down)
    u1 = net.send(view(i, 1), view(i, 1), up)
    d0 = net.send(view(i, 0), view(i, 0), down)
    yield
    u0.wait_recv()
    f0 = net.send(view(before, 0), view(before, 0), up)
    d1.wait_recv()
    f1 = net.send(view(after, 1), view(after, 1), down)
    if also is not None:
        also(view(before, 0))
        also(view(after, 1))
    yield
    u1.wait_recv()
    d0.wait_recv()
    if also is not None:
        also(view(before, 1))
        also(view(after, 0))
    f0.wait_recv()
    f1.wait_recv()
    if also is not None:
        also(view(across, 0))
        also(view(across, 1))


def cross_gather(net, place, one, two, view, late=None, also=None):
    ring = [lax.rem(place.ring(one) + k, 4) for k in range(4)]
    other = [lax.rem(place.ring(two) + k, 4) for k in range(4)]
    up = {one: place.step(one, 1), two: place.step(two, 1)}
    down = {one: place.step(one, -1), two: place.step(two, -1)}
    corners = []

    def spread(block, axis):
        return net.send(block, block, up[axis]), net.send(block, block, down[axis])

    def arrived(block):
        if also is not None:
            also(block)
        return block

    def along(axis, part, k, half=None):
        if axis == one:
            return view(part, ring[k], other[0], half)
        return view(part, ring[0], other[k], half)

    def turn(axis, part, k):
        across = two if axis == one else one
        half = 1 if axis == one else 0
        copies = spread(along(axis, part, k, half), across)
        corners.append((axis, part, k, half, across, copies))

    def own(part):
        block = view(part, ring[0], other[0], None)
        return {axis: spread(block, axis) for axis in (one, two)}

    crosses = [own(0)]
    if late is None:
        crosses.append(own(1))
    yield
    if late is not None:
        late.wait_recv()
        crosses.append(own(1))
        yield
    far = []
    for part in (0, 1):
        order = ((0, 3), (1, 1)) if part == 0 else ((1, 1), (0, 3))
        for n, (which, k) in enumerate(order):
            for axis in (one, two):
                crosses[part][axis][which].wait_recv()
                block = arrived(along(axis, part, k))
                if n == 0:
                    on = (up, down)[part][axis]
                    far.append((axis, part, net.send(block, block, on)))
                turn(axis, part, k)
        yield
    for axis, part, copy in far:
        copy.wait_recv()
        arrived(along(axis, part, 2))
        turn(axis, part, 2)
    yield
    last = []
    for n, (axis, part, k, half, across, copies) in enumerate(corners):
        for which, step_ in ((0, 3), (1, 1)):
            copies[which].wait_recv()
            if axis == one:
                block = view(part, ring[k], other[step_], half)
                final = view(part, ring[k], other[2], half)
            else:
                block = view(part, ring[step_], other[k], half)
                final = view(part, ring[2], other[k], half)
            arrived(block)
            if which == part:
                on = (up, down)[part][across]
                last.append((net.send(block, block, on), final))
        if n % 4 == 3:
            yield
    for copy, final in last:
        copy.wait_recv()
        arrived(final)


def ring_reduce(net, place, axis, view, far, near, out):
    i = place.ring(axis)
    before, after, across = lax.rem(i + 3, 4), lax.rem(i + 1, 4), lax.rem(i + 2, 4)
    up, down = place.step(axis, 1), place.step(axis, -1)
    f0 = net.send(view(across, 0), far.at[0], up)
    f1 = net.send(view(across, 1), far.at[1], down)
    u1 = net.send(view(after, 1), near.at[1], up)
    d0 = net.send(view(before, 0), near.at[2], down)
    yield
    f0.wait_recv()
    add_refs(far.at[0], [far.at[0], view(after, 0)])
    u0 = net.send(far.at[0], near.at[0], up)
    f1.wait_recv()
    add_refs(far.at[1], [far.at[1], view(before, 1)])
    d1 = net.send(far.at[1], near.at[3], down)
    yield
    u1.wait_recv()
    d0.wait_recv()
    u0.wait_recv()
    d1.wait_recv()
    add_refs(out(0), [view(i, 0), near.at[0], near.at[2]])
    add_refs(out(1), [view(i, 1), near.at[1], near.at[3]])


def torus_gather(net, place, buf):
    c = place.c
    other = place.core()
    swaps = []

    def also(block):
        swaps.append(net.send(block, block, other))

    def view(part, i, j, half):
        rows = pl.ds(0, 32) if half is None else pl.ds(half * 16, 16)
        return buf.at[i, j, c, rows, pl.ds(part * 1024, 1024)]

    also(buf.at[place.z, place.x, c])
    yield from cross_gather(net, place, "z", "x", view, also=also)
    yield
    for swap in swaps:
        swap.wait_recv()


def torus_buffers():
    return dict(
        both=pltpu.VMEM((4, 4, 32, 2048), BF),
        far_a=pltpu.VMEM((2, 4, 16, 1024), BF),
        near_a=pltpu.VMEM((4, 4, 16, 1024), BF),
        mid_a=pltpu.VMEM((2, 4, 16, 1024), BF),
        far_a2=pltpu.VMEM((2, 16, 1024), BF),
        near_a2=pltpu.VMEM((4, 16, 1024), BF),
        far_b=pltpu.VMEM((2, 4, 16, 1024), BF),
        near_b=pltpu.VMEM((4, 4, 16, 1024), BF),
        mid_b=pltpu.VMEM((2, 4, 16, 1024), BF),
        far_b2=pltpu.VMEM((2, 16, 1024), BF),
        near_b2=pltpu.VMEM((4, 16, 1024), BF),
        total=pltpu.VMEM((32, 2048), F32),
    )


def torus_reduce(net, place, src, swaps, s):
    x, z, c = place.x, place.z, place.c
    both, out = s.both, s.total
    for k, swap in enumerate(swaps):
        swap.wait_recv()
        add_refs(both.at[k], [both.at[k], src.at[k, :, c]])

    def first():
        mid = s.mid_a
        yield from ring_reduce(
            net, place, "z",
            lambda i, p: both.at[i, :, pl.ds(0, 16), pl.ds(p * 1024, 1024)],
            s.far_a, s.near_a, lambda p: mid.at[p],
        )
        yield
        yield from ring_reduce(
            net, place, "x",
            lambda i, p: mid.at[p, i],
            s.far_a2, s.near_a2,
            lambda p: out.at[pl.ds(0, 16), pl.ds(p * 1024, 1024)],
        )

    def second():
        mid = s.mid_b
        yield from ring_reduce(
            net, place, "x",
            lambda i, p: both.at[:, i, pl.ds(16, 16), pl.ds(p * 1024, 1024)],
            s.far_b, s.near_b, lambda p: mid.at[p],
        )
        yield
        yield from ring_reduce(
            net, place, "z",
            lambda i, p: mid.at[p, i],
            s.far_b2, s.near_b2,
            lambda p: out.at[pl.ds(16, 16), pl.ds(p * 1024, 1024)],
        )

    yield from together(first(), second())


def quad_gather(net, place, buf):
    c, zl = place.c, place.zl
    own = buf.at[pl.ds(c * 64 + zl * 32, 32)]
    one = net.send(own, own, place.zl_pair())
    yield
    one.wait_recv()
    half = buf.at[pl.ds(c * 64, 64)]
    two = net.send(half, half, place.core())
    yield
    two.wait_recv()


def quad_reduce(net, place, src, from_core, from_zl, tmp):
    c, zl = place.c, place.zl
    one = net.send(src.at[pl.ds((1 - c) * 64, 64)], from_core, place.core())
    yield
    one.wait_recv()
    theirs = src[pl.ds(c * 64 + (1 - zl) * 32, 32), :].astype(F32)
    tmp[...] = (theirs + from_core[pl.ds((1 - zl) * 32, 32), :].astype(F32)).astype(BF)
    two = net.send(tmp, from_zl, place.zl_pair())
    yield
    two.wait_recv()


def quad_total(place, src, from_core, from_zl):
    c, zl = place.c, place.zl
    mine = src[pl.ds(c * 64 + zl * 32, 32), :].astype(F32)
    mine = mine + from_core[pl.ds(zl * 32, 32), :].astype(F32)
    return mine + from_zl[...].astype(F32)


def sem_scratch(n):
    return [pltpu.SemaphoreType.DMA((n,)), pltpu.SemaphoreType.DMA((n,))]


ANY = pl.BlockSpec(memory_space=pl.ANY)
VM = pl.BlockSpec(memory_space=pltpu.VMEM)


def lanes(shape):
    return lax.broadcasted_iota(jnp.int32, shape, len(shape) - 1)


def partner(v):
    n = v.shape[-1]
    low = lax.rem(lanes(v.shape), 64) < 32
    return jnp.where(low, pltpu.roll(v, n - 32, 1), pltpu.roll(v, 32, 1))


def head_mean(v):
    n = v.shape[-1]
    r = lax.broadcasted_iota(jnp.int32, (n, n), 0)
    same = lax.div(r, 64) == lax.div(lanes((n, n)), 64)
    return lax.dot_general(
        v, jnp.where(same, 1.0 / 64.0, 0.0), (((1,), (0,)), ((), ())),
        precision=lax.Precision.HIGHEST, preferred_element_type=F32,
    )


def half_of(v, which):
    upper = lanes(v.shape) >= 64
    keep = upper if which else jnp.logical_not(upper)
    return jnp.where(keep, v, jnp.zeros_like(v))


def swap_halves(v):
    return pltpu.roll(v.astype(F32), 64, 1).astype(v.dtype)


def rows_rms(v):
    return lax.rsqrt(jnp.mean(v * v, axis=-1, keepdims=True) + EPS)


N_COPIES = 420
N_LOCAL = 8


def input_plan():
    return dict(
        tokens=VM, cot=VM, small=VM, cos=VM, sin=VM,
        wq=ANY, wk=ANY, wv=ANY, wo=ANY, wg=ANY, wu=ANY, wd=ANY,
    )


def output_plan():
    return dict(
        out=jax.ShapeDtypeStruct((128, 2048), BF),
        dx=jax.ShapeDtypeStruct((128, 2048), BF),
        att_grads=jax.ShapeDtypeStruct((2, 64, 1280), BF),
        ffn_grads=jax.ShapeDtypeStruct((3, 8, 2, 64, 256), BF),
        gain_sums=jax.ShapeDtypeStruct((8, 640), F32),
    )


def slice_buffers(n):
    return dict(
        far=pltpu.VMEM((2, 4, 64, n), BF),
        near=pltpu.VMEM((4, 4, 64, n), BF),
        mid=pltpu.VMEM((2, 4, 64, n), BF),
        far2=pltpu.VMEM((2, 64, n), BF),
        near2=pltpu.VMEM((4, 64, n), BF),
    )


def scratch_plan():
    return dict(
        att=pltpu.VMEM((2, 4, 4, 64, 1280), BF),
        gains=pltpu.VMEM((2, 4, 4, 16, 128), BF),
        ffn=pltpu.VMEM((3, 2, 4, 4, 64, 256), BF),
        cots=pltpu.VMEM((4, 4, 2, 32, 2048), BF),
        xn2=pltpu.VMEM((4, 4, 2, 32, 2048), BF),
        xn=pltpu.VMEM((128, 2048), BF),
        z=pltpu.VMEM((128, 640), F32),
        qk=pltpu.VMEM((128, 640), BF),
        v=pltpu.VMEM((128, 128), BF),
        p=pltpu.VMEM((8, 128, 128), F32),
        o=pltpu.VMEM((128, 512), BF),
        branch=pltpu.VMEM((128, 2048), BF),
        hidden=pltpu.VMEM((32, 2048), F32),
        branch_core=pltpu.VMEM((64, 2048), BF),
        branch_zl=pltpu.VMEM((32, 2048), BF),
        branch_tmp=pltpu.VMEM((32, 2048), BF),
        da=pltpu.VMEM((4, 256, 256), F32),
        ab=pltpu.VMEM((4, 256, 256), BF),
        dg=pltpu.VMEM((4, 256, 256), BF),
        du=pltpu.VMEM((4, 256, 256), BF),
        dxn2_part=pltpu.VMEM((4, 4, 2, 32, 2048), BF),
        ffn_part=pltpu.VMEM((3, 2, 4, 4, 64, 256), BF),
        ffn_far=pltpu.VMEM((2, 3, 4, 64, 256), BF),
        ffn_near=pltpu.VMEM((4, 3, 4, 64, 256), BF),
        ffn_mid=pltpu.VMEM((2, 3, 4, 64, 256), BF),
        dh=pltpu.VMEM((32, 2048), F32),
        dhb=pltpu.VMEM((128, 2048), BF),
        ffn_gain_grad=pltpu.VMEM((1, 2048), F32),
        d_heads=pltpu.VMEM((128, 640), F32),
        att_part=pltpu.VMEM((2, 4, 4, 64, 1280), BF),
        dxn_part=pltpu.VMEM((128, 2048), BF),
        dxn_core=pltpu.VMEM((64, 2048), BF),
        dxn_zl=pltpu.VMEM((32, 2048), BF),
        dxn_tmp=pltpu.VMEM((32, 2048), BF),
        both_z=pltpu.VMEM((2, 64, 1280), BF),
        other_z=pltpu.VMEM((64, 1280), BF),
        gain_in=pltpu.VMEM((7, 8, 640), F32),
        dxn2_sum=torus_buffers(),
        out_sum=torus_buffers(),
        slices=[slice_buffers(n) for _, n, _ in ATT_SLICES],
        send_sems=pltpu.SemaphoreType.DMA((N_COPIES,)),
        recv_sems=pltpu.SemaphoreType.DMA((N_COPIES,)),
        sems=pltpu.SemaphoreType.DMA((N_LOCAL,)),
    )


def named(plan):
    if isinstance(plan, dict):
        return types.SimpleNamespace(**{k: named(v) for k, v in plan.items()})
    if isinstance(plan, list):
        return [named(v) for v in plan]
    return plan


def kernel(*refs):
    s = types.SimpleNamespace()
    for plan in (input_plan(), output_plan(), scratch_plan()):
        leaves, tree = jax.tree.flatten(plan)
        part = jax.tree.unflatten(tree, refs[: len(leaves)])
        refs = refs[len(leaves):]
        vars(s).update(vars(named(part)))
    send_sems, recv_sems, sems = s.send_sems, s.recv_sems, s.sems
    me = Place()
    zh, y, x, c, zl, z = me.zh, me.y, me.x, me.c, me.zl, me.z
    greet(
        [me.step("x", 1), me.step("x", 2), me.step("x", -1)]
        + [me.step("y", 1), me.step("y", 2), me.step("y", -1)]
        + [me.step("z", 1), me.step("z", 2), me.step("z", -1)]
        + [me.core()]
        + [me.at(zh=1 - zh, x=lax.rem(x + k, 4)) for k in (1, 2, 3)]
    )
    net = Net(send_sems, recv_sems)
    att, ffn = s.att, s.ffn
    rows = pl.ds(c * 64 + zl * 32, 32)


    def piece(k):
        return pl.ds(pl.multiple_of(k * 512 + c * 256, 256), 256)

    own = att.at[zh, y, x]
    wide = pl.ds(pl.multiple_of(zl * 512, 512), 512)
    narrow = pl.ds(pl.multiple_of(zl * 128, 128), 128)
    mine = zh * 4 + x
    pairs = [
        (s.wq.at[:, wide], own.at[:, pl.ds(0, 512)]),
        (s.wk.at[:, narrow], own.at[:, pl.ds(512, 128)]),
        (s.wv.at[:, narrow], own.at[:, pl.ds(640, 128)]),
        (s.wo.at[:, wide], own.at[:, pl.ds(768, 512)]),
    ] + [(w.at[:, piece(mine)], ffn.at[m, zh, y, x]) for m, w in enumerate((s.wg, s.wu, s.wd))]
    copies = [pltpu.make_async_copy(a, b, sems.at[k]) for k, (a, b) in enumerate(pairs)]
    for copy in copies:
        copy.start()
    s.cots[z, x, c] = s.cot[rows, :]
    s.gains[zh, y, x] = s.small[...]

    def gather_attention():
        swap = net.send(own, own, me.zh_pair())
        halves = (
            pl.ds(0, ATT_GATHER_SPLIT),
            pl.ds(ATT_GATHER_SPLIT, 1280 - ATT_GATHER_SPLIT),
        )

        def view(part, i, j, half):
            block = att.at[1 - zh if part else zh, i, j]
            return block if half is None else block.at[:, halves[half]]

        yield from cross_gather(net, me, "y", "x", view, late=swap)

    def gather_ffn():
        arrivals = []
        for dz in (0, 1):
            for dx in range(4):
                if dz == 0 and dx == 0:
                    continue
                tx = lax.rem(x + dx, 4)
                tz = 1 - zh if dz else zh
                for m, w in enumerate((s.wg, s.wu, s.wd)):
                    arrivals.append(
                        net.send(
                            w.at[:, piece(tz * 4 + tx)],
                            ffn.at[m, zh, y, x],
                            me.at(zh=tz, x=tx),
                        )
                    )
        yield
        for copy in copies[4:]:
            copy.wait()
        for copy in arrivals:
            copy.wait_recv()
        yield from ring_gather(net, me, "y", lambda i, p: ffn.at[:, p, i])

    def gather_gains():
        gains = s.gains
        steps = [
            (gains.at[zh, y, x], me.zh_pair()),
            (gains.at[:, y, x], me.at(x=x + 1 - 2 * lax.rem(x, 2))),
            (gains.at[:, y, pl.ds(2 * lax.div(x, 2), 2)], me.step("x", 2)),
            (gains.at[:, y], me.at(y=y + 1 - 2 * lax.rem(y, 2))),
            (gains.at[:, pl.ds(2 * lax.div(y, 2), 2)], me.step("y", 2)),
        ]
        for block, device in steps:
            copy = net.send(block, block, device)
            yield
            copy.wait_recv()

    def gain_row(k):
        blocks = []
        for pair in range(16):
            a, b = 2 * pair, 2 * pair + 1
            total = None
            for d in (a, b):
                block = s.gains[d // 16, d // 4 % 4, d % 4].astype(F32)
                total = block if total is None else total + block
            blocks.append(total[k:k + 1, :])
        return jnp.concatenate(blocks, axis=1)

    for copy in copies[:4]:
        copy.wait()
    attention = gather_attention()
    step(attention)
    gains = gather_gains()
    step(gains, attention)
    weights = gather_ffn()
    step(weights)
    for _ in range(2):
        step(gains, attention)
    finish(gains)
    t = s.tokens[...].astype(F32)
    s.xn[...] = (t * rows_rms(t) * gain_row(0)).astype(BF)
    finish(attention)


    cots = torus_gather(net, me, s.cots)
    step(weights, cots)
    raw = nn(s.xn[...], att[:, :, :, :, 0:768].reshape(2048, 768))
    z_raw = raw[:, 0:640]
    s.z[...] = z_raw
    v = raw[:, 640:768].astype(BF)
    s.v[...] = v
    step(cots)
    both_gains = s.small[...].astype(F32)[2:3, :]
    turned = pltpu.roll(both_gains, 64, 1)
    low = lanes((1, 128)) < 64
    gain_q = jnp.where(low, both_gains, turned)
    gain_k = jnp.where(low, turned, both_gains)
    head_gain = jnp.concatenate([gain_q] * 4 + [gain_k], axis=1)
    cos = jnp.concatenate([s.cos[...]] * 5, axis=1)
    sin = jnp.concatenate([s.sin[...]] * 5, axis=1)
    n = z_raw * lax.rsqrt(head_mean(z_raw * z_raw) + EPS) * head_gain
    s.qk[...] = (n * cos + partner(n) * sin).astype(BF)
    step(cots)
    k = s.qk[:, 512:640]
    k_at = {True: k, False: swap_halves(k)}
    v_at = {True: v, False: swap_halves(v)}
    causal = lax.broadcasted_iota(jnp.int32, (128, 128), 0) >= lanes((128, 128))
    for block in range(4):
        out = None
        for side in range(2):
            h = 2 * block + side
            same = side == h // 4
            q = half_of(s.qk[:, block * 128:(block + 1) * 128], side)
            score = jnp.where(causal, nt(q, k_at[same]) * 0.125, -1e30)
            e = jnp.exp(score - jnp.max(score, axis=-1, keepdims=True))
            p = e / jnp.sum(e, axis=-1, keepdims=True)
            s.p[h] = p
            part = nn(p.astype(BF), half_of(v_at[same], side))
            out = part if out is None else out + part
        s.o[:, block * 128:(block + 1) * 128] = out.astype(BF)
    s.branch[...] = nt(s.o[...], att[:, :, :, :, 768:1280].reshape(2048, 512)).astype(BF)
    quad = quad_reduce(
        net, me, s.branch, s.branch_core, s.branch_zl, s.branch_tmp
    )
    step(quad, cots)
    finish(quad)
    hidden = s.tokens[rows, :].astype(F32)
    hidden = hidden + quad_total(me, s.branch, s.branch_core, s.branch_zl)
    s.hidden[...] = hidden
    s.xn2[z, x, c] = (hidden * rows_rms(hidden) * gain_row(1)).astype(BF)
    normed_net = Tagged(net)
    normed = torus_gather(normed_net, me, s.xn2)
    step(normed, weights)
    for _ in range(3):
        step(normed, cots)
    finish(cots)
    step(normed)
    finish(weights)


    def weight(m):
        return ffn[m].reshape(2048, 256)

    for k in range(4):
        s.da[k] = nn(s.cots[k].reshape(256, 2048), weight(2))
        step(normed)
    finish(normed)
    swaps = []
    for k in range(4):
        xk = s.xn2[k].reshape(256, 2048)
        g, u, da = nn(xk, weight(0)), nn(xk, weight(1)), s.da[k]
        sigma = jax.nn.sigmoid(g)
        swish = g * sigma
        s.ab[k] = (swish * u).astype(BF)
        dg = (da * u * sigma * (1.0 + g * (1.0 - sigma))).astype(BF)
        du = (da * swish).astype(BF)
        s.dg[k] = dg
        s.du[k] = du
        part = (nt(dg, weight(0)) + nt(du, weight(1))).astype(BF)
        s.dxn2_part[k] = part.reshape(4, 2, 32, 2048)
        swaps.append(
            net.send(s.dxn2_part.at[k, :, 1 - c], s.dxn2_sum.both.at[k], me.core())
        )


    dxn2 = torus_reduce(net, me, s.dxn2_part, swaps, s.dxn2_sum)
    step(dxn2)

    def weight_grads(first, last):
        def one(d, carry):
            cols = pl.ds(pl.multiple_of(d * 256, 256), 256)
            at = (lax.div(d, 4), lax.rem(d, 4))
            xd = s.xn2[:, :, :, :, cols].reshape(1024, 256)
            dyd = s.cots[:, :, :, :, cols].reshape(1024, 256)
            for m, left, right in ((0, xd, s.dg), (1, xd, s.du), (2, dyd, s.ab)):
                grad = tn(left, right[...].reshape(1024, 256))
                s.ffn_part[(m,) + at] = grad.astype(BF).reshape(4, 64, 256)
            return carry

        lax.fori_loop(first, last, one, 0)

    def reduce_ffn_grads():
        part, mid, grads = s.ffn_part, s.ffn_mid, s.ffn_grads
        yield from ring_reduce(
            net, me, "y", lambda i, p: part.at[:, p, i],
            s.ffn_far, s.ffn_near, lambda p: mid.at[p],
        )
        arrivals = []
        for dz in (0, 1):
            for dx in range(4):
                if dz == 0 and dx == 0:
                    continue
                tx = lax.rem(x + dx, 4)
                tz = 1 - zh if dz else zh
                arrivals.append(
                    net.send(mid.at[tz, :, tx], grads.at[:, mine, c], me.at(zh=tz, x=tx))
                )
        keep = pltpu.make_async_copy(mid.at[zh, :, x], grads.at[:, mine, c], sems.at[7])
        keep.start()
        yield
        keep.wait()
        for copy in arrivals:
            copy.wait_recv()
        swap = net.send(grads.at[:, :, c], grads.at[:, :, c], me.core())
        yield
        swap.wait_recv()

    weight_grads(0, 4)
    step(dxn2)
    weight_grads(4, 8)
    ffn_grads = reduce_ffn_grads()
    step(ffn_grads, dxn2)
    swaps = []
    normed_net.drain()
    for k in range(4):
        part = nt(s.ab[k], weight(2)).astype(BF)
        s.xn2[k] = part.reshape(4, 2, 32, 2048)
        swaps.append(net.send(s.xn2.at[k, :, 1 - c], s.out_sum.both.at[k], me.core()))
        if k % 2 == 1:
            step(dxn2)
    step(ffn_grads)
    finish(dxn2)
    hidden = s.hidden[...]
    r = rows_rms(hidden)
    hat = hidden * r
    d = s.dxn2_sum.total[...]
    s.ffn_gain_grad[...] = jnp.sum(d * hat, axis=0, keepdims=True)
    scaled = d * gain_row(1)
    dh = s.cot[rows, :].astype(F32)
    dh = dh + r * (scaled - hat * jnp.mean(scaled * hat, axis=-1, keepdims=True))
    s.dh[...] = dh
    s.dhb[rows, :] = dh.astype(BF)
    spread = quad_gather(net, me, s.dhb)
    step(spread)

    def finish_output():
        yield from torus_reduce(net, me, s.xn2, swaps, s.out_sum)
        s.out[rows, :] = (s.hidden[...] + s.out_sum.total[...]).astype(BF)
        yield from quad_gather(net, me, s.out)

    output = finish_output()
    step(spread)
    step(output)
    finish(spread)


    def reduce_att_grads(k):
        start, width, order = ATT_SLICES[k]
        cols = pl.ds(start, width)
        part, mid, both_z = s.att_part, s.slices[k].mid, s.both_z
        one, two = order
        if one == "y":
            view = lambda i, p: part.at[p, i, :, :, cols]
        else:
            view = lambda i, p: part.at[p, :, i, :, cols]
        yield from ring_reduce(
            net, me, one, view, s.slices[k].far, s.slices[k].near, lambda p: mid.at[p]
        )
        yield
        yield from ring_reduce(
            net, me, two, lambda i, p: mid.at[p, i],
            s.slices[k].far2, s.slices[k].near2, lambda p: both_z.at[p, :, cols],
        )
        other = s.other_z.at[:, cols]
        swap = net.send(both_z.at[1 - zh, :, cols], other, me.zh_pair())
        yield
        swap.wait_recv()
        done = s.att_grads.at[zl, :, cols]
        add_refs(done, [both_z.at[zh, :, cols], other])
        swap = net.send(done, done, me.zl_pair())
        yield
        swap.wait_recv()

    dhb = s.dhb[...]
    grad = tn(dhb, s.o[...]).astype(BF)
    s.att_part[:, :, :, :, 768:1280] = grad.reshape(2, 4, 4, 64, 512)
    slices = [reduce_att_grads(k) for k in range(4)]
    step(slices[2], slices[3])
    do = nn(dhb, att[:, :, :, :, 768:1280].reshape(2048, 512)).astype(BF)
    step(output, ffn_grads)
    v = s.v[...]
    k = s.qk[:, 512:640]
    k_at = {True: k, False: swap_halves(k)}
    v_at = {True: v, False: swap_halves(v)}
    zero = jnp.zeros((128, 128), F32)
    dk = {True: zero, False: zero}
    dv = {True: zero, False: zero}
    for block in range(4):
        dq = None
        for side in range(2):
            h = 2 * block + side
            same = side == h // 4
            p = s.p[h]
            dob = half_of(do[:, block * 128:(block + 1) * 128], side)
            q = half_of(s.qk[:, block * 128:(block + 1) * 128], side)
            dp = nt(dob, v_at[same])
            dv[same] = dv[same] + tn(p.astype(BF), dob)
            ds = (p * (dp - jnp.sum(p * dp, axis=-1, keepdims=True))).astype(BF)
            part = nn(ds, half_of(k_at[same], side))
            dq = part if dq is None else dq + part
            dk[same] = dk[same] + tn(ds, q)
        s.d_heads[:, block * 128:(block + 1) * 128] = dq * 0.125
    s.d_heads[:, 512:640] = (dk[True] + pltpu.roll(dk[False], 64, 1)) * 0.125
    dvb = (dv[True] + pltpu.roll(dv[False], 64, 1)).astype(BF)
    step(output, ffn_grads, slices[2], slices[3])
    dout = s.d_heads[...]
    dn = dout * cos - partner(dout) * sin
    z_raw = s.z[...]
    r = lax.rsqrt(head_mean(z_raw * z_raw) + EPS)
    zhat = z_raw * r
    dgain = jnp.sum(dn * zhat, axis=0, keepdims=True)
    q_pairs = dgain[:, 0:128] + dgain[:, 128:256] + dgain[:, 256:384] + dgain[:, 384:512]
    q_pairs = q_pairs + pltpu.roll(q_pairs, 64, 1)
    k_pairs = dgain[:, 512:640]
    k_pairs = k_pairs + pltpu.roll(k_pairs, 64, 1)
    dz = dn * head_gain
    dz = r * (dz - zhat * head_mean(dz * zhat))
    low_grads = jnp.concatenate([dz.astype(BF), dvb], axis=1)
    back = nt(low_grads, att[:, :, :, :, 0:768].reshape(2048, 768))
    s.dxn_part[...] = back.astype(BF)
    quad = quad_reduce(net, me, s.dxn_part, s.dxn_core, s.dxn_zl, s.dxn_tmp)
    step(quad, output, ffn_grads)
    grad = tn(s.xn[...], low_grads).astype(BF)
    s.att_part[:, :, :, :, 0:768] = grad.reshape(2, 4, 4, 64, 768)
    step(slices[0], slices[1])


    def tokens_and_gains():
        yield from quad
        d = quad_total(me, s.dxn_part, s.dxn_core, s.dxn_zl)
        t = s.tokens[rows, :].astype(F32)
        r = rows_rms(t)
        hat = t * r
        scaled = d * gain_row(0)
        total = s.dh[...]
        total = total + r * (scaled - hat * jnp.mean(scaled * hat, axis=-1, keepdims=True))
        s.dx[rows, :] = total.astype(BF)
        gain_grad = jnp.sum(d * hat, axis=0, keepdims=True)
        sums = s.gain_sums
        for k in range(8):
            part = slice(k * 256, (k + 1) * 256)
            sums[k:k + 1, 0:256] = gain_grad[:, part]
            sums[k:k + 1, 256:512] = s.ffn_gain_grad[:, part]
        row = lax.broadcasted_iota(jnp.int32, (8, 128), 0)
        head_grad = jnp.where(lanes((8, 128)) < 64, q_pairs, k_pairs)
        sums[:, 512:640] = jnp.where(row == 0, head_grad, 0.0)
        spread = quad_gather(net, me, s.dx)
        step(spread)
        devices = [
            me.core(),
            me.zl_pair(),
            me.zh_pair(),
            me.at(x=x + 1 - 2 * lax.rem(x, 2)),
            me.step("x", 2),
            me.at(y=y + 1 - 2 * lax.rem(y, 2)),
            me.step("y", 2),
        ]
        for k, device in enumerate(devices):
            copy = net.send(sums, s.gain_in.at[k], device)
            yield
            copy.wait_recv()
            net.wait_send(copy)
            sums[...] = sums[...] + s.gain_in[k]
            step(spread)

    rest = tokens_and_gains()
    finish(rest, slices[2], slices[3], slices[0], slices[1], output, ffn_grads)
    net.drain()


def everything(**args):
    in_specs, in_tree = jax.tree.flatten(input_plan())
    out_shapes, out_tree = jax.tree.flatten(output_plan())
    results = pl.pallas_call(
        kernel,
        out_shape=tuple(out_shapes),
        in_specs=in_specs,
        out_specs=[VM] * len(out_shapes),
        scratch_shapes=jax.tree.leaves(scratch_plan()),
        compiler_params=pltpu.CompilerParams(
            vmem_limit_bytes=VMEM_BYTES, collective_id=1, has_side_effects=True
        ),
        name="everything",
    )(*in_tree.flatten_up_to(args))
    return named(jax.tree.unflatten(out_tree, results))


def finish_kernel(
    out_in, dx_in, att, ffn, sums,
    out, dx, gq, gk, gv, go, gate, up, down, attn_gain, ffn_gain, gain_q, gain_k,
):
    out[...] = out_in[...]
    dx[...] = dx_in[...].astype(F32)
    for zl in range(2):
        for ref, start, width in ((gq, 0, 512), (gk, 512, 128), (gv, 640, 128), (go, 768, 512)):
            ref[:, zl * width:(zl + 1) * width] = att[zl, :, start:start + width].astype(F32)
    for m, ref in enumerate((gate, up, down)):
        for k in range(8):
            for c in range(2):
                start = k * 512 + c * 256
                ref[:, start:start + 256] = ffn[m, k, c].astype(F32)
    dp = lax.axis_index("dp")
    row = sums[pl.ds(lax.div(dp, 4), 1), :]
    shift = lax.rem(4 - lax.rem(dp, 4), 4) * 64
    attn_gain[...] = pltpu.roll(row[:, 0:256], shift, 1)[:, 0:64]
    ffn_gain[...] = pltpu.roll(row[:, 256:512], shift, 1)[:, 0:64]
    gain_q[...] = sums[0:1, 512:576]
    gain_k[...] = sums[0:1, 576:640]


def rows_block(*shape):
    n = len(shape)
    return pl.BlockSpec(shape, lambda t: (0,) * (n - 2) + (t, 0))


def whole_block(*shape):
    return pl.BlockSpec(shape, lambda t: (0,) * len(shape))


def finished(r):
    tall = rows_block(32, 2048)
    full, half, wide = (rows_block(16, n) for n in (1024, 256, 4096))
    one = whole_block(1, 64)
    sizes = [(64, 1024), (64, 256), (64, 256), (64, 1024)] + [(64, 4096)] * 3 + [(1, 64)] * 4
    return pl.pallas_call(
        finish_kernel,
        grid=(4,),
        out_shape=(
            jax.ShapeDtypeStruct((128, 2048), BF),
            jax.ShapeDtypeStruct((128, 2048), F32),
        )
        + tuple(jax.ShapeDtypeStruct(size, F32) for size in sizes),
        in_specs=[
            tall, tall, rows_block(2, 16, 1280), rows_block(3, 8, 2, 16, 256), whole_block(8, 640),
        ],
        out_specs=[tall, tall, full, half, half, full, wide, wide, wide, one, one, one, one],
        name="finished",
    )(r.out, r.dx, r.att_grads, r.ffn_grads, r.gain_sums)


def rotary_tables():
    position = np.arange(128, dtype=np.float64)[:, None]
    lane = np.arange(128)
    angle = position * THETA ** (-2.0 * (lane % 32) / 64.0)[None, :]
    sign = np.where(lane % 64 < 32, -1.0, 1.0)
    return np.cos(angle).astype(np.float32), (np.sin(angle) * sign).astype(np.float32)


def on_device(
    tokens, gain_attn, w_query, w_key, w_value, gain_query, gain_key, w_out, gain_ffn,
    w_gate, w_up, w_down, cotangent,
):
    cos, sin = (jnp.asarray(t) for t in rotary_tables())
    dp = lax.axis_index("dp")
    odd = lax.rem(dp, 2)
    lane = lax.broadcasted_iota(jnp.int32, (2, 128), 1)
    two = jnp.stack([gain_attn, gain_ffn])
    placed = jnp.where(lax.div(lane, 64) == odd, jnp.concatenate([two, two], axis=1), 0)
    heads = jnp.concatenate([gain_query, gain_key]).reshape(1, 128)
    small = jnp.concatenate([placed.astype(BF), heads, jnp.zeros((13, 128), BF)], axis=0)
    r = everything(
        tokens=tokens, cot=cotangent, small=small, cos=cos, sin=sin,
        wq=w_query, wk=w_key, wv=w_value, wo=w_out, wg=w_gate, wu=w_up, wd=w_down,
    )
    out, dx, gq, gk, gv, go, gate, up, down, attn, ffn, gain_q, gain_k = finished(r)
    attn, ffn, gain_q, gain_k = (v.reshape(64) for v in (attn, ffn, gain_q, gain_k))
    return out, dx, attn, gq, gk, gv, gain_q, gain_k, go, ffn, gate, up, down


def solution(mesh):
    return jax.shard_map(
        on_device,
        mesh=mesh,
        in_specs=(
            P("dp", None), P("dp"), P("dp", "head"), P("dp", "head"), P("dp", "head"),
            P(), P(), P("dp", "head"), P("dp"),
            P("dp", "tensor"), P("dp", "tensor"), P("dp", "tensor"), P("dp", None),
        ),
        out_specs=(
            P("dp", None), P("dp", None), P("dp"),
            P("dp", "head"), P("dp", "head"), P("dp", "head"),
            P(), P(), P("dp", "head"), P("dp"),
            P("dp", "tensor"), P("dp", "tensor"), P("dp", "tensor"),
        ),
        check_vma=False,
    )
```

```python
import types

import jax
import jax.numpy as jnp
import numpy as np
from jax import lax
from jax.experimental import pallas as pl
from jax.experimental.pallas import tpu as pltpu
from jax.sharding import PartitionSpec as P

BF = jnp.bfloat16
F32 = jnp.float32
MESH = pl.DeviceIdType.MESH
EPS = 1e-05
THETA = 1000000.0
VMEM_BYTES = 62 << 20
ATT_GATHER_SPLIT = 896
ATT_SLICES = ((0, 384, "yx"), (384, 384, "xy"), (768, 256, "yx"), (1024, 256, "xy"))


def nn(a, b):
    return lax.dot_general(a, b, (((1,), (0,)), ((), ())), preferred_element_type=F32)


def nt(a, b):
    return lax.dot_general(a, b, (((1,), (1,)), ((), ())), preferred_element_type=F32)


def tn(a, b):
    return lax.dot_general(a, b, (((0,), (0,)), ((), ())), preferred_element_type=F32)


class Place:
    def __init__(self):
        dp = lax.axis_index("dp")
        self.c = lax.axis_index("head")
        self.zl = lax.axis_index("tensor")
        self.zh = lax.div(dp, 16)
        self.y = lax.rem(lax.div(dp, 4), 4)
        self.x = lax.rem(dp, 4)
        self.z = self.zh * 2 + self.zl

    def at(self, zh=None, y=None, x=None, c=None, zl=None):
        zh = self.zh if zh is None else zh
        y = self.y if y is None else y
        x = self.x if x is None else x
        return (zh * 16 + y * 4 + x, self.c if c is None else c, self.zl if zl is None else zl)

    def step(self, axis, by):
        if axis == "x":
            return self.at(x=lax.rem(self.x + by + 4, 4))
        if axis == "y":
            return self.at(y=lax.rem(self.y + by + 4, 4))
        z = lax.rem(self.z + by + 4, 4)
        return self.at(zh=lax.div(z, 2), zl=lax.rem(z, 2))

    def core(self):
        return self.at(c=1 - self.c)

    def zl_pair(self):
        return self.at(zl=1 - self.zl)

    def zh_pair(self):
        return self.at(zh=1 - self.zh)

    def ring(self, axis):
        return {"x": self.x, "y": self.y, "z": self.z}[axis]


class Copy:
    def __init__(self, copy):
        self.copy = copy
        self.left = True

    def wait_recv(self):
        self.copy.wait_recv()

    def wait_send(self):
        if self.left:
            self.copy.wait_send()
            self.left = False


class Group:
    def __init__(self, sem):
        self.sem = sem

    def wait(self, like):
        pltpu.make_async_copy(like, like, self.sem).wait()


class Net:
    def __init__(self, send_sems, recv_sems):
        self.send_sems = send_sems
        self.recv_sems = recv_sems
        self.slots = [None] * send_sems.shape[0]
        self.sends = 0
        self.groups = 0

    def group(self):
        k = self.groups
        assert k < self.recv_sems.shape[0], k
        self.groups += 1
        return Group(self.recv_sems.at[k])

    def send(self, src, dst, device, group=None):
        slot = self.sends % len(self.slots)
        self.sends += 1
        if self.slots[slot] is not None:
            self.slots[slot].wait_send()
        copy = pltpu.make_async_remote_copy(
            src_ref=src,
            dst_ref=dst,
            send_sem=self.send_sems.at[slot],
            recv_sem=(group or self.group()).sem,
            device_id=device,
            device_id_type=MESH,
        )
        copy.start()
        self.slots[slot] = Copy(copy)
        return self.slots[slot]

    def drain(self):
        for copy in self.slots:
            if copy is not None:
                copy.wait_send()


class Tagged:
    def __init__(self, net):
        self.net = net
        self.copies = []

    def group(self):
        return self.net.group()

    def send(self, src, dst, device, group=None):
        self.copies.append(self.net.send(src, dst, device, group))
        return self.copies[-1]

    def drain(self):
        for copy in self.copies:
            copy.wait_send()


def greet(devices):
    barrier = pltpu.get_barrier_semaphore()
    for device in devices:
        pl.semaphore_signal(barrier, inc=1, device_id=device, device_id_type=MESH)
    pl.semaphore_wait(barrier, len(devices))


def together(*pipelines):
    live = list(pipelines)
    while live:
        for pipe in list(live):
            try:
                next(pipe)
            except StopIteration:
                live.remove(pipe)
        yield


def step(*pipelines):
    for pipe in pipelines:
        next(pipe, None)


def finish(*pipelines):
    for _ in together(*pipelines):
        pass


def local(pairs, sems):
    copies = [pltpu.make_async_copy(s, d, sems.at[i]) for i, (s, d) in enumerate(pairs)]
    for copy in copies:
        copy.start()
    for copy in copies:
        copy.wait()


def add_refs(dst, srcs, rows=32):
    lead, height = dst.shape[:-2], dst.shape[-2]
    rows = min(rows, height)
    per = height // rows
    count = int(np.prod(lead, dtype=np.int64)) * per

    def body(t, carry):
        r = lax.rem(t, per)
        rest = lax.div(t, per)
        index = []
        for size in reversed(lead):
            index.insert(0, lax.rem(rest, size))
            rest = lax.div(rest, size)
        at = tuple(index) + (pl.ds(r * rows, rows), slice(None))
        total = srcs[0][at].astype(F32)
        for src in srcs[1:]:
            total = total + src[at].astype(F32)
        dst[at] = total.astype(dst.dtype)
        return carry

    lax.fori_loop(0, count, body, 0)


def ring_gather(net, place, axis, view, like):
    i = place.ring(axis)
    before, after = lax.rem(i + 3, 4), lax.rem(i + 1, 4)
    up, down = place.step(axis, 1), place.step(axis, -1)
    rest = net.group()
    u0 = net.send(view(i, 0), view(i, 0), up)
    d1 = net.send(view(i, 1), view(i, 1), down)
    net.send(view(i, 1), view(i, 1), up, rest)
    net.send(view(i, 0), view(i, 0), down, rest)
    yield
    u0.wait_recv()
    net.send(view(before, 0), view(before, 0), up, rest)
    d1.wait_recv()
    net.send(view(after, 1), view(after, 1), down, rest)
    yield
    rest.wait(like)


def ring_reduce(net, place, axis, view, far, near, out):
    i = place.ring(axis)
    before, after, across = lax.rem(i + 3, 4), lax.rem(i + 1, 4), lax.rem(i + 2, 4)
    up, down = place.step(axis, 1), place.step(axis, -1)
    fars, nears = net.group(), net.group()
    net.send(view(across, 0), far.at[0], up, fars)
    net.send(view(across, 1), far.at[1], down, fars)
    yield
    net.send(view(after, 1), near.at[1], up, nears)
    net.send(view(before, 0), near.at[2], down, nears)
    yield
    fars.wait(far)
    add_refs(far.at[0], [far.at[0], view(after, 0)])
    net.send(far.at[0], near.at[0], up, nears)
    add_refs(far.at[1], [far.at[1], view(before, 1)])
    net.send(far.at[1], near.at[3], down, nears)
    yield
    nears.wait(near)
    add_refs(out(0), [view(i, 0), near.at[0], near.at[2]])
    add_refs(out(1), [view(i, 1), near.at[1], near.at[3]])


def cross_gather(net, place, one, two, view, likes, late=None, also=None, only=None):
    ring = [lax.rem(place.ring(one) + k, 4) for k in range(4)]
    other = [lax.rem(place.ring(two) + k, 4) for k in range(4)]
    up = {one: place.step(one, 1), two: place.step(two, 1)}
    down = {one: place.step(one, -1), two: place.step(two, -1)}
    corners = []
    last = [net.group(), net.group()]
    finals = [[], []]

    def spread(block, axis, group):
        net.send(block, block, up[axis], group)
        net.send(block, block, down[axis], group)

    def arrived(block):
        if also is not None:
            also(block)
        return block

    def along(axis, part, k, half=None):
        if axis == one:
            return view(part, ring[k], other[0], half)
        return view(part, ring[0], other[k], half)

    def turn(axis, part, k):
        across = two if axis == one else one
        half = 1 if axis == one else 0
        if only is not None and half != only:
            return
        group = net.group()
        spread(along(axis, part, k, half), across, group)
        corners.append((axis, part, k, half, across, group))

    def own(part):
        group = net.group()
        block = view(part, ring[0], other[0], None)
        for axis in (one, two):
            spread(block, axis, group)
        return group

    crosses = [own(0)]
    if late is None:
        crosses.append(own(1))
    yield
    if late is not None:
        late.wait_recv()
        crosses.append(own(1))
        yield
    far = net.group()
    for part in (0, 1):
        crosses[part].wait(likes(None, 4))
        order = (3, 1) if part == 0 else (1, 3)
        for n, k in enumerate(order):
            for axis in (one, two):
                block = arrived(along(axis, part, k))
                if n == 0:
                    net.send(block, block, (up, down)[part][axis], far)
                turn(axis, part, k)
        yield
    far.wait(likes(None, 4))
    for part in (0, 1):
        for axis in (one, two):
            arrived(along(axis, part, 2))
            turn(axis, part, 2)
    yield
    for n, (axis, part, k, half, across, group) in enumerate(corners):
        group.wait(likes(half, 2))
        for which, by in ((0, 3), (1, 1)):
            if axis == one:
                block = view(part, ring[k], other[by], half)
                final = view(part, ring[k], other[2], half)
            else:
                block = view(part, ring[by], other[k], half)
                final = view(part, ring[2], other[k], half)
            arrived(block)
            if which == part:
                net.send(block, block, (up, down)[part][across], last[half])
                finals[half].append(final)
        if n % 4 == 3:
            yield
    for half in (0, 1):
        if finals[half]:
            last[half].wait(likes(half, len(finals[half])))
            for final in finals[half]:
                arrived(final)


def order_reduce(net, place, one, two, view, s, out):
    ring = [lax.rem(place.ring(one) + k, 4) for k in range(4)]
    other = [lax.rem(place.ring(two) + k, 4) for k in range(4)]
    up, down = place.step(one, 1), place.step(one, -1)
    order = (2, 1, 3, 0)
    fars = {k: net.group() for k in order}
    nears = {k: net.group() for k in order}
    others = net.group()
    for k in order:
        net.send(view(0, ring[2], other[k]), s.far.at[k, 0], up, fars[k])
        net.send(view(1, ring[2], other[k]), s.far.at[k, 1], down, fars[k])
    for k in order:
        net.send(view(1, ring[1], other[k]), s.near.at[k, 1], up, nears[k])
        net.send(view(0, ring[3], other[k]), s.near.at[k, 2], down, nears[k])
    yield
    for k in order:
        fars[k].wait(s.far.at[k])
        add_refs(s.far.at[k, 0], [s.far.at[k, 0], view(0, ring[1], other[k])])
        net.send(s.far.at[k, 0], s.near.at[k, 0], up, nears[k])
        add_refs(s.far.at[k, 1], [s.far.at[k, 1], view(1, ring[3], other[k])])
        net.send(s.far.at[k, 1], s.near.at[k, 3], down, nears[k])
        if k != 1:
            yield
    for k in order:
        nears[k].wait(s.near.at[k])
        for p in (0, 1):
            add_refs(
                s.mid.at[k, p],
                [view(p, ring[0], other[k]), s.near.at[k, p], s.near.at[k, 2 + p]],
            )
        if k:
            net.send(s.mid.at[k], s.last.at[k - 1], place.step(two, k), others)
        if k != 1:
            yield
    others.wait(s.last)
    for p in (0, 1):
        add_refs(out(p), [s.mid.at[0, p]] + [s.last.at[k, p] for k in range(3)])


def order_buffers(rows, columns):
    return dict(
        far=pltpu.VMEM((4, 2, rows, columns), BF),
        near=pltpu.VMEM((4, 4, rows, columns), BF),
        mid=pltpu.VMEM((4, 2, rows, columns), BF),
        last=pltpu.VMEM((3, 2, rows, columns), BF),
    )


def torus_gather(net, place, buf, only=None):
    c = place.c
    other = place.core()
    swaps = net.group()

    def also(block):
        net.send(block, block, other, swaps)

    def rows(half):
        return pl.ds(0, 32) if half is None or only is not None else pl.ds(half * 16, 16)

    def view(part, i, j, half):
        return buf.at[i, j, c, rows(half), pl.ds(part * 1024, 1024)]

    def likes(half, n):
        return buf.at[pl.ds(0, 2), pl.ds(0, n // 2), 0, rows(half), pl.ds(0, 1024)]

    also(buf.at[place.z, place.x, c])
    yield from cross_gather(net, place, "z", "x", view, likes, also=also, only=only)
    yield
    swaps.wait(buf.at[:, :, 1 - c])


def torus_buffers():
    return dict(
        both=pltpu.VMEM((4, 4, 32, 2048), BF),
        halves=[order_buffers(16, 1024), order_buffers(16, 1024)],
        total=pltpu.VMEM((32, 2048), F32),
    )


def torus_reduce(net, place, src, swaps, s):
    c = place.c
    for k, swap in enumerate(swaps):
        swap.wait_recv()
        add_refs(s.both.at[k], [s.both.at[k], src.at[k, :, c]])

    def part_of(half, part):
        return pl.ds(half * 16, 16), pl.ds(part * 1024, 1024)

    yield from together(
        order_reduce(
            net, place, "z", "x", lambda p, i, j: s.both.at[(i, j) + part_of(0, p)],
            s.halves[0], lambda p: s.total.at[part_of(0, p)],
        ),
        order_reduce(
            net, place, "x", "z", lambda p, i, j: s.both.at[(j, i) + part_of(1, p)],
            s.halves[1], lambda p: s.total.at[part_of(1, p)],
        ),
    )


def quad_gather(net, place, buf):
    c, zl = place.c, place.zl
    own = buf.at[pl.ds(c * 64 + zl * 32, 32)]
    one = net.send(own, own, place.zl_pair())
    yield
    one.wait_recv()
    half = buf.at[pl.ds(c * 64, 64)]
    two = net.send(half, half, place.core())
    yield
    two.wait_recv()


def quad_reduce(net, place, src, from_core, from_zl, tmp):
    c, zl = place.c, place.zl
    one = net.send(src.at[pl.ds((1 - c) * 64, 64)], from_core, place.core())
    yield
    one.wait_recv()
    theirs = src[pl.ds(c * 64 + (1 - zl) * 32, 32), :].astype(F32)
    tmp[...] = (theirs + from_core[pl.ds((1 - zl) * 32, 32), :].astype(F32)).astype(BF)
    two = net.send(tmp, from_zl, place.zl_pair())
    yield
    two.wait_recv()


def quad_total(place, src, from_core, from_zl):
    c, zl = place.c, place.zl
    mine = src[pl.ds(c * 64 + zl * 32, 32), :].astype(F32)
    mine = mine + from_core[pl.ds(zl * 32, 32), :].astype(F32)
    return mine + from_zl[...].astype(F32)


def sem_scratch(n):
    return [pltpu.SemaphoreType.DMA((n,)), pltpu.SemaphoreType.DMA((n,))]


ANY = pl.BlockSpec(memory_space=pl.ANY)
VM = pl.BlockSpec(memory_space=pltpu.VMEM)


def lanes(shape):
    return lax.broadcasted_iota(jnp.int32, shape, len(shape) - 1)


def partner(v):
    n = v.shape[-1]
    low = lax.rem(lanes(v.shape), 64) < 32
    return jnp.where(low, pltpu.roll(v, n - 32, 1), pltpu.roll(v, 32, 1))


def head_mean(v):
    n = v.shape[-1]
    r = lax.broadcasted_iota(jnp.int32, (n, n), 0)
    same = lax.div(r, 64) == lax.div(lanes((n, n)), 64)
    return lax.dot_general(
        v, jnp.where(same, 1.0 / 64.0, 0.0), (((1,), (0,)), ((), ())),
        precision=lax.Precision.HIGHEST, preferred_element_type=F32,
    )


def half_of(v, which):
    upper = lanes(v.shape) >= 64
    keep = upper if which else jnp.logical_not(upper)
    return jnp.where(keep, v, jnp.zeros_like(v))


def swap_halves(v):
    return pltpu.roll(v.astype(F32), 64, 1).astype(v.dtype)


def rows_rms(v):
    return lax.rsqrt(jnp.mean(v * v, axis=-1, keepdims=True) + EPS)


N_SENDS = 64
N_GROUPS = 190
N_LOCAL = 13


def input_plan():
    return dict(
        tokens=ANY, cot=ANY, small=ANY, cos=ANY, sin=ANY,
        wq=ANY, wk=ANY, wv=ANY, wo=ANY, wg=ANY, wu=ANY, wd=ANY,
    )


def output_plan():
    return dict(
        out=jax.ShapeDtypeStruct((128, 2048), BF),
        dx=jax.ShapeDtypeStruct((128, 2048), BF),
        att_grads=jax.ShapeDtypeStruct((2, 64, 1280), BF),
        ffn_grads=jax.ShapeDtypeStruct((3, 8, 2, 64, 256), BF),
        gain_sums=jax.ShapeDtypeStruct((8, 640), F32),
    )


def scratch_plan():
    return dict(
        tok=pltpu.VMEM((128, 2048), BF),
        small_in=pltpu.VMEM((16, 128), BF),
        cos_in=pltpu.VMEM((128, 128), F32),
        sin_in=pltpu.VMEM((128, 128), F32),
        att=pltpu.VMEM((2, 4, 4, 64, 1280), BF),
        gains=pltpu.VMEM((2, 4, 4, 16, 128), BF),
        ffn=pltpu.VMEM((3, 2, 4, 4, 64, 256), BF),
        cots=pltpu.VMEM((4, 4, 2, 32, 2048), BF),
        xn2=pltpu.VMEM((4, 4, 2, 32, 2048), BF),
        xn=pltpu.VMEM((128, 2048), BF),
        z=pltpu.VMEM((128, 640), F32),
        qk=pltpu.VMEM((128, 640), BF),
        v=pltpu.VMEM((128, 128), BF),
        p=pltpu.VMEM((8, 128, 128), F32),
        o=pltpu.VMEM((128, 512), BF),
        branch=pltpu.VMEM((128, 2048), BF),
        hidden=pltpu.VMEM((32, 2048), F32),
        branch_core=pltpu.VMEM((64, 2048), BF),
        branch_zl=pltpu.VMEM((32, 2048), BF),
        branch_tmp=pltpu.VMEM((32, 2048), BF),
        da=pltpu.VMEM((4, 256, 256), F32),
        ab=pltpu.VMEM((4, 256, 256), BF),
        dg=pltpu.VMEM((4, 256, 256), BF),
        du=pltpu.VMEM((4, 256, 256), BF),
        dxn2_part=pltpu.VMEM((4, 4, 2, 32, 2048), BF),
        ffn_part=pltpu.VMEM((3, 2, 4, 4, 64, 256), BF),
        ffn_far=pltpu.VMEM((4, 2, 3, 64, 256), BF),
        ffn_near=pltpu.VMEM((4, 4, 3, 64, 256), BF),
        ffn_mid=pltpu.VMEM((4, 2, 3, 64, 256), BF),
        dh=pltpu.VMEM((32, 2048), F32),
        dhb=pltpu.VMEM((128, 2048), BF),
        ffn_gain_grad=pltpu.VMEM((1, 2048), F32),
        d_heads=pltpu.VMEM((128, 640), F32),
        att_part=pltpu.VMEM((2, 4, 4, 64, 1280), BF),
        dxn_part=pltpu.VMEM((128, 2048), BF),
        dxn_core=pltpu.VMEM((64, 2048), BF),
        dxn_zl=pltpu.VMEM((32, 2048), BF),
        dxn_tmp=pltpu.VMEM((32, 2048), BF),
        both_z=pltpu.VMEM((2, 64, 1280), BF),
        from_z=pltpu.VMEM((2, 2, 64, 1280), BF),
        gain_quad=pltpu.VMEM((4, 8, 640), F32),
        gain_y=pltpu.VMEM((4, 8, 640), F32),
        gain_xz=pltpu.VMEM((8, 8, 640), F32),
        dxn2_sum=torus_buffers(),
        out_sum=torus_buffers(),
        slices=[order_buffers(64, n) for _, n, _ in ATT_SLICES],
        send_sems=pltpu.SemaphoreType.DMA((N_SENDS,)),
        recv_sems=pltpu.SemaphoreType.DMA((N_GROUPS,)),
        sems=pltpu.SemaphoreType.DMA((N_LOCAL,)),
    )


def named(plan):
    if isinstance(plan, dict):
        return types.SimpleNamespace(**{k: named(v) for k, v in plan.items()})
    if isinstance(plan, list):
        return [named(v) for v in plan]
    return plan


def kernel(*refs):
    s = types.SimpleNamespace()
    for plan in (input_plan(), output_plan(), scratch_plan()):
        leaves, tree = jax.tree.flatten(plan)
        part = jax.tree.unflatten(tree, refs[: len(leaves)])
        refs = refs[len(leaves):]
        vars(s).update(vars(named(part)))
    send_sems, recv_sems, sems = s.send_sems, s.recv_sems, s.sems
    me = Place()
    zh, y, x, c, zl, z = me.zh, me.y, me.x, me.c, me.zl, me.z
    net = Net(send_sems, recv_sems)
    att, ffn = s.att, s.ffn
    rows = pl.ds(c * 64 + zl * 32, 32)


    def piece(k):
        return pl.ds(pl.multiple_of(k * 512 + c * 256, 256), 256)

    def load(pairs):
        started = []
        for src, dst in pairs:
            started.append(pltpu.make_async_copy(src, dst, sems.at[len(loads)]))
            loads.append(started[-1])
            started[-1].start()
        return started

    loads = []
    own = att.at[zh, y, x]
    wide = pl.ds(pl.multiple_of(zl * 512, 512), 512)
    narrow = pl.ds(pl.multiple_of(zl * 128, 128), 128)
    mine = zh * 4 + x
    att_copies = load(
        [
            (s.wq.at[:, wide], own.at[:, pl.ds(0, 512)]),
            (s.wk.at[:, narrow], own.at[:, pl.ds(512, 128)]),
            (s.wv.at[:, narrow], own.at[:, pl.ds(640, 128)]),
            (s.wo.at[:, wide], own.at[:, pl.ds(768, 512)]),
        ]
    )
    (small_copy,) = load([(s.small, s.small_in)])
    (cots_copy,) = load([(s.cot.at[rows], s.cots.at[z, x, c])])
    ffn_copies = load(
        [(w.at[:, piece(mine)], ffn.at[m, zh, y, x]) for m, w in enumerate((s.wg, s.wu, s.wd))]
    )
    other_copies = load([(s.tokens, s.tok), (s.cos, s.cos_in), (s.sin, s.sin_in)])
    greet(
        [me.step("x", 1), me.step("x", 2), me.step("x", -1)]
        + [me.step("y", 1), me.step("y", 2), me.step("y", -1)]
        + [me.step("z", 1), me.step("z", 2), me.step("z", -1)]
        + [me.core(), me.at(c=1 - c, zl=1 - zl)]
        + [me.at(zh=1 - zh, x=lax.rem(x + k, 4)) for k in (1, 2, 3)]
    )

    def gather_attention():
        swap = net.send(own, own, me.zh_pair())
        halves = (
            pl.ds(0, ATT_GATHER_SPLIT),
            pl.ds(ATT_GATHER_SPLIT, 1280 - ATT_GATHER_SPLIT),
        )

        def view(part, i, j, half):
            block = att.at[1 - zh if part else zh, i, j]
            return block if half is None else block.at[:, halves[half]]

        def likes(half, n):
            cols = slice(None) if half is None else halves[half]
            return att.at[:, 0, pl.ds(0, n // 2), :, cols]

        yield from cross_gather(net, me, "y", "x", view, likes, late=swap)

    def gather_ffn():
        arrivals = [net.group(), net.group()]
        for dz in (0, 1):
            for dx in range(4):
                if dz == 0 and dx == 0:
                    continue
                tx = lax.rem(x + dx, 4)
                tz = 1 - zh if dz else zh
                for m, w in enumerate((s.wg, s.wu, s.wd)):
                    net.send(
                        w.at[:, piece(tz * 4 + tx)],
                        ffn.at[m, zh, y, x],
                        me.at(zh=tz, x=tx),
                        arrivals[dz],
                    )
        yield
        arrivals[0].wait(s.ffn_part.at[:, 0, 0, pl.ds(0, 3)])
        arrivals[1].wait(s.ffn_part.at[:, 0, 0])
        for copy in ffn_copies:
            copy.wait()
        yield from ring_gather(
            net, me, "y", lambda i, p: ffn.at[:, p, i], s.ffn_part.at[:, 0]
        )

    def gather_gains():
        own_gain = s.gains.at[zh, y, x]
        near, far = net.group(), net.group()
        for k in range(4):
            device = lax.rem(x + k, 4)
            if k:
                net.send(own_gain, own_gain, me.at(x=device), near)
            net.send(own_gain, own_gain, me.at(zh=1 - zh, x=device), far)
        yield
        near.wait(s.gains.at[0, 0, pl.ds(0, 3)])
        far.wait(s.gains.at[0, 0])
        row = s.gains.at[:, y]
        group = net.group()
        for k in (1, -1, 2):
            net.send(row, row, me.step("y", k), group)
        yield
        group.wait(s.gains.at[:, pl.ds(0, 3)])

    def gain_row(k):
        blocks = []
        for pair in range(16):
            a, b = 2 * pair, 2 * pair + 1
            total = None
            for d in (a, b):
                block = s.gains[d // 16, d // 4 % 4, d % 4].astype(F32)
                total = block if total is None else total + block
            blocks.append(total[k:k + 1, :])
        return jnp.concatenate(blocks, axis=1)

    for copy in att_copies:
        copy.wait()
    attention = gather_attention()
    gains = gather_gains()
    weights = gather_ffn()
    cots = torus_gather(net, me, s.cots, only=0)
    step(attention)
    small_copy.wait()
    small = s.small_in[...].astype(F32)
    s.gains[zh, y, x] = jnp.where(lax.rem(x, 2) == 1, pltpu.roll(small, 64, 1), small).astype(BF)
    step(gains, attention, attention, gains, attention)
    cots_copy.wait()
    step(cots, attention, weights, attention, cots)
    finish(gains)
    for copy in other_copies:
        copy.wait()
    t = s.tok[...].astype(F32)
    s.xn[...] = (t * rows_rms(t) * gain_row(0)).astype(BF)
    step(attention, attention, cots, attention, attention, cots)
    finish(attention)


    step(weights, cots)
    raw = nn(s.xn[...], att[:, :, :, :, 0:768].reshape(2048, 768))
    z_raw = raw[:, 0:640]
    s.z[...] = z_raw
    v = raw[:, 640:768].astype(BF)
    s.v[...] = v
    step(cots)
    both_gains = small[2:3, :]
    turned = pltpu.roll(both_gains, 64, 1)
    low = lanes((1, 128)) < 64
    gain_q = jnp.where(low, both_gains, turned)
    gain_k = jnp.where(low, turned, both_gains)
    head_gain = jnp.concatenate([gain_q] * 4 + [gain_k], axis=1)
    cos = jnp.concatenate([s.cos_in[...]] * 5, axis=1)
    sin = jnp.concatenate([s.sin_in[...]] * 5, axis=1)
    n = z_raw * lax.rsqrt(head_mean(z_raw * z_raw) + EPS) * head_gain
    s.qk[...] = (n * cos + partner(n) * sin).astype(BF)
    step(cots)
    k = s.qk[:, 512:640]
    k_at = {True: k, False: swap_halves(k)}
    v_at = {True: v, False: swap_halves(v)}
    causal = lax.broadcasted_iota(jnp.int32, (128, 128), 0) >= lanes((128, 128))
    for block in range(4):
        out = None
        for side in range(2):
            h = 2 * block + side
            same = side == h // 4
            q = half_of(s.qk[:, block * 128:(block + 1) * 128], side)
            score = jnp.where(causal, nt(q, k_at[same]) * 0.125, -1e30)
            e = jnp.exp(score - jnp.max(score, axis=-1, keepdims=True))
            p = e / jnp.sum(e, axis=-1, keepdims=True)
            s.p[h] = p
            part = nn(p.astype(BF), half_of(v_at[same], side))
            out = part if out is None else out + part
        s.o[:, block * 128:(block + 1) * 128] = out.astype(BF)
    s.branch[...] = nt(s.o[...], att[:, :, :, :, 768:1280].reshape(2048, 512)).astype(BF)
    quad = quad_reduce(
        net, me, s.branch, s.branch_core, s.branch_zl, s.branch_tmp
    )
    step(quad, cots)
    finish(quad)
    hidden = s.tok[rows, :].astype(F32)
    hidden = hidden + quad_total(me, s.branch, s.branch_core, s.branch_zl)
    s.hidden[...] = hidden
    s.xn2[z, x, c] = (hidden * rows_rms(hidden) * gain_row(1)).astype(BF)
    normed_net = Tagged(net)
    normed = torus_gather(normed_net, me, s.xn2)
    step(normed, normed, weights, normed)
    finish(cots)
    step(normed, normed)
    finish(weights)


    def weight(m):
        return ffn[m].reshape(2048, 256)

    for k in range(4):
        s.da[k] = nn(s.cots[k].reshape(256, 2048), weight(2))
        step(normed)
    finish(normed)
    swaps = []
    for k in range(4):
        xk = s.xn2[k].reshape(256, 2048)
        g, u, da = nn(xk, weight(0)), nn(xk, weight(1)), s.da[k]
        sigma = jax.nn.sigmoid(g)
        swish = g * sigma
        s.ab[k] = (swish * u).astype(BF)
        dg = (da * u * sigma * (1.0 + g * (1.0 - sigma))).astype(BF)
        du = (da * swish).astype(BF)
        s.dg[k] = dg
        s.du[k] = du
        part = (nt(dg, weight(0)) + nt(du, weight(1))).astype(BF)
        s.dxn2_part[k] = part.reshape(4, 2, 32, 2048)
        swaps.append(
            net.send(s.dxn2_part.at[k, :, 1 - c], s.dxn2_sum.both.at[k], me.core())
        )


    dxn2 = torus_reduce(net, me, s.dxn2_part, swaps, s.dxn2_sum)
    step(dxn2)

    def weight_grads(k):
        yk = lax.rem(y + k, 4)

        def one(p, carry):
            cols = pl.ds(pl.multiple_of((p * 4 + yk) * 256, 256), 256)
            xd = s.xn2[:, :, :, :, cols].reshape(1024, 256)
            dyd = s.cots[:, :, :, :, cols].reshape(1024, 256)
            for m, left, right in ((0, xd, s.dg), (1, xd, s.du), (2, dyd, s.ab)):
                grad = tn(left, right[...].reshape(1024, 256))
                s.ffn_part[m, p, yk] = grad.astype(BF).reshape(4, 64, 256)
            return carry

        lax.fori_loop(0, 2, one, 0)

    def reduce_ffn_grads():
        part, grads = s.ffn_part, s.ffn_grads
        arrivals = [net.group(), net.group()]
        dst = grads.at[:, mine, c]
        keep = pltpu.make_async_copy(s.ffn_mid.at[0, zh], dst, sems.at[N_LOCAL - 1])

        def block(k):
            xk = lax.rem(x + k, 4)
            far, near, mid = (ref.at[k] for ref in (s.ffn_far, s.ffn_near, s.ffn_mid))
            yield from ring_reduce(
                net, me, "y", lambda i, p: part.at[:, p, i, xk], far, near, lambda p: mid.at[p]
            )
            if k:
                net.send(mid.at[zh], dst, me.at(x=xk), arrivals[0])
            else:
                keep.start()
            net.send(mid.at[1 - zh], dst, me.at(zh=1 - zh, x=xk), arrivals[1])

        yield from together(*[block(k) for k in (2, 1, 3, 0)])
        keep.wait()
        arrivals[0].wait(s.ffn_part.at[:, 0, 0, pl.ds(0, 3)])
        arrivals[1].wait(s.ffn_part.at[:, 0, 0])
        swap = net.send(grads.at[:, :, c], grads.at[:, :, c], me.core())
        yield
        swap.wait_recv()

    ffn_grads = reduce_ffn_grads()
    weight_grads(2)
    step(ffn_grads)
    weight_grads(1)
    weight_grads(3)
    step(ffn_grads, dxn2, dxn2)
    weight_grads(0)
    step(dxn2)
    swaps = []
    normed_net.drain()
    for k in range(4):
        part = nt(s.ab[k], weight(2)).astype(BF)
        s.xn2[k] = part.reshape(4, 2, 32, 2048)
        swaps.append(net.send(s.xn2.at[k, :, 1 - c], s.out_sum.both.at[k], me.core()))
        if k % 2 == 1:
            step(dxn2)
    finish(dxn2)
    hidden = s.hidden[...]
    r = rows_rms(hidden)
    hat = hidden * r
    d = s.dxn2_sum.total[...]
    s.ffn_gain_grad[...] = jnp.sum(d * hat, axis=0, keepdims=True)
    scaled = d * gain_row(1)
    dh = s.cots[z, x, c].astype(F32)
    dh = dh + r * (scaled - hat * jnp.mean(scaled * hat, axis=-1, keepdims=True))
    s.dh[...] = dh
    s.dhb[rows, :] = dh.astype(BF)
    spread = quad_gather(net, me, s.dhb)
    step(spread)

    def finish_output():
        yield from torus_reduce(net, me, s.xn2, swaps, s.out_sum)
        s.out[rows, :] = (s.hidden[...] + s.out_sum.total[...]).astype(BF)
        yield from quad_gather(net, me, s.out)

    output = finish_output()
    step(spread, output)
    finish(spread)


    def reduce_att_grads(k):
        start, width, order = ATT_SLICES[k]
        cols = pl.ds(start, width)
        part, both_z = s.att_part, s.both_z

        def view(p, i, j):
            yi, xi = (i, j) if order == "yx" else (j, i)
            return part.at[p, yi, xi, :, cols]

        yield from order_reduce(
            net, me, order[0], order[1], view, s.slices[k], lambda p: both_z.at[p, :, cols]
        )
        arrivals = net.group()
        mine_z = both_z.at[zh, :, cols]
        theirs = both_z.at[1 - zh, :, cols]
        net.send(theirs, s.from_z.at[zl, 1, :, cols], me.at(zh=1 - zh), arrivals)
        net.send(theirs, s.from_z.at[zl, 1, :, cols], me.at(zh=1 - zh, zl=1 - zl), arrivals)
        net.send(mine_z, s.from_z.at[zl, 0, :, cols], me.at(zl=1 - zl), arrivals)
        yield
        arrivals.wait(s.slices[k].last.at[:, 0])
        add_refs(s.att_grads.at[zl, :, cols], [mine_z, s.from_z.at[zl, 1, :, cols]])
        add_refs(
            s.att_grads.at[1 - zl, :, cols],
            [s.from_z.at[1 - zl, 0, :, cols], s.from_z.at[1 - zl, 1, :, cols]],
        )

    dhb = s.dhb[...]
    grad = tn(dhb, s.o[...]).astype(BF)
    s.att_part[:, :, :, :, 768:1280] = grad.reshape(2, 4, 4, 64, 512)
    slices = [reduce_att_grads(k) for k in range(4)]
    step(slices[2], slices[3])
    do = nn(dhb, att[:, :, :, :, 768:1280].reshape(2048, 512)).astype(BF)
    step(output)
    v = s.v[...]
    k = s.qk[:, 512:640]
    k_at = {True: k, False: swap_halves(k)}
    v_at = {True: v, False: swap_halves(v)}
    zero = jnp.zeros((128, 128), F32)
    dk = {True: zero, False: zero}
    dv = {True: zero, False: zero}
    for block in range(4):
        dq = None
        for side in range(2):
            h = 2 * block + side
            same = side == h // 4
            p = s.p[h]
            dob = half_of(do[:, block * 128:(block + 1) * 128], side)
            q = half_of(s.qk[:, block * 128:(block + 1) * 128], side)
            dp = nt(dob, v_at[same])
            dv[same] = dv[same] + tn(p.astype(BF), dob)
            ds = (p * (dp - jnp.sum(p * dp, axis=-1, keepdims=True))).astype(BF)
            part = nn(ds, half_of(k_at[same], side))
            dq = part if dq is None else dq + part
            dk[same] = dk[same] + tn(ds, q)
        s.d_heads[:, block * 128:(block + 1) * 128] = dq * 0.125
    s.d_heads[:, 512:640] = (dk[True] + pltpu.roll(dk[False], 64, 1)) * 0.125
    dvb = (dv[True] + pltpu.roll(dv[False], 64, 1)).astype(BF)
    step(output, ffn_grads, slices[2], slices[3])
    dout = s.d_heads[...]
    dn = dout * cos - partner(dout) * sin
    z_raw = s.z[...]
    r = lax.rsqrt(head_mean(z_raw * z_raw) + EPS)
    zhat = z_raw * r
    dgain = jnp.sum(dn * zhat, axis=0, keepdims=True)
    q_pairs = dgain[:, 0:128] + dgain[:, 128:256] + dgain[:, 256:384] + dgain[:, 384:512]
    q_pairs = q_pairs + pltpu.roll(q_pairs, 64, 1)
    k_pairs = dgain[:, 512:640]
    k_pairs = k_pairs + pltpu.roll(k_pairs, 64, 1)
    dz = dn * head_gain
    dz = r * (dz - zhat * head_mean(dz * zhat))
    low_grads = jnp.concatenate([dz.astype(BF), dvb], axis=1)
    grad = tn(s.xn[...], low_grads).astype(BF)
    s.att_part[:, :, :, :, 0:768] = grad.reshape(2, 4, 4, 64, 768)
    step(slices[0], slices[1])
    back = nt(low_grads, att[:, :, :, :, 0:768].reshape(2048, 768))
    s.dxn_part[...] = back.astype(BF)
    quad = quad_reduce(net, me, s.dxn_part, s.dxn_core, s.dxn_zl, s.dxn_tmp)
    step(quad, output)


    def tokens_and_gains():
        yield from quad
        d = quad_total(me, s.dxn_part, s.dxn_core, s.dxn_zl)
        t = s.tok[rows, :].astype(F32)
        r = rows_rms(t)
        hat = t * r
        scaled = d * gain_row(0)
        total = s.dh[...]
        total = total + r * (scaled - hat * jnp.mean(scaled * hat, axis=-1, keepdims=True))
        s.dx[rows, :] = total.astype(BF)
        gain_grad = jnp.sum(d * hat, axis=0, keepdims=True)
        sums = s.gain_sums
        for k in range(8):
            part = slice(k * 256, (k + 1) * 256)
            sums[k:k + 1, 0:256] = gain_grad[:, part]
            sums[k:k + 1, 256:512] = s.ffn_gain_grad[:, part]
        row = lax.broadcasted_iota(jnp.int32, (8, 128), 0)
        head_grad = jnp.where(lanes((8, 128)) < 64, q_pairs, k_pairs)
        sums[:, 512:640] = jnp.where(row == 0, head_grad, 0.0)
        spread = quad_gather(net, me, s.dx)
        step(spread)

        def total(buf, own, devices):
            group = net.group()
            for device in devices:
                net.send(buf.at[own], buf.at[own], device, group)
            yield
            group.wait(buf.at[pl.ds(0, len(devices))])
            step(spread)
            sums[...] = sum(buf[k] for k in range(1, len(devices) + 1)) + buf[0]

        s.gain_quad[c * 2 + zl] = sums[...]
        yield from total(
            s.gain_quad, c * 2 + zl, [me.core(), me.zl_pair(), me.at(c=1 - c, zl=1 - zl)]
        )
        s.gain_y[y] = sums[...]
        yield from total(s.gain_y, y, [me.step("y", k) for k in (1, 2, 3)])
        s.gain_xz[mine] = sums[...]
        yield from total(
            s.gain_xz,
            mine,
            [me.step("x", k) for k in (1, 2, 3)]
            + [me.at(zh=1 - zh, x=lax.rem(x + k, 4)) for k in range(4)],
        )
        finish(spread)

    rest = tokens_and_gains()
    finish(rest, slices[2], slices[3], output, ffn_grads, slices[0], slices[1])
    net.drain()


def everything(**args):
    in_specs, in_tree = jax.tree.flatten(input_plan())
    out_shapes, out_tree = jax.tree.flatten(output_plan())
    results = pl.pallas_call(
        kernel,
        out_shape=tuple(out_shapes),
        in_specs=in_specs,
        out_specs=[VM] * len(out_shapes),
        scratch_shapes=jax.tree.leaves(scratch_plan()),
        compiler_params=pltpu.CompilerParams(
            vmem_limit_bytes=VMEM_BYTES, collective_id=1, has_side_effects=True
        ),
        name="everything",
    )(*in_tree.flatten_up_to(args))
    return named(jax.tree.unflatten(out_tree, results))


def finish_kernel(
    out_in, dx_in, att, ffn, sums,
    out, dx, gq, gk, gv, go, gate, up, down, attn_gain, ffn_gain, gain_q, gain_k,
):
    out[...] = out_in[...]
    dx[...] = dx_in[...].astype(F32)
    for zl in range(2):
        for ref, start, width in ((gq, 0, 512), (gk, 512, 128), (gv, 640, 128), (go, 768, 512)):
            ref[:, zl * width:(zl + 1) * width] = att[zl, :, start:start + width].astype(F32)
    for m, ref in enumerate((gate, up, down)):
        for k in range(8):
            for c in range(2):
                start = k * 512 + c * 256
                ref[:, start:start + 256] = ffn[m, k, c].astype(F32)
    dp = lax.axis_index("dp")
    row = sums[pl.ds(lax.div(dp, 4), 1), :]
    shift = lax.rem(4 - lax.rem(dp, 4), 4) * 64
    attn_gain[...] = pltpu.roll(row[:, 0:256], shift, 1)[:, 0:64]
    ffn_gain[...] = pltpu.roll(row[:, 256:512], shift, 1)[:, 0:64]
    gain_q[...] = sums[0:1, 512:576]
    gain_k[...] = sums[0:1, 576:640]


def rows_block(*shape):
    n = len(shape)
    return pl.BlockSpec(shape, lambda t: (0,) * (n - 2) + (t, 0))


def whole_block(*shape):
    return pl.BlockSpec(shape, lambda t: (0,) * len(shape))


def finished(r):
    tall = rows_block(32, 2048)
    full, half, wide = (rows_block(16, n) for n in (1024, 256, 4096))
    one = whole_block(1, 64)
    sizes = [(64, 1024), (64, 256), (64, 256), (64, 1024)] + [(64, 4096)] * 3 + [(1, 64)] * 4
    return pl.pallas_call(
        finish_kernel,
        grid=(4,),
        out_shape=(
            jax.ShapeDtypeStruct((128, 2048), BF),
            jax.ShapeDtypeStruct((128, 2048), F32),
        )
        + tuple(jax.ShapeDtypeStruct(size, F32) for size in sizes),
        in_specs=[
            tall, tall, rows_block(2, 16, 1280), rows_block(3, 8, 2, 16, 256), whole_block(8, 640),
        ],
        out_specs=[tall, tall, full, half, half, full, wide, wide, wide, one, one, one, one],
        name="finished",
    )(r.out, r.dx, r.att_grads, r.ffn_grads, r.gain_sums)


def rotary_tables():
    position = np.arange(128, dtype=np.float64)[:, None]
    lane = np.arange(128)
    angle = position * THETA ** (-2.0 * (lane % 32) / 64.0)[None, :]
    sign = np.where(lane % 64 < 32, -1.0, 1.0)
    return np.cos(angle).astype(np.float32), (np.sin(angle) * sign).astype(np.float32)


def on_device(
    tokens, gain_attn, w_query, w_key, w_value, gain_query, gain_key, w_out, gain_ffn,
    w_gate, w_up, w_down, cotangent,
):
    cos, sin = (jnp.asarray(t) for t in rotary_tables())
    rows = [jnp.pad(v, (0, 64)).reshape(1, 128) for v in (gain_attn, gain_ffn)]
    rows.append(jnp.concatenate([gain_query, gain_key]).reshape(1, 128))
    small = jnp.pad(jnp.concatenate(rows, axis=0), ((0, 13), (0, 0)))
    r = everything(
        tokens=tokens, cot=cotangent, small=small, cos=cos, sin=sin,
        wq=w_query, wk=w_key, wv=w_value, wo=w_out, wg=w_gate, wu=w_up, wd=w_down,
    )
    out, dx, gq, gk, gv, go, gate, up, down, attn, ffn, gain_q, gain_k = finished(r)
    attn, ffn, gain_q, gain_k = (v.reshape(64) for v in (attn, ffn, gain_q, gain_k))
    return out, dx, attn, gq, gk, gv, gain_q, gain_k, go, ffn, gate, up, down


def solution(mesh):
    return jax.shard_map(
        on_device,
        mesh=mesh,
        in_specs=(
            P("dp", None), P("dp"), P("dp", "head"), P("dp", "head"), P("dp", "head"),
            P(), P(), P("dp", "head"), P("dp"),
            P("dp", "tensor"), P("dp", "tensor"), P("dp", "tensor"), P("dp", None),
        ),
        out_specs=(
            P("dp", None), P("dp", None), P("dp"),
            P("dp", "head"), P("dp", "head"), P("dp", "head"),
            P(), P(), P("dp", "head"), P("dp"),
            P("dp", "tensor"), P("dp", "tensor"), P("dp", "tensor"),
        ),
        check_vma=False,
    )
```

```python
import types

import jax
import jax.numpy as jnp
import numpy as np
from jax import lax
from jax.experimental import pallas as pl
from jax.experimental.pallas import tpu as pltpu
from jax.sharding import PartitionSpec as P

BF = jnp.bfloat16
F32 = jnp.float32
MESH = pl.DeviceIdType.MESH
EPS = 1e-05
THETA = 1000000.0
VMEM_BYTES = 62 << 20
ATT_SLICES = ((0, 384), (384, 256))


def nn(a, b):
    return lax.dot_general(a, b, (((1,), (0,)), ((), ())), preferred_element_type=F32)


def nt(a, b):
    return lax.dot_general(a, b, (((1,), (1,)), ((), ())), preferred_element_type=F32)


def tn(a, b):
    return lax.dot_general(a, b, (((0,), (0,)), ((), ())), preferred_element_type=F32)


class Place:
    def __init__(self):
        dp = lax.axis_index("dp")
        self.c = lax.axis_index("head")
        self.zl = lax.axis_index("tensor")
        self.zh = lax.div(dp, 16)
        self.y = lax.rem(lax.div(dp, 4), 4)
        self.x = lax.rem(dp, 4)
        self.odd = lax.rem(self.y, 2)
        self.z = self.zh * 2 + self.zl

    def at(self, zh=None, y=None, x=None, c=None, zl=None):
        zh = self.zh if zh is None else zh
        y = self.y if y is None else y
        x = self.x if x is None else x
        return (zh * 16 + y * 4 + x, self.c if c is None else c, self.zl if zl is None else zl)

    def step(self, axis, by):
        if axis == "x":
            return self.at(x=lax.rem(self.x + by + 4, 4))
        if axis == "y":
            return self.at(y=lax.rem(self.y + by + 4, 4))
        z = lax.rem(self.z + by + 4, 4)
        return self.at(zh=lax.div(z, 2), zl=lax.rem(z, 2))

    def core(self):
        return self.at(c=1 - self.c)

    def zl_pair(self):
        return self.at(zl=1 - self.zl)

    def y_pair(self):
        return self.at(y=self.y + 1 - 2 * self.odd)

    def zh_pair(self):
        return self.at(zh=1 - self.zh)

    def ring(self, axis):
        return {"x": self.x, "y": self.y, "z": self.z}[axis]


class Copy:
    def __init__(self, copy):
        self.copy = copy
        self.left = True

    def wait_recv(self):
        self.copy.wait_recv()

    def wait_send(self):
        if self.left:
            self.copy.wait_send()
            self.left = False


class Group:
    def __init__(self, sem):
        self.sem = sem

    def wait(self, like):
        pltpu.make_async_copy(like, like, self.sem).wait()


class Net:
    def __init__(self, send_sems, recv_sems):
        self.send_sems = send_sems
        self.recv_sems = recv_sems
        self.slots = [None] * send_sems.shape[0]
        self.sends = 0
        self.groups = 0

    def group(self):
        k = self.groups
        assert k < self.recv_sems.shape[0], k
        self.groups += 1
        return Group(self.recv_sems.at[k])

    def send(self, src, dst, device, group=None):
        slot = self.sends % len(self.slots)
        self.sends += 1
        if self.slots[slot] is not None:
            self.slots[slot].wait_send()
        copy = pltpu.make_async_remote_copy(
            src_ref=src,
            dst_ref=dst,
            send_sem=self.send_sems.at[slot],
            recv_sem=(group or self.group()).sem,
            device_id=device,
            device_id_type=MESH,
        )
        copy.start()
        self.slots[slot] = Copy(copy)
        return self.slots[slot]

    def drain(self):
        for copy in self.slots:
            if copy is not None:
                copy.wait_send()


class Tagged:
    def __init__(self, net):
        self.net = net
        self.copies = []

    def group(self):
        return self.net.group()

    def send(self, src, dst, device, group=None):
        self.copies.append(self.net.send(src, dst, device, group))
        return self.copies[-1]

    def drain(self):
        for copy in self.copies:
            copy.wait_send()


def greet(devices):
    barrier = pltpu.get_barrier_semaphore()
    for device in devices:
        pl.semaphore_signal(barrier, inc=1, device_id=device, device_id_type=MESH)
    pl.semaphore_wait(barrier, len(devices))


def together(*pipelines):
    live = list(pipelines)
    while live:
        for pipe in list(live):
            try:
                next(pipe)
            except StopIteration:
                live.remove(pipe)
        yield


def step(*pipelines):
    for pipe in pipelines:
        next(pipe, None)


def finish(*pipelines):
    for _ in together(*pipelines):
        pass


def local(pairs, sems):
    copies = [pltpu.make_async_copy(s, d, sems.at[i]) for i, (s, d) in enumerate(pairs)]
    for copy in copies:
        copy.start()
    for copy in copies:
        copy.wait()


def add_refs(dst, srcs, rows=32):
    lead, height = dst.shape[:-2], dst.shape[-2]
    rows = min(rows, height)
    per = height // rows
    count = int(np.prod(lead, dtype=np.int64)) * per

    def body(t, carry):
        r = lax.rem(t, per)
        rest = lax.div(t, per)
        index = []
        for size in reversed(lead):
            index.insert(0, lax.rem(rest, size))
            rest = lax.div(rest, size)
        at = tuple(index) + (pl.ds(r * rows, rows), slice(None))
        total = srcs[0][at].astype(F32)
        for src in srcs[1:]:
            total = total + src[at].astype(F32)
        dst[at] = total.astype(dst.dtype)
        return carry

    lax.fori_loop(0, count, body, 0)


def ring_gather(net, place, axis, view, like):
    i = place.ring(axis)
    before, after = lax.rem(i + 3, 4), lax.rem(i + 1, 4)
    up, down = place.step(axis, 1), place.step(axis, -1)
    rest = net.group()
    u0 = net.send(view(i, 0), view(i, 0), up)
    d1 = net.send(view(i, 1), view(i, 1), down)
    net.send(view(i, 1), view(i, 1), up, rest)
    net.send(view(i, 0), view(i, 0), down, rest)
    yield
    u0.wait_recv()
    net.send(view(before, 0), view(before, 0), up, rest)
    d1.wait_recv()
    net.send(view(after, 1), view(after, 1), down, rest)
    yield
    rest.wait(like)


def ring_reduce(net, place, axis, view, far, near, out):
    i = place.ring(axis)
    before, after, across = lax.rem(i + 3, 4), lax.rem(i + 1, 4), lax.rem(i + 2, 4)
    up, down = place.step(axis, 1), place.step(axis, -1)
    fars, nears = net.group(), net.group()
    net.send(view(across, 0), far.at[0], up, fars)
    net.send(view(across, 1), far.at[1], down, fars)
    yield
    net.send(view(after, 1), near.at[1], up, nears)
    net.send(view(before, 0), near.at[2], down, nears)
    yield
    fars.wait(far)
    add_refs(far.at[0], [far.at[0], view(after, 0)])
    net.send(far.at[0], near.at[0], up, nears)
    add_refs(far.at[1], [far.at[1], view(before, 1)])
    net.send(far.at[1], near.at[3], down, nears)
    yield
    nears.wait(near)
    add_refs(out(0), [view(i, 0), near.at[0], near.at[2]])
    add_refs(out(1), [view(i, 1), near.at[1], near.at[3]])


def cross_gather(net, place, one, two, view, likes, late=None, also=None, only=None):
    ring = [lax.rem(place.ring(one) + k, 4) for k in range(4)]
    other = [lax.rem(place.ring(two) + k, 4) for k in range(4)]
    up = {one: place.step(one, 1), two: place.step(two, 1)}
    down = {one: place.step(one, -1), two: place.step(two, -1)}
    corners = []
    last = [net.group(), net.group()]
    finals = [[], []]

    def spread(block, axis, group):
        net.send(block, block, up[axis], group)
        net.send(block, block, down[axis], group)

    def arrived(block):
        if also is not None:
            also(block)
        return block

    def along(axis, part, k, half=None):
        if axis == one:
            return view(part, ring[k], other[0], half)
        return view(part, ring[0], other[k], half)

    def turn(axis, part, k):
        across = two if axis == one else one
        half = 1 if axis == one else 0
        if only is not None and half != only:
            return
        group = net.group()
        spread(along(axis, part, k, half), across, group)
        corners.append((axis, part, k, half, across, group))

    def own(part):
        group = net.group()
        block = view(part, ring[0], other[0], None)
        for axis in (one, two):
            spread(block, axis, group)
        return group

    crosses = [own(0)]
    if late is None:
        crosses.append(own(1))
    yield
    if late is not None:
        late.wait_recv()
        crosses.append(own(1))
        yield
    far = net.group()
    for part in (0, 1):
        crosses[part].wait(likes(None, 4))
        order = (3, 1) if part == 0 else (1, 3)
        for n, k in enumerate(order):
            for axis in (one, two):
                block = arrived(along(axis, part, k))
                if n == 0:
                    net.send(block, block, (up, down)[part][axis], far)
                turn(axis, part, k)
        yield
    far.wait(likes(None, 4))
    for part in (0, 1):
        for axis in (one, two):
            arrived(along(axis, part, 2))
            turn(axis, part, 2)
    yield
    for n, (axis, part, k, half, across, group) in enumerate(corners):
        group.wait(likes(half, 2))
        for which, by in ((0, 3), (1, 1)):
            if axis == one:
                block = view(part, ring[k], other[by], half)
                final = view(part, ring[k], other[2], half)
            else:
                block = view(part, ring[by], other[k], half)
                final = view(part, ring[2], other[k], half)
            arrived(block)
            if which == part:
                net.send(block, block, (up, down)[part][across], last[half])
                finals[half].append(final)
        if n % 4 == 3:
            yield
    for half in (0, 1):
        if finals[half]:
            last[half].wait(likes(half, len(finals[half])))
            for final in finals[half]:
                arrived(final)


def order_reduce(net, place, one, two, view, s, out, other_out=None):
    ring = [lax.rem(place.ring(one) + k, 4) for k in range(4)]
    other = [lax.rem(place.ring(two) + k, 4) for k in range(4)]
    up, down = place.step(one, 1), place.step(one, -1)
    order = (2, 1, 3, 0)
    fars = {k: net.group() for k in order}
    nears = {k: net.group() for k in order}
    others = net.group()
    for k in order:
        net.send(view(0, ring[2], other[k]), s.far.at[k, 0], up, fars[k])
        net.send(view(1, ring[2], other[k]), s.far.at[k, 1], down, fars[k])
    for k in order:
        net.send(view(1, ring[1], other[k]), s.near.at[k, 1], up, nears[k])
        net.send(view(0, ring[3], other[k]), s.near.at[k, 2], down, nears[k])
    yield
    for k in order:
        fars[k].wait(s.far.at[k])
        add_refs(s.far.at[k, 0], [s.far.at[k, 0], view(0, ring[1], other[k])])
        net.send(s.far.at[k, 0], s.near.at[k, 0], up, nears[k])
        add_refs(s.far.at[k, 1], [s.far.at[k, 1], view(1, ring[3], other[k])])
        net.send(s.far.at[k, 1], s.near.at[k, 3], down, nears[k])
        if k != 1:
            yield
    for k in order:
        nears[k].wait(s.near.at[k])
        for p in (0, 1):
            add_refs(
                s.mid.at[k, p],
                [view(p, ring[0], other[k]), s.near.at[k, p], s.near.at[k, 2 + p]],
            )
        if k:
            net.send(s.mid.at[k], s.last.at[k - 1], place.step(two, k), others)
        if k != 1:
            yield
    others.wait(s.last)
    for p in (0, 1):
        if other_out is None:
            add_refs(out(p), [s.mid.at[0, p]] + [s.last.at[k, p] for k in range(3)])
        else:
            add_refs(out(p), [s.mid.at[0, p], s.last.at[1, p]])
            add_refs(other_out(p), [s.last.at[0, p], s.last.at[2, p]])


def order_buffers(rows, columns):
    return dict(
        far=pltpu.VMEM((4, 2, rows, columns), BF),
        near=pltpu.VMEM((4, 4, rows, columns), BF),
        mid=pltpu.VMEM((4, 2, rows, columns), BF),
        last=pltpu.VMEM((3, 2, rows, columns), BF),
    )


def torus_gather(net, place, buf, only=None):
    c = place.c
    other = place.core()
    swaps = net.group()

    def also(block):
        net.send(block, block, other, swaps)

    def rows(half):
        return pl.ds(0, 32) if half is None or only is not None else pl.ds(half * 16, 16)

    def view(part, i, j, half):
        return buf.at[i, j, c, rows(half), pl.ds(part * 1024, 1024)]

    def likes(half, n):
        return buf.at[pl.ds(0, 2), pl.ds(0, n // 2), 0, rows(half), pl.ds(0, 1024)]

    also(buf.at[place.z, place.x, c])
    yield from cross_gather(net, place, "z", "x", view, likes, also=also, only=only)
    yield
    swaps.wait(buf.at[:, :, 1 - c])


def torus_buffers():
    return dict(
        both=pltpu.VMEM((4, 4, 32, 2048), BF),
        halves=[order_buffers(16, 1024), order_buffers(16, 1024)],
        total=pltpu.VMEM((32, 2048), F32),
    )


def core_sum(place, src, swap, s, k):
    swap.wait_recv()
    add_refs(s.both.at[k], [s.both.at[k], src.at[k, :, place.c]])


def torus_reduce(net, place, s, orders):
    def half(k):
        def at(part):
            return pl.ds(k * 16, 16), pl.ds(part * 1024, 1024)

        def view(p, i, j):
            zi, xi = (i, j) if orders[k] == "z" else (j, i)
            return s.both.at[(zi, xi) + at(p)]

        second = "x" if orders[k] == "z" else "z"
        return order_reduce(
            net, place, orders[k], second, view, s.halves[k], lambda p: s.total.at[at(p)]
        )

    yield from together(half(0), half(1))


def quad_gather(net, place, buf):
    c, zl = place.c, place.zl
    own = buf.at[pl.ds(c * 64 + zl * 32, 32)]
    one = net.send(own, own, place.zl_pair())
    yield
    one.wait_recv()
    half = buf.at[pl.ds(c * 64, 64)]
    two = net.send(half, half, place.core())
    yield
    two.wait_recv()


def oct_reduce(net, place, src, b):
    c, zl, q = place.c, place.zl, place.odd
    one = net.send(src.at[:, pl.ds((1 - c) * 64, 64)], b.core, place.core())
    yield
    one.wait_recv()
    b.for_y[...] = (
        src[1 - q, pl.ds(c * 64, 64), :].astype(F32) + b.core[1 - q].astype(F32)
    ).astype(BF)
    far, near = pl.ds((1 - zl) * 32, 32), pl.ds(zl * 32, 32)
    two = [net.send(b.for_y.at[r], b.y.at[r], place.y_pair()) for r in (far, near)]
    yield
    two[0].wait_recv()
    theirs = src[q, pl.ds(c * 64 + (1 - zl) * 32, 32), :].astype(F32)
    theirs = theirs + b.core[q, far, :].astype(F32) + b.y[far, :].astype(F32)
    b.for_zl[...] = theirs.astype(BF)
    three = net.send(b.for_zl, b.zl, place.zl_pair())
    yield
    two[1].wait_recv()
    three.wait_recv()


def oct_total(place, src, b):
    c, zl, q = place.c, place.zl, place.odd
    near = pl.ds(zl * 32, 32)
    total = src[q, pl.ds(c * 64 + zl * 32, 32), :].astype(F32) + b.core[q, near, :].astype(F32)
    return total + b.y[near, :].astype(F32) + b.zl[...].astype(F32)


def oct_buffers():
    return dict(
        core=pltpu.VMEM((2, 64, 2048), BF),
        for_y=pltpu.VMEM((64, 2048), BF),
        y=pltpu.VMEM((64, 2048), BF),
        for_zl=pltpu.VMEM((32, 2048), BF),
        zl=pltpu.VMEM((32, 2048), BF),
    )


def quad_gather(net, place, buf):
    c, zl = place.c, place.zl
    own = buf.at[pl.ds(c * 64 + zl * 32, 32)]
    one = net.send(own, own, place.zl_pair())
    yield
    one.wait_recv()
    half = buf.at[pl.ds(c * 64, 64)]
    two = net.send(half, half, place.core())
    yield
    two.wait_recv()


def oct_gather(net, place, buf):
    c, zl, q = place.c, place.zl, place.odd
    own = buf.at[q, pl.ds(c * 64 + zl * 32, 32)]
    from_zl = net.send(own, own, place.zl_pair())
    from_y = [net.send(own, own, place.y_pair())]
    yield
    from_zl.wait_recv()
    other = buf.at[q, pl.ds(c * 64 + (1 - zl) * 32, 32)]
    from_y.append(net.send(other, other, place.y_pair()))
    half = buf.at[q, pl.ds(c * 64, 64)]
    from_core = [net.send(half, half, place.core())]
    yield
    for copy in from_y:
        copy.wait_recv()
    half = buf.at[1 - q, pl.ds(c * 64, 64)]
    from_core.append(net.send(half, half, place.core()))
    yield
    for copy in from_core:
        copy.wait_recv()


def sem_scratch(n):
    return [pltpu.SemaphoreType.DMA((n,)), pltpu.SemaphoreType.DMA((n,))]


ANY = pl.BlockSpec(memory_space=pl.ANY)
VM = pl.BlockSpec(memory_space=pltpu.VMEM)


def lanes(shape):
    return lax.broadcasted_iota(jnp.int32, shape, len(shape) - 1)


def partner(v):
    n = v.shape[-1]
    low = lax.rem(lanes(v.shape), 64) < 32
    return jnp.where(low, pltpu.roll(v, n - 32, 1), pltpu.roll(v, 32, 1))


def head_mean(v):
    n = v.shape[-1]
    r = lax.broadcasted_iota(jnp.int32, (n, n), 0)
    same = lax.div(r, 64) == lax.div(lanes((n, n)), 64)
    return lax.dot_general(
        v, jnp.where(same, 1.0 / 64.0, 0.0), (((1,), (0,)), ((), ())),
        precision=lax.Precision.HIGHEST, preferred_element_type=F32,
    )


def half_of(v, which):
    upper = lanes(v.shape) >= 64
    keep = upper if which else jnp.logical_not(upper)
    return jnp.where(keep, v, jnp.zeros_like(v))


def swap_halves(v):
    return pltpu.roll(v.astype(F32), 64, 1).astype(v.dtype)


def rows_rms(v):
    return lax.rsqrt(jnp.mean(v * v, axis=-1, keepdims=True) + EPS)


N_SENDS = 48
N_GROUPS = 147
N_LOCAL = 17


def input_plan():
    return dict(
        tokens=ANY, cot=ANY, small=ANY, cos=ANY, sin=ANY,
        wq=ANY, wk=ANY, wv=ANY, wo=ANY, wg=ANY, wu=ANY, wd=ANY,
    )


def output_plan():
    return dict(
        out=jax.ShapeDtypeStruct((128, 2048), BF),
        dx=jax.ShapeDtypeStruct((128, 2048), BF),
        att_grads=jax.ShapeDtypeStruct((2, 2, 64, 640), BF),
        ffn_grads=jax.ShapeDtypeStruct((3, 8, 2, 64, 256), BF),
        gain_sums=jax.ShapeDtypeStruct((8, 640), F32),
    )


def scratch_plan():
    return dict(
        tok=pltpu.VMEM((2, 128, 2048), BF),
        kv_in=pltpu.VMEM((2, 64, 128), BF),
        shard=pltpu.VMEM((2, 2, 64, 640), BF),
        small_in=pltpu.VMEM((16, 128), BF),
        cos_in=pltpu.VMEM((128, 128), F32),
        sin_in=pltpu.VMEM((128, 128), F32),
        att=pltpu.VMEM((2, 4, 4, 64, 640), BF),
        gains=pltpu.VMEM((2, 4, 4, 16, 128), BF),
        ffn=pltpu.VMEM((3, 2, 4, 4, 64, 256), BF),
        cots=pltpu.VMEM((4, 4, 2, 32, 2048), BF),
        xn2=pltpu.VMEM((4, 4, 2, 32, 2048), BF),
        xn=pltpu.VMEM((256, 2048), BF),
        z=pltpu.VMEM((256, 384), F32),
        qk=pltpu.VMEM((256, 384), BF),
        p=pltpu.VMEM((8, 128, 128), F32),
        o=pltpu.VMEM((256, 256), BF),
        branch=pltpu.VMEM((2, 128, 2048), BF),
        branch_sum=oct_buffers(),
        dxn_sum=oct_buffers(),
        hidden=pltpu.VMEM((32, 2048), F32),
        da=pltpu.VMEM((4, 256, 256), F32),
        ab=pltpu.VMEM((4, 256, 256), BF),
        dg=pltpu.VMEM((4, 256, 256), BF),
        du=pltpu.VMEM((4, 256, 256), BF),
        dxn2_part=pltpu.VMEM((4, 4, 2, 32, 2048), BF),
        ffn_part=pltpu.VMEM((3, 2, 4, 4, 64, 256), BF),
        ffn_far=pltpu.VMEM((4, 2, 3, 64, 256), BF),
        ffn_near=pltpu.VMEM((4, 4, 3, 64, 256), BF),
        ffn_mid=pltpu.VMEM((4, 2, 3, 64, 256), BF),
        dh=pltpu.VMEM((32, 2048), F32),
        dhb=pltpu.VMEM((2, 128, 2048), BF),
        ffn_gain_grad=pltpu.VMEM((1, 2048), F32),
        d_heads=pltpu.VMEM((256, 384), F32),
        att_part=pltpu.VMEM((2, 4, 4, 64, 640), BF),
        dxn_part=pltpu.VMEM((2, 128, 2048), BF),
        both_z=pltpu.VMEM((2, 2, 64, 640), BF),
        from_z=pltpu.VMEM((2, 2, 2, 64, 640), BF),
        gain_quad=pltpu.VMEM((4, 8, 640), F32),
        gain_y=pltpu.VMEM((4, 8, 640), F32),
        gain_xz=pltpu.VMEM((8, 8, 640), F32),
        dxn2_sum=torus_buffers(),
        out_sum=torus_buffers(),
        slices=[order_buffers(64, n) for _, n in ATT_SLICES],
        send_sems=pltpu.SemaphoreType.DMA((N_SENDS,)),
        recv_sems=pltpu.SemaphoreType.DMA((N_GROUPS,)),
        sems=pltpu.SemaphoreType.DMA((N_LOCAL,)),
    )


def named(plan):
    if isinstance(plan, dict):
        return types.SimpleNamespace(**{k: named(v) for k, v in plan.items()})
    if isinstance(plan, list):
        return [named(v) for v in plan]
    return plan


def kernel(*refs):
    s = types.SimpleNamespace()
    for plan in (input_plan(), output_plan(), scratch_plan()):
        leaves, tree = jax.tree.flatten(plan)
        part = jax.tree.unflatten(tree, refs[: len(leaves)])
        refs = refs[len(leaves):]
        vars(s).update(vars(named(part)))
    send_sems, recv_sems, sems = s.send_sems, s.recv_sems, s.sems
    me = Place()
    zh, y, x, c, zl, z, odd = me.zh, me.y, me.x, me.c, me.zl, me.z, me.odd
    net = Net(send_sems, recv_sems)
    att, ffn = s.att, s.ffn
    rows = pl.ds(c * 64 + zl * 32, 32)


    def piece(k):
        return pl.ds(pl.multiple_of(k * 512 + c * 256, 256), 256)

    def load(pairs):
        started = []
        for src, dst in pairs:
            started.append(pltpu.make_async_copy(src, dst, sems.at[len(loads)]))
            loads.append(started[-1])
            started[-1].start()
        return started

    loads = []
    narrow = pl.ds(pl.multiple_of(zl * 128, 128), 128)
    mine = zh * 4 + x
    att_copies = load([(w.at[:, narrow], s.kv_in.at[k]) for k, w in enumerate((s.wk, s.wv))])
    for parity in range(2):
        wide = pl.ds(pl.multiple_of(zl * 512 + parity * 256, 256), 256)
        block = s.shard.at[0, parity]
        att_copies += load(
            [
                (s.wq.at[:, wide], block.at[:, pl.ds(0, 256)]),
                (s.wo.at[:, wide], block.at[:, pl.ds(384, 256)]),
            ]
        )
    (small_copy,) = load([(s.small, s.small_in)])
    (cots_copy,) = load([(s.cot.at[rows], s.cots.at[z, x, c])])
    ffn_copies = load(
        [(w.at[:, piece(mine)], ffn.at[m, zh, y, x]) for m, w in enumerate((s.wg, s.wu, s.wd))]
    )
    (tok_copy,) = load([(s.tokens, s.tok.at[odd])])
    other_copies = load([(s.cos, s.cos_in), (s.sin, s.sin_in)])
    greet(
        [me.step("x", 1), me.step("x", 2), me.step("x", -1)]
        + [me.step("y", 1), me.step("y", 2), me.step("y", -1)]
        + [me.step("z", 1), me.step("z", 2), me.step("z", -1)]
        + [me.core(), me.at(c=1 - c, zl=1 - zl)]
        + [me.at(zh=1 - zh, x=lax.rem(x + k, 4)) for k in (1, 2, 3)]
    )

    def gather_attention():
        shard = s.shard

        def plane(p):
            return 1 - zh if p else zh

        def blocks(n):
            return att.at[0, 0, pl.ds(0, n)]

        rings = {}
        last = net.group()

        def set_off(p, k):
            block = att.at[plane(p), lax.rem(y + k, 4), x]
            rings[p, k] = net.group()
            net.send(block, block, me.step("x", 1), rings[p, k])
            net.send(block, block, me.step("x", -1), rings[p, k])

        def along_y(p):
            group = net.group()
            for k in (1, 3, 2):
                parity = odd if k == 2 else 1 - odd
                dst = att.at[plane(p), y, x]
                net.send(shard.at[p, parity], dst, me.step("y", k), group)
            s.att[plane(p), y, x] = shard[p, odd]
            set_off(p, 0)
            return group

        swap = net.send(shard.at[0], shard.at[1], me.zh_pair())
        groups = [along_y(0)]
        yield
        swap.wait_recv()
        groups.append(along_y(1))
        yield
        for p in (0, 1):
            groups[p].wait(blocks(3))
            for k in (1, 3, 2):
                set_off(p, k)
            yield
        for k in (0, 1, 3, 2):
            for p in (0, 1):
                rings[p, k].wait(blocks(2))
                by = 1 if p else 3
                block = att.at[plane(p), lax.rem(y + k, 4), lax.rem(x + by, 4)]
                net.send(block, block, me.step("x", -1 if p else 1), last)
            yield
        last.wait(att.at[:, 0])

    def gather_tokens():
        half = s.tok.at[odd, pl.ds(c * 64, 64)]
        copy = net.send(half, half, me.y_pair())
        yield
        copy.wait_recv()
        half = s.tok.at[1 - odd, pl.ds(c * 64, 64)]
        copy = net.send(half, half, me.core())
        yield
        copy.wait_recv()

    def gather_ffn():
        arrivals = [net.group(), net.group()]
        for dz in (0, 1):
            for dx in range(4):
                if dz == 0 and dx == 0:
                    continue
                tx = lax.rem(x + dx, 4)
                tz = 1 - zh if dz else zh
                for m, w in enumerate((s.wg, s.wu, s.wd)):
                    net.send(
                        w.at[:, piece(tz * 4 + tx)],
                        ffn.at[m, zh, y, x],
                        me.at(zh=tz, x=tx),
                        arrivals[dz],
                    )
        yield
        arrivals[0].wait(s.ffn_part.at[:, 0, 0, pl.ds(0, 3)])
        arrivals[1].wait(s.ffn_part.at[:, 0, 0])
        for copy in ffn_copies:
            copy.wait()
        yield from ring_gather(
            net, me, "y", lambda i, p: ffn.at[:, p, i], s.ffn_part.at[:, 0]
        )

    def gather_gains():
        own_gain = s.gains.at[zh, y, x]
        near, far = net.group(), net.group()
        for k in range(4):
            device = lax.rem(x + k, 4)
            if k:
                net.send(own_gain, own_gain, me.at(x=device), near)
            net.send(own_gain, own_gain, me.at(zh=1 - zh, x=device), far)
        yield
        near.wait(s.gains.at[0, 0, pl.ds(0, 3)])
        far.wait(s.gains.at[0, 0])
        row = s.gains.at[:, y]
        group = net.group()
        for k in (1, -1, 2):
            net.send(row, row, me.step("y", k), group)
        yield
        group.wait(s.gains.at[:, pl.ds(0, 3)])

    def gain_row(k):
        blocks = []
        for pair in range(16):
            a, b = 2 * pair, 2 * pair + 1
            total = None
            for d in (a, b):
                block = s.gains[d // 16, d // 4 % 4, d % 4].astype(F32)
                total = block if total is None else total + block
            blocks.append(total[k:k + 1, :])
        return jnp.concatenate(blocks, axis=1)

    for copy in att_copies:
        copy.wait()
    key, value = s.kv_in[0], s.kv_in[1]
    low_half = lanes((64, 128)) < 64
    s.shard[0, 0, :, 256:384] = jnp.where(low_half, key, swap_halves(value))
    s.shard[0, 1, :, 256:384] = jnp.where(low_half, swap_halves(key), value)
    attention = gather_attention()
    gains = gather_gains()
    weights = gather_ffn()
    cots = torus_gather(net, me, s.cots, only=0)
    pair_tokens = gather_tokens()
    step(attention)
    small_copy.wait()
    small = s.small_in[...].astype(F32)
    s.gains[zh, y, x] = jnp.where(lax.rem(x, 2) == 1, pltpu.roll(small, 64, 1), small).astype(BF)
    step(gains, weights, attention, attention, gains, attention)
    tok_copy.wait()
    step(pair_tokens, attention)
    finish(gains)
    for copy in other_copies:
        copy.wait()
    step(pair_tokens, attention, weights)
    cots_copy.wait()
    step(attention, cots)
    finish(pair_tokens)
    t = s.tok[...].reshape(256, 2048).astype(F32)
    s.xn[...] = (t * rows_rms(t) * gain_row(0)).astype(BF)
    step(attention, cots)
    finish(attention)


    step(cots)
    raw = nn(s.xn[...], att[:, :, :, :, 0:384].reshape(2048, 384))
    s.z[...] = raw
    step(weights, cots)
    both_gains = small[2:3, :]
    turned = pltpu.roll(both_gains, 64, 1)
    low = lanes((1, 128)) < 64
    gain_q = jnp.where(low, both_gains, turned)
    head_gain = jnp.concatenate([gain_q, gain_q, turned], axis=1)
    cos, sin = (
        jnp.concatenate([jnp.concatenate([ref[...]] * 3, axis=1)] * 2, axis=0)
        for ref in (s.cos_in, s.sin_in)
    )
    is_value = lanes((256, 384)) >= 320
    n = raw * lax.rsqrt(head_mean(raw * raw) + EPS) * head_gain
    s.qk[...] = jnp.where(is_value, raw, n * cos + partner(n) * sin).astype(BF)
    step(cots)
    causal = lax.broadcasted_iota(jnp.int32, (128, 128), 0) >= lanes((128, 128))
    for q in range(2):
        at = slice(q * 128, (q + 1) * 128)
        kv = s.qk[at, 256:384]
        sides = (kv, swap_halves(kv))
        for block in range(2):
            cols = slice(block * 128, (block + 1) * 128)
            out = None
            for side in range(2):
                query = half_of(s.qk[at, cols], side)
                score = jnp.where(causal, nt(query, sides[side]) * 0.125, -1e30)
                e = jnp.exp(score - jnp.max(score, axis=-1, keepdims=True))
                p = e / jnp.sum(e, axis=-1, keepdims=True)
                s.p[q * 4 + 2 * block + side] = p
                part = nn(p.astype(BF), half_of(sides[1 - side], side))
                out = part if out is None else out + part
            s.o[at, cols] = out.astype(BF)
    branch = nt(s.o[...], att[:, :, :, :, 384:640].reshape(2048, 256)).astype(BF)
    s.branch[...] = branch.reshape(2, 128, 2048)
    summed = oct_reduce(net, me, s.branch, s.branch_sum)
    step(summed, cots)
    finish(summed)
    hidden = s.tok[odd, rows, :].astype(F32)
    hidden = hidden + oct_total(me, s.branch, s.branch_sum)
    s.hidden[...] = hidden
    s.xn2[z, x, c] = (hidden * rows_rms(hidden) * gain_row(1)).astype(BF)
    normed_net = Tagged(net)
    normed = torus_gather(normed_net, me, s.xn2)
    step(normed, normed, normed)
    finish(cots, weights)
    step(normed, normed)


    def weight(m):
        return ffn[m].reshape(2048, 256)

    for k in range(4):
        s.da[k] = nn(s.cots[k].reshape(256, 2048), weight(2))
        step(normed)
    finish(normed)
    swaps = []
    for k in range(4):
        xk = s.xn2[k].reshape(256, 2048)
        g, u, da = nn(xk, weight(0)), nn(xk, weight(1)), s.da[k]
        sigma = jax.nn.sigmoid(g)
        swish = g * sigma
        s.ab[k] = (swish * u).astype(BF)
        dg = (da * u * sigma * (1.0 + g * (1.0 - sigma))).astype(BF)
        du = (da * swish).astype(BF)
        s.dg[k] = dg
        s.du[k] = du
        part = (nt(dg, weight(0)) + nt(du, weight(1))).astype(BF)
        s.dxn2_part[k] = part.reshape(4, 2, 32, 2048)
        swaps.append(
            net.send(s.dxn2_part.at[k, :, 1 - c], s.dxn2_sum.both.at[k], me.core())
        )
        if k:
            core_sum(me, s.dxn2_part, swaps[k - 1], s.dxn2_sum, k - 1)


    dxn2 = torus_reduce(net, me, s.dxn2_sum, "zx")

    def weight_grads(k):
        yk = lax.rem(y + k, 4)

        def one(p, carry):
            cols = pl.ds(pl.multiple_of((p * 4 + yk) * 256, 256), 256)
            xd = s.xn2[:, :, :, :, cols].reshape(1024, 256)
            dyd = s.cots[:, :, :, :, cols].reshape(1024, 256)
            for m, left, right in ((0, xd, s.dg), (1, xd, s.du), (2, dyd, s.ab)):
                grad = tn(left, right[...].reshape(1024, 256))
                s.ffn_part[m, p, yk] = grad.astype(BF).reshape(4, 64, 256)
            return carry

        lax.fori_loop(0, 2, one, 0)

    def reduce_ffn_grads():
        part, grads = s.ffn_part, s.ffn_grads
        arrivals = [net.group(), net.group()]
        dst = grads.at[:, mine, c]
        keep = pltpu.make_async_copy(s.ffn_mid.at[0, zh], dst, sems.at[N_LOCAL - 1])

        def block(k):
            xk = lax.rem(x + k, 4)
            far, near, mid = (ref.at[k] for ref in (s.ffn_far, s.ffn_near, s.ffn_mid))
            yield from ring_reduce(
                net, me, "y", lambda i, p: part.at[:, p, i, xk], far, near, lambda p: mid.at[p]
            )
            if k:
                net.send(mid.at[zh], dst, me.at(x=xk), arrivals[0])
            else:
                keep.start()
            net.send(mid.at[1 - zh], dst, me.at(zh=1 - zh, x=xk), arrivals[1])

        yield from together(*[block(k) for k in (2, 1, 3, 0)])
        keep.wait()
        arrivals[0].wait(s.ffn_part.at[:, 0, 0, pl.ds(0, 3)])
        arrivals[1].wait(s.ffn_part.at[:, 0, 0])
        swap = net.send(grads.at[:, :, c], grads.at[:, :, c], me.core())
        yield
        swap.wait_recv()

    ffn_grads = reduce_ffn_grads()
    weight_grads(2)
    step(ffn_grads)
    core_sum(me, s.dxn2_part, swaps[3], s.dxn2_sum, 3)
    step(dxn2)
    weight_grads(1)
    weight_grads(3)
    step(ffn_grads, dxn2, dxn2)
    weight_grads(0)
    step(dxn2)
    swaps = []
    normed_net.drain()
    for k in range(4):
        part = nt(s.ab[k], weight(2)).astype(BF)
        s.xn2[k] = part.reshape(4, 2, 32, 2048)
        swaps.append(net.send(s.xn2.at[k, :, 1 - c], s.out_sum.both.at[k], me.core()))
        if k % 2 == 1:
            step(dxn2)
    finish(dxn2)
    hidden = s.hidden[...]
    r = rows_rms(hidden)
    hat = hidden * r
    d = s.dxn2_sum.total[...]
    s.ffn_gain_grad[...] = jnp.sum(d * hat, axis=0, keepdims=True)
    scaled = d * gain_row(1)
    dh = s.cots[z, x, c].astype(F32)
    dh = dh + r * (scaled - hat * jnp.mean(scaled * hat, axis=-1, keepdims=True))
    s.dh[...] = dh
    s.dhb[odd, rows, :] = dh.astype(BF)
    spread = oct_gather(net, me, s.dhb)
    step(spread)

    def finish_output():
        for k in range(4):
            core_sum(me, s.xn2, swaps[k], s.out_sum, k)
        yield from torus_reduce(net, me, s.out_sum, "zz")
        s.out[rows, :] = (s.hidden[...] + s.out_sum.total[...]).astype(BF)
        yield from quad_gather(net, me, s.out)

    output = finish_output()
    step(spread, output, spread)
    finish(spread)
    step(ffn_grads)


    def reduce_att_grads(k):
        start, width = ATT_SLICES[k]
        cols = pl.ds(start, width)
        both_z = s.both_z
        yield from order_reduce(
            net, me, "x", "y", lambda p, i, j: s.att_part.at[p, j, i, :, cols], s.slices[k],
            lambda p: both_z.at[p, odd, :, cols], lambda p: both_z.at[p, 1 - odd, :, cols],
        )
        arrivals = net.group()
        mine_z = both_z.at[zh, :, :, cols]
        theirs = both_z.at[1 - zh, :, :, cols]
        dst = s.from_z.at[zl, 1, :, :, cols]
        net.send(theirs, dst, me.at(zh=1 - zh), arrivals)
        net.send(theirs, dst, me.at(zh=1 - zh, zl=1 - zl), arrivals)
        net.send(mine_z, s.from_z.at[zl, 0, :, :, cols], me.at(zl=1 - zl), arrivals)
        yield
        arrivals.wait(s.slices[k].last)
        add_refs(s.att_grads.at[zl, :, :, cols], [mine_z, s.from_z.at[zl, 1, :, :, cols]])
        add_refs(
            s.att_grads.at[1 - zl, :, :, cols],
            [s.from_z.at[1 - zl, 0, :, :, cols], s.from_z.at[1 - zl, 1, :, :, cols]],
        )

    dhb = s.dhb[...].reshape(256, 2048)
    grad = tn(dhb, s.o[...]).astype(BF)
    s.att_part[:, :, :, :, 384:640] = grad.reshape(2, 4, 4, 64, 256)
    slices = [reduce_att_grads(k) for k in range(2)]
    step(slices[1])
    do = nn(dhb, att[:, :, :, :, 384:640].reshape(2048, 256)).astype(BF)
    step(output)
    for q in range(2):
        at = slice(q * 128, (q + 1) * 128)
        kv = s.qk[at, 256:384]
        sides = (kv, swap_halves(kv))
        dk = [jnp.zeros((128, 128), F32)] * 2
        dv = [jnp.zeros((128, 128), F32)] * 2
        for block in range(2):
            cols = slice(block * 128, (block + 1) * 128)
            dq = None
            for side in range(2):
                p = s.p[q * 4 + 2 * block + side]
                dob = half_of(do[at, cols], side)
                query = half_of(s.qk[at, cols], side)
                dp = nt(dob, sides[1 - side])
                dv[side] = dv[side] + tn(p.astype(BF), dob)
                ds = (p * (dp - jnp.sum(p * dp, axis=-1, keepdims=True))).astype(BF)
                part = nn(ds, half_of(sides[side], side))
                dq = part if dq is None else dq + part
                dk[side] = dk[side] + tn(ds, query)
            s.d_heads[at, cols] = dq * 0.125
        dkey = (dk[0] + pltpu.roll(dk[1], 64, 1)) * 0.125
        s.d_heads[at, 256:384] = dkey + dv[1] + pltpu.roll(dv[0], 64, 1)
    step(output, slices[1])
    dout = s.d_heads[...]
    dn = dout * cos - partner(dout) * sin
    z_raw = s.z[...]
    r = lax.rsqrt(head_mean(z_raw * z_raw) + EPS)
    zhat = z_raw * r
    dgain = jnp.sum(dn * zhat, axis=0, keepdims=True)
    q_pairs = dgain[:, 0:128] + dgain[:, 128:256]
    q_pairs = q_pairs + pltpu.roll(q_pairs, 64, 1)
    k_pairs = pltpu.roll(dgain[:, 256:384], 64, 1)
    dz = dn * head_gain
    dz = r * (dz - zhat * head_mean(dz * zhat))
    low_grads = jnp.where(is_value, dout, dz).astype(BF)
    step(slices[1], ffn_grads)
    grad = tn(s.xn[...], low_grads).astype(BF)
    s.att_part[:, :, :, :, 0:384] = grad.reshape(2, 4, 4, 64, 384)
    step(slices[0], slices[1])
    gain_grad = jnp.zeros((1, 2048), F32)
    for q in range(2):
        at = slice(q * 128, (q + 1) * 128)
        back = nt(low_grads[at], att[:, :, :, :, 0:384].reshape(2048, 384))
        s.dxn_part[q] = back.astype(BF)
        t = s.tok[q].astype(F32)
        gain_grad = gain_grad + jnp.sum(back * (t * rows_rms(t)), axis=0, keepdims=True)
    summed = oct_reduce(net, me, s.dxn_part, s.dxn_sum)
    step(summed)

    def gain_grads():
        sums = s.gain_sums
        for k in range(8):
            part = slice(k * 256, (k + 1) * 256)
            sums[k:k + 1, 0:256] = gain_grad[:, part]
            sums[k:k + 1, 256:512] = s.ffn_gain_grad[:, part]
        row = lax.broadcasted_iota(jnp.int32, (8, 128), 0)
        head_grad = jnp.where(lanes((8, 128)) < 64, q_pairs, k_pairs)
        sums[:, 512:640] = jnp.where(row == 0, head_grad, 0.0)

        def total(buf, own, devices):
            group = net.group()
            for device in devices:
                net.send(buf.at[own], buf.at[own], device, group)
            yield
            group.wait(buf.at[pl.ds(0, len(devices))])
            sums[...] = sum(buf[k] for k in range(1, len(devices) + 1)) + buf[0]

        s.gain_quad[c * 2 + zl] = sums[...]
        yield from total(
            s.gain_quad, c * 2 + zl, [me.core(), me.zl_pair(), me.at(c=1 - c, zl=1 - zl)]
        )
        s.gain_y[y] = sums[...]
        yield from total(s.gain_y, y, [me.step("y", k) for k in (1, 2, 3)])
        s.gain_xz[mine] = sums[...]
        yield from total(
            s.gain_xz,
            mine,
            [me.step("x", k) for k in (1, 2, 3)]
            + [me.at(zh=1 - zh, x=lax.rem(x + k, 4)) for k in range(4)],
        )

    gains = gain_grads()
    step(gains, output, slices[1])


    def input_grad():
        yield from summed
        d = oct_total(me, s.dxn_part, s.dxn_sum)
        t = s.tok[odd, rows, :].astype(F32)
        r = rows_rms(t)
        hat = t * r
        scaled = d * gain_row(0)
        total = s.dh[...]
        total = total + r * (scaled - hat * jnp.mean(scaled * hat, axis=-1, keepdims=True))
        s.dx[rows, :] = total.astype(BF)
        yield from quad_gather(net, me, s.dx)

    rest = input_grad()
    finish(rest, gains, slices[1], slices[0], output, ffn_grads)
    net.drain()


def everything(**args):
    in_specs, in_tree = jax.tree.flatten(input_plan())
    out_shapes, out_tree = jax.tree.flatten(output_plan())
    results = pl.pallas_call(
        kernel,
        out_shape=tuple(out_shapes),
        in_specs=in_specs,
        out_specs=[VM] * len(out_shapes),
        scratch_shapes=jax.tree.leaves(scratch_plan()),
        compiler_params=pltpu.CompilerParams(
            vmem_limit_bytes=VMEM_BYTES, collective_id=1, has_side_effects=True
        ),
        name="everything",
    )(*in_tree.flatten_up_to(args))
    return named(jax.tree.unflatten(out_tree, results))


def finish_kernel(
    out_in, dx_in, att, ffn, sums,
    out, dx, gq, gk, gv, go, gate, up, down, attn_gain, ffn_gain, gain_q, gain_k,
):
    out[...] = out_in[...]
    dx[...] = dx_in[...].astype(F32)
    for zl in range(2):
        even, odd = att[zl, 0].astype(F32), att[zl, 1].astype(F32)
        for parity, block in enumerate((even, odd)):
            start = zl * 512 + parity * 256
            gq[:, start:start + 256] = block[:, 0:256]
            go[:, start:start + 256] = block[:, 384:640]
        even, odd = even[:, 256:384], odd[:, 256:384]
        low = lanes(even.shape) < 64
        gk[:, zl * 128:(zl + 1) * 128] = jnp.where(low, even, pltpu.roll(odd, 64, 1))
        gv[:, zl * 128:(zl + 1) * 128] = jnp.where(low, pltpu.roll(even, 64, 1), odd)
    for m, ref in enumerate((gate, up, down)):
        for k in range(8):
            for c in range(2):
                start = k * 512 + c * 256
                ref[:, start:start + 256] = ffn[m, k, c].astype(F32)
    dp = lax.axis_index("dp")
    row = sums[pl.ds(lax.div(dp, 4), 1), :]
    shift = lax.rem(4 - lax.rem(dp, 4), 4) * 64
    attn_gain[...] = pltpu.roll(row[:, 0:256], shift, 1)[:, 0:64]
    ffn_gain[...] = pltpu.roll(row[:, 256:512], shift, 1)[:, 0:64]
    gain_q[...] = sums[0:1, 512:576]
    gain_k[...] = sums[0:1, 576:640]


def rows_block(*shape):
    n = len(shape)
    return pl.BlockSpec(shape, lambda t: (0,) * (n - 2) + (t, 0))


def whole_block(*shape):
    return pl.BlockSpec(shape, lambda t: (0,) * len(shape))


def finished(r):
    tall = rows_block(64, 2048)
    full, half, wide = (rows_block(32, n) for n in (1024, 256, 4096))
    one = whole_block(1, 64)
    sizes = [(64, 1024), (64, 256), (64, 256), (64, 1024)] + [(64, 4096)] * 3 + [(1, 64)] * 4
    return pl.pallas_call(
        finish_kernel,
        grid=(2,),
        out_shape=(
            jax.ShapeDtypeStruct((128, 2048), BF),
            jax.ShapeDtypeStruct((128, 2048), F32),
        )
        + tuple(jax.ShapeDtypeStruct(size, F32) for size in sizes),
        in_specs=[
            tall, tall, rows_block(2, 2, 32, 640), rows_block(3, 8, 2, 32, 256), whole_block(8, 640),
        ],
        out_specs=[tall, tall, full, half, half, full, wide, wide, wide, one, one, one, one],
        name="finished",
    )(r.out, r.dx, r.att_grads, r.ffn_grads, r.gain_sums)


def rotary_tables():
    position = np.arange(128, dtype=np.float64)[:, None]
    lane = np.arange(128)
    angle = position * THETA ** (-2.0 * (lane % 32) / 64.0)[None, :]
    sign = np.where(lane % 64 < 32, -1.0, 1.0)
    return np.cos(angle).astype(np.float32), (np.sin(angle) * sign).astype(np.float32)


def on_device(
    tokens, gain_attn, w_query, w_key, w_value, gain_query, gain_key, w_out, gain_ffn,
    w_gate, w_up, w_down, cotangent,
):
    cos, sin = (jnp.asarray(t) for t in rotary_tables())
    rows = [jnp.pad(v, (0, 64)).reshape(1, 128) for v in (gain_attn, gain_ffn)]
    rows.append(jnp.concatenate([gain_query, gain_key]).reshape(1, 128))
    small = jnp.pad(jnp.concatenate(rows, axis=0), ((0, 13), (0, 0)))
    r = everything(
        tokens=tokens, cot=cotangent, small=small, cos=cos, sin=sin,
        wq=w_query, wk=w_key, wv=w_value, wo=w_out, wg=w_gate, wu=w_up, wd=w_down,
    )
    out, dx, gq, gk, gv, go, gate, up, down, attn, ffn, gain_q, gain_k = finished(r)
    attn, ffn, gain_q, gain_k = (v.reshape(64) for v in (attn, ffn, gain_q, gain_k))
    return out, dx, attn, gq, gk, gv, gain_q, gain_k, go, ffn, gate, up, down


def solution(mesh):
    return jax.shard_map(
        on_device,
        mesh=mesh,
        in_specs=(
            P("dp", None), P("dp"), P("dp", "head"), P("dp", "head"), P("dp", "head"),
            P(), P(), P("dp", "head"), P("dp"),
            P("dp", "tensor"), P("dp", "tensor"), P("dp", "tensor"), P("dp", None),
        ),
        out_specs=(
            P("dp", None), P("dp", None), P("dp"),
            P("dp", "head"), P("dp", "head"), P("dp", "head"),
            P(), P(), P("dp", "head"), P("dp"),
            P("dp", "tensor"), P("dp", "tensor"), P("dp", "tensor"),
        ),
        check_vma=False,
    )
```

```python
import types

import jax
import jax.numpy as jnp
import numpy as np
from jax import lax
from jax.experimental import pallas as pl
from jax.experimental.pallas import tpu as pltpu
from jax.sharding import PartitionSpec as P

BF = jnp.bfloat16
F32 = jnp.float32
MESH = pl.DeviceIdType.MESH
EPS = 1e-05
THETA = 1000000.0
VMEM_BYTES = 62 << 20
ATT_SLICES = ((0, 384), (384, 256))


def nn(a, b):
    return lax.dot_general(a, b, (((1,), (0,)), ((), ())), preferred_element_type=F32)


def nt(a, b):
    return lax.dot_general(a, b, (((1,), (1,)), ((), ())), preferred_element_type=F32)


def tn(a, b):
    return lax.dot_general(a, b, (((0,), (0,)), ((), ())), preferred_element_type=F32)


class Place:
    def __init__(self):
        dp = lax.axis_index("dp")
        self.c = lax.axis_index("head")
        self.zl = lax.axis_index("tensor")
        self.zh = lax.div(dp, 16)
        self.y = lax.rem(lax.div(dp, 4), 4)
        self.x = lax.rem(dp, 4)
        self.odd = lax.rem(self.y, 2)
        self.z = self.zh * 2 + self.zl

    def at(self, zh=None, y=None, x=None, c=None, zl=None):
        zh = self.zh if zh is None else zh
        y = self.y if y is None else y
        x = self.x if x is None else x
        return (zh * 16 + y * 4 + x, self.c if c is None else c, self.zl if zl is None else zl)

    def step(self, axis, by):
        if axis == "x":
            return self.at(x=lax.rem(self.x + by + 4, 4))
        if axis == "y":
            return self.at(y=lax.rem(self.y + by + 4, 4))
        z = lax.rem(self.z + by + 4, 4)
        return self.at(zh=lax.div(z, 2), zl=lax.rem(z, 2))

    def core(self):
        return self.at(c=1 - self.c)

    def zl_pair(self):
        return self.at(zl=1 - self.zl)

    def y_pair(self):
        return self.at(y=self.y + 1 - 2 * self.odd)

    def zh_pair(self):
        return self.at(zh=1 - self.zh)

    def ring(self, axis):
        return {"x": self.x, "y": self.y, "z": self.z}[axis]


class Copy:
    def __init__(self, copy):
        self.copy = copy
        self.left = True

    def wait_recv(self):
        self.copy.wait_recv()

    def wait_send(self):
        if self.left:
            self.copy.wait_send()
            self.left = False


class Group:
    def __init__(self, sem):
        self.sem = sem

    def wait(self, like):
        pltpu.make_async_copy(like, like, self.sem).wait()


class Net:
    def __init__(self, send_sems, recv_sems):
        self.send_sems = send_sems
        self.recv_sems = recv_sems
        self.slots = [None] * send_sems.shape[0]
        self.sends = 0
        self.groups = 0

    def group(self):
        k = self.groups
        assert k < self.recv_sems.shape[0], k
        self.groups += 1
        return Group(self.recv_sems.at[k])

    def send(self, src, dst, device, group=None):
        slot = self.sends % len(self.slots)
        self.sends += 1
        if self.slots[slot] is not None:
            self.slots[slot].wait_send()
        copy = pltpu.make_async_remote_copy(
            src_ref=src,
            dst_ref=dst,
            send_sem=self.send_sems.at[slot],
            recv_sem=(group or self.group()).sem,
            device_id=device,
            device_id_type=MESH,
        )
        copy.start()
        self.slots[slot] = Copy(copy)
        return self.slots[slot]

    def drain(self):
        for copy in self.slots:
            if copy is not None:
                copy.wait_send()


class Tagged:
    def __init__(self, net):
        self.net = net
        self.copies = []

    def group(self):
        return self.net.group()

    def send(self, src, dst, device, group=None):
        self.copies.append(self.net.send(src, dst, device, group))
        return self.copies[-1]

    def drain(self):
        for copy in self.copies:
            copy.wait_send()


def greet(devices):
    barrier = pltpu.get_barrier_semaphore()
    for device in devices:
        pl.semaphore_signal(barrier, inc=1, device_id=device, device_id_type=MESH)
    pl.semaphore_wait(barrier, len(devices))


def together(*pipelines):
    live = list(pipelines)
    while live:
        for pipe in list(live):
            try:
                next(pipe)
            except StopIteration:
                live.remove(pipe)
        yield


def step(*pipelines):
    for pipe in pipelines:
        next(pipe, None)


def finish(*pipelines):
    for _ in together(*pipelines):
        pass


def local(pairs, sems):
    copies = [pltpu.make_async_copy(s, d, sems.at[i]) for i, (s, d) in enumerate(pairs)]
    for copy in copies:
        copy.start()
    for copy in copies:
        copy.wait()


def add_refs(dst, srcs, rows=32):
    lead, height = dst.shape[:-2], dst.shape[-2]
    rows = min(rows, height)
    per = height // rows
    count = int(np.prod(lead, dtype=np.int64)) * per

    def body(t, carry):
        r = lax.rem(t, per)
        rest = lax.div(t, per)
        index = []
        for size in reversed(lead):
            index.insert(0, lax.rem(rest, size))
            rest = lax.div(rest, size)
        at = tuple(index) + (pl.ds(r * rows, rows), slice(None))
        total = srcs[0][at].astype(F32)
        for src in srcs[1:]:
            total = total + src[at].astype(F32)
        dst[at] = total.astype(dst.dtype)
        return carry

    lax.fori_loop(0, count, body, 0)


def ring_gather(net, place, axis, view, like):
    i = place.ring(axis)
    before, after = lax.rem(i + 3, 4), lax.rem(i + 1, 4)
    up, down = place.step(axis, 1), place.step(axis, -1)
    rest = net.group()
    u0 = net.send(view(i, 0), view(i, 0), up)
    d1 = net.send(view(i, 1), view(i, 1), down)
    net.send(view(i, 1), view(i, 1), up, rest)
    net.send(view(i, 0), view(i, 0), down, rest)
    yield
    u0.wait_recv()
    net.send(view(before, 0), view(before, 0), up, rest)
    d1.wait_recv()
    net.send(view(after, 1), view(after, 1), down, rest)
    yield
    rest.wait(like)


def ring_reduce(net, place, axis, view, far, near, out):
    i = place.ring(axis)
    before, after, across = lax.rem(i + 3, 4), lax.rem(i + 1, 4), lax.rem(i + 2, 4)
    up, down = place.step(axis, 1), place.step(axis, -1)
    fars, nears = net.group(), net.group()
    net.send(view(across, 0), far.at[0], up, fars)
    net.send(view(across, 1), far.at[1], down, fars)
    yield
    net.send(view(after, 1), near.at[1], up, nears)
    net.send(view(before, 0), near.at[2], down, nears)
    yield
    fars.wait(far)
    add_refs(far.at[0], [far.at[0], view(after, 0)])
    net.send(far.at[0], near.at[0], up, nears)
    add_refs(far.at[1], [far.at[1], view(before, 1)])
    net.send(far.at[1], near.at[3], down, nears)
    yield
    nears.wait(near)
    add_refs(out(0), [view(i, 0), near.at[0], near.at[2]])
    add_refs(out(1), [view(i, 1), near.at[1], near.at[3]])


def cross_gather(net, place, one, two, view, likes, late=None, also=None, only=None):
    ring = [lax.rem(place.ring(one) + k, 4) for k in range(4)]
    other = [lax.rem(place.ring(two) + k, 4) for k in range(4)]
    up = {one: place.step(one, 1), two: place.step(two, 1)}
    down = {one: place.step(one, -1), two: place.step(two, -1)}
    corners = []
    last = [net.group(), net.group()]
    finals = [[], []]

    def spread(block, axis, group):
        net.send(block, block, up[axis], group)
        net.send(block, block, down[axis], group)

    def arrived(block):
        if also is not None:
            also(block)
        return block

    def along(axis, part, k, half=None):
        if axis == one:
            return view(part, ring[k], other[0], half)
        return view(part, ring[0], other[k], half)

    def turn(axis, part, k):
        across = two if axis == one else one
        half = 1 if axis == one else 0
        if only is not None and half != only:
            return
        group = net.group()
        spread(along(axis, part, k, half), across, group)
        corners.append((axis, part, k, half, across, group))

    def own(part):
        group = net.group()
        block = view(part, ring[0], other[0], None)
        for axis in (one, two):
            spread(block, axis, group)
        return group

    crosses = [own(0)]
    if late is None:
        crosses.append(own(1))
    yield
    if late is not None:
        late.wait_recv()
        crosses.append(own(1))
        yield
    far = net.group()
    for part in (0, 1):
        crosses[part].wait(likes(None, 4))
        order = (3, 1) if part == 0 else (1, 3)
        for n, k in enumerate(order):
            for axis in (one, two):
                block = arrived(along(axis, part, k))
                if n == 0:
                    net.send(block, block, (up, down)[part][axis], far)
                turn(axis, part, k)
        yield
    far.wait(likes(None, 4))
    for part in (0, 1):
        for axis in (one, two):
            arrived(along(axis, part, 2))
            turn(axis, part, 2)
    yield
    for n, (axis, part, k, half, across, group) in enumerate(corners):
        group.wait(likes(half, 2))
        for which, by in ((0, 3), (1, 1)):
            if axis == one:
                block = view(part, ring[k], other[by], half)
                final = view(part, ring[k], other[2], half)
            else:
                block = view(part, ring[by], other[k], half)
                final = view(part, ring[2], other[k], half)
            arrived(block)
            if which == part:
                net.send(block, block, (up, down)[part][across], last[half])
                finals[half].append(final)
        if n % 4 == 3:
            yield
    for half in (0, 1):
        if finals[half]:
            last[half].wait(likes(half, len(finals[half])))
            for final in finals[half]:
                arrived(final)


def order_reduce(net, place, one, two, view, s, out, other_out=None):
    ring = [lax.rem(place.ring(one) + k, 4) for k in range(4)]
    other = [lax.rem(place.ring(two) + k, 4) for k in range(4)]
    up, down = place.step(one, 1), place.step(one, -1)
    order = (2, 1, 3, 0)
    fars = {k: net.group() for k in order}
    nears = {k: net.group() for k in order}
    others = net.group()
    for k in order:
        net.send(view(0, ring[2], other[k]), s.far.at[k, 0], up, fars[k])
        net.send(view(1, ring[2], other[k]), s.far.at[k, 1], down, fars[k])
    for k in order:
        net.send(view(1, ring[1], other[k]), s.near.at[k, 1], up, nears[k])
        net.send(view(0, ring[3], other[k]), s.near.at[k, 2], down, nears[k])
    yield
    for k in order:
        fars[k].wait(s.far.at[k])
        add_refs(s.far.at[k, 0], [s.far.at[k, 0], view(0, ring[1], other[k])])
        net.send(s.far.at[k, 0], s.near.at[k, 0], up, nears[k])
        add_refs(s.far.at[k, 1], [s.far.at[k, 1], view(1, ring[3], other[k])])
        net.send(s.far.at[k, 1], s.near.at[k, 3], down, nears[k])
        if k != 1:
            yield
    for k in order:
        nears[k].wait(s.near.at[k])
        for p in (0, 1):
            add_refs(
                s.mid.at[k, p],
                [view(p, ring[0], other[k]), s.near.at[k, p], s.near.at[k, 2 + p]],
            )
        if k:
            net.send(s.mid.at[k], s.last.at[k - 1], place.step(two, k), others)
        if k != 1:
            yield
    others.wait(s.last)
    for p in (0, 1):
        if other_out is None:
            add_refs(out(p), [s.mid.at[0, p]] + [s.last.at[k, p] for k in range(3)])
        else:
            add_refs(out(p), [s.mid.at[0, p], s.last.at[1, p]])
            add_refs(other_out(p), [s.last.at[0, p], s.last.at[2, p]])


def order_buffers(rows, columns):
    return dict(
        far=pltpu.VMEM((4, 2, rows, columns), BF),
        near=pltpu.VMEM((4, 4, rows, columns), BF),
        mid=pltpu.VMEM((4, 2, rows, columns), BF),
        last=pltpu.VMEM((3, 2, rows, columns), BF),
    )


def torus_gather(net, place, buf, only=None):
    c = place.c
    other = place.core()
    swaps = net.group()

    def also(block):
        net.send(block, block, other, swaps)

    def rows(half):
        return pl.ds(0, 32) if half is None or only is not None else pl.ds(half * 16, 16)

    def view(part, i, j, half):
        return buf.at[i, j, c, rows(half), pl.ds(part * 1024, 1024)]

    def likes(half, n):
        return buf.at[pl.ds(0, 2), pl.ds(0, n // 2), 0, rows(half), pl.ds(0, 1024)]

    also(buf.at[place.z, place.x, c])
    yield from cross_gather(net, place, "z", "x", view, likes, also=also, only=only)
    yield
    swaps.wait(buf.at[:, :, 1 - c])


def torus_buffers():
    return dict(
        both=pltpu.VMEM((4, 4, 32, 2048), BF),
        halves=[order_buffers(16, 1024), order_buffers(16, 1024)],
        total=pltpu.VMEM((32, 2048), F32),
    )


def core_sum(place, src, swap, s, k):
    swap.wait_recv()
    add_refs(s.both.at[k], [s.both.at[k], src.at[k, :, place.c]])


def torus_reduce(net, place, s, orders):
    def half(k):
        def at(part):
            return pl.ds(k * 16, 16), pl.ds(part * 1024, 1024)

        def view(p, i, j):
            zi, xi = (i, j) if orders[k] == "z" else (j, i)
            return s.both.at[(zi, xi) + at(p)]

        second = "x" if orders[k] == "z" else "z"
        return order_reduce(
            net, place, orders[k], second, view, s.halves[k], lambda p: s.total.at[at(p)]
        )

    yield from together(half(0), half(1))


def quad_gather(net, place, buf):
    c, zl = place.c, place.zl
    own = buf.at[pl.ds(c * 64 + zl * 32, 32)]
    one = net.send(own, own, place.zl_pair())
    yield
    one.wait_recv()
    half = buf.at[pl.ds(c * 64, 64)]
    two = net.send(half, half, place.core())
    yield
    two.wait_recv()


def oct_reduce(net, place, src, b):
    c, zl, q = place.c, place.zl, place.odd
    theirs = pl.ds((1 - c) * 64, 64)
    one = net.send(src.at[1 - q, theirs], b.core.at[1 - q], place.core())
    yield
    one.wait_recv()
    b.for_y[...] = (
        src[1 - q, pl.ds(c * 64, 64), :].astype(F32) + b.core[1 - q].astype(F32)
    ).astype(BF)
    far, near = pl.ds((1 - zl) * 32, 32), pl.ds(zl * 32, 32)
    two = [net.send(b.for_y.at[r], b.y.at[r], place.y_pair()) for r in (far, near)]
    yield
    one = net.send(src.at[q, theirs], b.core.at[q], place.core())
    yield
    one.wait_recv()
    two[0].wait_recv()
    theirs = src[q, pl.ds(c * 64 + (1 - zl) * 32, 32), :].astype(F32)
    theirs = theirs + b.core[q, far, :].astype(F32) + b.y[far, :].astype(F32)
    b.for_zl[...] = theirs.astype(BF)
    three = net.send(b.for_zl, b.zl, place.zl_pair())
    yield
    two[1].wait_recv()
    three.wait_recv()


def oct_total(place, src, b):
    c, zl, q = place.c, place.zl, place.odd
    near = pl.ds(zl * 32, 32)
    total = src[q, pl.ds(c * 64 + zl * 32, 32), :].astype(F32) + b.core[q, near, :].astype(F32)
    return total + b.y[near, :].astype(F32) + b.zl[...].astype(F32)


def oct_buffers():
    return dict(
        core=pltpu.VMEM((2, 64, 2048), BF),
        for_y=pltpu.VMEM((64, 2048), BF),
        y=pltpu.VMEM((64, 2048), BF),
        for_zl=pltpu.VMEM((32, 2048), BF),
        zl=pltpu.VMEM((32, 2048), BF),
    )


def quad_gather(net, place, buf):
    c, zl = place.c, place.zl
    own = buf.at[pl.ds(c * 64 + zl * 32, 32)]
    one = net.send(own, own, place.zl_pair())
    yield
    one.wait_recv()
    half = buf.at[pl.ds(c * 64, 64)]
    two = net.send(half, half, place.core())
    yield
    two.wait_recv()


def oct_gather(net, place, buf):
    c, zl, q = place.c, place.zl, place.odd
    own = buf.at[q, pl.ds(c * 64 + zl * 32, 32)]
    from_zl = net.send(own, own, place.zl_pair())
    from_y = [net.send(own, own, place.y_pair())]
    yield
    from_zl.wait_recv()
    other = buf.at[q, pl.ds(c * 64 + (1 - zl) * 32, 32)]
    from_y.append(net.send(other, other, place.y_pair()))
    half = buf.at[q, pl.ds(c * 64, 64)]
    from_core = net.send(half, half, place.core())
    yield
    from_core.wait_recv()
    yield
    for copy in from_y:
        copy.wait_recv()
    half = buf.at[1 - q, pl.ds(c * 64, 64)]
    from_core = net.send(half, half, place.core())
    yield
    from_core.wait_recv()


def sem_scratch(n):
    return [pltpu.SemaphoreType.DMA((n,)), pltpu.SemaphoreType.DMA((n,))]


ANY = pl.BlockSpec(memory_space=pl.ANY)
VM = pl.BlockSpec(memory_space=pltpu.VMEM)


def lanes(shape):
    return lax.broadcasted_iota(jnp.int32, shape, len(shape) - 1)


def partner(v):
    n = v.shape[-1]
    low = lax.rem(lanes(v.shape), 64) < 32
    return jnp.where(low, pltpu.roll(v, n - 32, 1), pltpu.roll(v, 32, 1))


def head_mean(v):
    n = v.shape[-1]
    r = lax.broadcasted_iota(jnp.int32, (n, n), 0)
    same = lax.div(r, 64) == lax.div(lanes((n, n)), 64)
    return lax.dot_general(
        v, jnp.where(same, 1.0 / 64.0, 0.0), (((1,), (0,)), ((), ())),
        precision=lax.Precision.HIGHEST, preferred_element_type=F32,
    )


def half_of(v, which):
    upper = lanes(v.shape) >= 64
    keep = upper if which else jnp.logical_not(upper)
    return jnp.where(keep, v, jnp.zeros_like(v))


def swap_halves(v):
    return pltpu.roll(v.astype(F32), 64, 1).astype(v.dtype)


def rows_rms(v):
    return lax.rsqrt(jnp.mean(v * v, axis=-1, keepdims=True) + EPS)


N_SENDS = 48
N_GROUPS = 149
N_LOCAL = 17


def input_plan():
    return dict(
        tokens=ANY, cot=ANY, small=ANY, cos=ANY, sin=ANY,
        wq=ANY, wk=ANY, wv=ANY, wo=ANY, wg=ANY, wu=ANY, wd=ANY,
    )


def output_plan():
    return dict(
        out=jax.ShapeDtypeStruct((128, 2048), BF),
        dx=jax.ShapeDtypeStruct((128, 2048), BF),
        att_grads=jax.ShapeDtypeStruct((2, 2, 64, 640), BF),
        ffn_grads=jax.ShapeDtypeStruct((3, 8, 2, 64, 256), BF),
        gain_sums=jax.ShapeDtypeStruct((8, 640), F32),
    )


def scratch_plan():
    return dict(
        tok=pltpu.VMEM((2, 128, 2048), BF),
        kv_in=pltpu.VMEM((2, 64, 128), BF),
        shard=pltpu.VMEM((2, 2, 64, 640), BF),
        small_in=pltpu.VMEM((16, 128), BF),
        cos_in=pltpu.VMEM((128, 128), F32),
        sin_in=pltpu.VMEM((128, 128), F32),
        att=pltpu.VMEM((2, 4, 4, 64, 640), BF),
        gains=pltpu.VMEM((2, 4, 4, 16, 128), BF),
        ffn=pltpu.VMEM((3, 2, 4, 4, 64, 256), BF),
        cots=pltpu.VMEM((4, 4, 2, 32, 2048), BF),
        xn2=pltpu.VMEM((4, 4, 2, 32, 2048), BF),
        xn=pltpu.VMEM((256, 2048), BF),
        z=pltpu.VMEM((256, 384), F32),
        qk=pltpu.VMEM((256, 384), BF),
        p=pltpu.VMEM((8, 128, 128), F32),
        o=pltpu.VMEM((256, 256), BF),
        branch=pltpu.VMEM((2, 128, 2048), BF),
        branch_sum=oct_buffers(),
        dxn_sum=oct_buffers(),
        hidden=pltpu.VMEM((32, 2048), F32),
        da=pltpu.VMEM((4, 256, 256), F32),
        ab=pltpu.VMEM((4, 256, 256), BF),
        dg=pltpu.VMEM((4, 256, 256), BF),
        du=pltpu.VMEM((4, 256, 256), BF),
        dxn2_part=pltpu.VMEM((4, 4, 2, 32, 2048), BF),
        ffn_part=pltpu.VMEM((3, 2, 4, 4, 64, 256), BF),
        ffn_far=pltpu.VMEM((4, 2, 3, 64, 256), BF),
        ffn_near=pltpu.VMEM((4, 4, 3, 64, 256), BF),
        ffn_mid=pltpu.VMEM((4, 2, 3, 64, 256), BF),
        dh=pltpu.VMEM((32, 2048), F32),
        dhb=pltpu.VMEM((2, 128, 2048), BF),
        ffn_gain_grad=pltpu.VMEM((1, 2048), F32),
        d_heads=pltpu.VMEM((256, 384), F32),
        att_part=pltpu.VMEM((2, 4, 4, 64, 640), BF),
        dxn_part=pltpu.VMEM((2, 128, 2048), BF),
        both_z=pltpu.VMEM((2, 2, 64, 640), BF),
        from_z=pltpu.VMEM((2, 2, 2, 64, 640), BF),
        gain_quad=pltpu.VMEM((4, 8, 640), F32),
        gain_y=pltpu.VMEM((4, 8, 640), F32),
        gain_xz=pltpu.VMEM((8, 8, 640), F32),
        dxn2_sum=torus_buffers(),
        out_sum=torus_buffers(),
        slices=[order_buffers(64, n) for _, n in ATT_SLICES],
        send_sems=pltpu.SemaphoreType.DMA((N_SENDS,)),
        recv_sems=pltpu.SemaphoreType.DMA((N_GROUPS,)),
        sems=pltpu.SemaphoreType.DMA((N_LOCAL,)),
    )


def named(plan):
    if isinstance(plan, dict):
        return types.SimpleNamespace(**{k: named(v) for k, v in plan.items()})
    if isinstance(plan, list):
        return [named(v) for v in plan]
    return plan


def kernel(*refs):
    s = types.SimpleNamespace()
    for plan in (input_plan(), output_plan(), scratch_plan()):
        leaves, tree = jax.tree.flatten(plan)
        part = jax.tree.unflatten(tree, refs[: len(leaves)])
        refs = refs[len(leaves):]
        vars(s).update(vars(named(part)))
    send_sems, recv_sems, sems = s.send_sems, s.recv_sems, s.sems
    me = Place()
    zh, y, x, c, zl, z, odd = me.zh, me.y, me.x, me.c, me.zl, me.z, me.odd
    net = Net(send_sems, recv_sems)
    att, ffn = s.att, s.ffn
    rows = pl.ds(c * 64 + zl * 32, 32)


    def piece(k):
        return pl.ds(pl.multiple_of(k * 512 + c * 256, 256), 256)

    def load(pairs):
        started = []
        for src, dst in pairs:
            started.append(pltpu.make_async_copy(src, dst, sems.at[len(loads)]))
            loads.append(started[-1])
            started[-1].start()
        return started

    loads = []
    narrow = pl.ds(pl.multiple_of(zl * 128, 128), 128)
    mine = zh * 4 + x
    att_copies = load([(w.at[:, narrow], s.kv_in.at[k]) for k, w in enumerate((s.wk, s.wv))])
    for parity in range(2):
        wide = pl.ds(pl.multiple_of(zl * 512 + parity * 256, 256), 256)
        block = s.shard.at[0, parity]
        att_copies += load(
            [
                (s.wq.at[:, wide], block.at[:, pl.ds(0, 256)]),
                (s.wo.at[:, wide], block.at[:, pl.ds(384, 256)]),
            ]
        )
    (small_copy,) = load([(s.small, s.small_in)])
    (cots_copy,) = load([(s.cot.at[rows], s.cots.at[z, x, c])])
    ffn_copies = load(
        [(w.at[:, piece(mine)], ffn.at[m, zh, y, x]) for m, w in enumerate((s.wg, s.wu, s.wd))]
    )
    (tok_copy,) = load([(s.tokens, s.tok.at[odd])])
    other_copies = load([(s.cos, s.cos_in), (s.sin, s.sin_in)])
    greet(
        [me.step("x", 1), me.step("x", 2), me.step("x", -1)]
        + [me.step("y", 1), me.step("y", 2), me.step("y", -1)]
        + [me.step("z", 1), me.step("z", 2), me.step("z", -1)]
        + [me.core(), me.at(c=1 - c, zl=1 - zl)]
        + [me.at(zh=1 - zh, x=lax.rem(x + k, 4)) for k in (1, 2, 3)]
    )

    def gather_attention():
        shard = s.shard

        def plane(p):
            return 1 - zh if p else zh

        def blocks(n):
            return att.at[0, 0, pl.ds(0, n)]

        rings = {}
        last = net.group()

        def set_off(p, k):
            block = att.at[plane(p), lax.rem(y + k, 4), x]
            rings[p, k] = net.group()
            net.send(block, block, me.step("x", 1), rings[p, k])
            net.send(block, block, me.step("x", -1), rings[p, k])

        def along_y(p):
            group = net.group()
            for k in (1, 3, 2):
                parity = odd if k == 2 else 1 - odd
                dst = att.at[plane(p), y, x]
                net.send(shard.at[p, parity], dst, me.step("y", k), group)
            s.att[plane(p), y, x] = shard[p, odd]
            set_off(p, 0)
            return group

        swap = net.send(shard.at[0], shard.at[1], me.zh_pair())
        groups = [along_y(0)]
        yield
        swap.wait_recv()
        groups.append(along_y(1))
        yield
        for p in (0, 1):
            groups[p].wait(blocks(3))
            for k in (1, 3, 2):
                set_off(p, k)
            yield
        for k in (0, 1, 3, 2):
            for p in (0, 1):
                rings[p, k].wait(blocks(2))
                by = 1 if p else 3
                block = att.at[plane(p), lax.rem(y + k, 4), lax.rem(x + by, 4)]
                net.send(block, block, me.step("x", -1 if p else 1), last)
            yield
        last.wait(att.at[:, 0])

    def gather_tokens():
        half = s.tok.at[odd, pl.ds(c * 64, 64)]
        copy = net.send(half, half, me.y_pair())
        yield
        copy.wait_recv()
        half = s.tok.at[1 - odd, pl.ds(c * 64, 64)]
        copy = net.send(half, half, me.core())
        yield
        copy.wait_recv()

    def gather_ffn():
        arrivals = [net.group(), net.group()]
        for dz in (0, 1):
            for dx in range(4):
                if dz == 0 and dx == 0:
                    continue
                tx = lax.rem(x + dx, 4)
                tz = 1 - zh if dz else zh
                for m, w in enumerate((s.wg, s.wu, s.wd)):
                    net.send(
                        w.at[:, piece(tz * 4 + tx)],
                        ffn.at[m, zh, y, x],
                        me.at(zh=tz, x=tx),
                        arrivals[dz],
                    )
        yield
        arrivals[0].wait(s.ffn_part.at[:, 0, 0, pl.ds(0, 3)])
        arrivals[1].wait(s.ffn_part.at[:, 0, 0])
        for copy in ffn_copies:
            copy.wait()
        yield from ring_gather(
            net, me, "y", lambda i, p: ffn.at[:, p, i], s.ffn_part.at[:, 0]
        )

    def gather_gains():
        own_gain = s.gains.at[zh, y, x]
        near, far = net.group(), net.group()
        for k in range(4):
            device = lax.rem(x + k, 4)
            if k:
                net.send(own_gain, own_gain, me.at(x=device), near)
            net.send(own_gain, own_gain, me.at(zh=1 - zh, x=device), far)
        yield
        near.wait(s.gains.at[0, 0, pl.ds(0, 3)])
        far.wait(s.gains.at[0, 0])
        row = s.gains.at[:, y]
        group = net.group()
        for k in (1, -1, 2):
            net.send(row, row, me.step("y", k), group)
        yield
        group.wait(s.gains.at[:, pl.ds(0, 3)])

    def gain_row(k):
        blocks = []
        for pair in range(16):
            a, b = 2 * pair, 2 * pair + 1
            total = None
            for d in (a, b):
                block = s.gains[d // 16, d // 4 % 4, d % 4].astype(F32)
                total = block if total is None else total + block
            blocks.append(total[k:k + 1, :])
        return jnp.concatenate(blocks, axis=1)

    for copy in att_copies:
        copy.wait()
    key, value = s.kv_in[0], s.kv_in[1]
    low_half = lanes((64, 128)) < 64
    s.shard[0, 0, :, 256:384] = jnp.where(low_half, key, swap_halves(value))
    s.shard[0, 1, :, 256:384] = jnp.where(low_half, swap_halves(key), value)
    attention = gather_attention()
    gains = gather_gains()
    weights = gather_ffn()
    cots = torus_gather(net, me, s.cots, only=0)
    pair_tokens = gather_tokens()
    step(attention)
    small_copy.wait()
    small = s.small_in[...].astype(F32)
    s.gains[zh, y, x] = jnp.where(lax.rem(x, 2) == 1, pltpu.roll(small, 64, 1), small).astype(BF)
    step(gains, weights, attention, attention, gains, attention)
    tok_copy.wait()
    step(pair_tokens, attention)
    finish(gains)
    for copy in other_copies:
        copy.wait()
    step(pair_tokens, attention, weights)
    cots_copy.wait()
    step(attention, cots)
    finish(pair_tokens)
    t = s.tok[...].reshape(256, 2048).astype(F32)
    s.xn[...] = (t * rows_rms(t) * gain_row(0)).astype(BF)
    step(attention, cots)
    finish(attention)


    step(cots)
    raw = nn(s.xn[...], att[:, :, :, :, 0:384].reshape(2048, 384))
    s.z[...] = raw
    step(cots)
    both_gains = small[2:3, :]
    turned = pltpu.roll(both_gains, 64, 1)
    low = lanes((1, 128)) < 64
    gain_q = jnp.where(low, both_gains, turned)
    head_gain = jnp.concatenate([gain_q, gain_q, turned], axis=1)
    cos, sin = (
        jnp.concatenate([jnp.concatenate([ref[...]] * 3, axis=1)] * 2, axis=0)
        for ref in (s.cos_in, s.sin_in)
    )
    is_value = lanes((256, 384)) >= 320
    n = raw * lax.rsqrt(head_mean(raw * raw) + EPS) * head_gain
    s.qk[...] = jnp.where(is_value, raw, n * cos + partner(n) * sin).astype(BF)
    step(cots)
    causal = lax.broadcasted_iota(jnp.int32, (128, 128), 0) >= lanes((128, 128))

    def attend(q):
        at = pl.ds(pl.multiple_of(q * 128, 128), 128)
        kv = s.qk[at, 256:384]
        sides = (kv, swap_halves(kv))
        for block in range(2):
            cols = slice(block * 128, (block + 1) * 128)
            out = None
            for side in range(2):
                query = half_of(s.qk[at, cols], side)
                score = jnp.where(causal, nt(query, sides[side]) * 0.125, -1e30)
                e = jnp.exp(score - jnp.max(score, axis=-1, keepdims=True))
                p = e / jnp.sum(e, axis=-1, keepdims=True)
                s.p[q * 4 + 2 * block + side] = p
                part = nn(p.astype(BF), half_of(sides[1 - side], side))
                out = part if out is None else out + part
            s.o[at, cols] = out.astype(BF)

    def project(q):
        at = pl.ds(pl.multiple_of(q * 128, 128), 128)
        branch = nt(s.o[at, :], att[:, :, :, :, 384:640].reshape(2048, 256))
        s.branch[q] = branch.astype(BF)

    attend(1 - odd)
    project(1 - odd)
    summed = oct_reduce(net, me, s.branch, s.branch_sum)
    step(summed)
    attend(odd)
    step(summed)
    project(odd)
    step(summed, cots, weights)
    finish(summed)
    hidden = s.tok[odd, rows, :].astype(F32)
    hidden = hidden + oct_total(me, s.branch, s.branch_sum)
    s.hidden[...] = hidden
    s.xn2[z, x, c] = (hidden * rows_rms(hidden) * gain_row(1)).astype(BF)
    normed_net = Tagged(net)
    normed = torus_gather(normed_net, me, s.xn2)
    step(normed, normed, normed)
    finish(cots, weights)
    step(normed, normed)


    def weight(m):
        return ffn[m].reshape(2048, 256)

    for k in range(4):
        s.da[k] = nn(s.cots[k].reshape(256, 2048), weight(2))
        step(normed)
    finish(normed)
    swaps = []
    for k in range(4):
        xk = s.xn2[k].reshape(256, 2048)
        g, u, da = nn(xk, weight(0)), nn(xk, weight(1)), s.da[k]
        sigma = jax.nn.sigmoid(g)
        swish = g * sigma
        s.ab[k] = (swish * u).astype(BF)
        dg = (da * u * sigma * (1.0 + g * (1.0 - sigma))).astype(BF)
        du = (da * swish).astype(BF)
        s.dg[k] = dg
        s.du[k] = du
        part = (nt(dg, weight(0)) + nt(du, weight(1))).astype(BF)
        s.dxn2_part[k] = part.reshape(4, 2, 32, 2048)
        swaps.append(
            net.send(s.dxn2_part.at[k, :, 1 - c], s.dxn2_sum.both.at[k], me.core())
        )
        if k:
            core_sum(me, s.dxn2_part, swaps[k - 1], s.dxn2_sum, k - 1)


    dxn2 = torus_reduce(net, me, s.dxn2_sum, "zx")

    def weight_grads(k):
        yk = lax.rem(y + k, 4)

        def one(p, carry):
            cols = pl.ds(pl.multiple_of((p * 4 + yk) * 256, 256), 256)
            xd = s.xn2[:, :, :, :, cols].reshape(1024, 256)
            dyd = s.cots[:, :, :, :, cols].reshape(1024, 256)
            for m, left, right in ((0, xd, s.dg), (1, xd, s.du), (2, dyd, s.ab)):
                grad = tn(left, right[...].reshape(1024, 256))
                s.ffn_part[m, p, yk] = grad.astype(BF).reshape(4, 64, 256)
            return carry

        lax.fori_loop(0, 2, one, 0)

    def reduce_ffn_grads():
        part, grads = s.ffn_part, s.ffn_grads
        arrivals = [net.group(), net.group()]
        dst = grads.at[:, mine, c]
        keep = pltpu.make_async_copy(s.ffn_mid.at[0, zh], dst, sems.at[N_LOCAL - 1])

        def block(k):
            xk = lax.rem(x + k, 4)
            far, near, mid = (ref.at[k] for ref in (s.ffn_far, s.ffn_near, s.ffn_mid))
            yield from ring_reduce(
                net, me, "y", lambda i, p: part.at[:, p, i, xk], far, near, lambda p: mid.at[p]
            )
            if k:
                net.send(mid.at[zh], dst, me.at(x=xk), arrivals[0])
            else:
                keep.start()
            net.send(mid.at[1 - zh], dst, me.at(zh=1 - zh, x=xk), arrivals[1])

        yield from together(*[block(k) for k in (2, 1, 3, 0)])
        keep.wait()
        arrivals[0].wait(s.ffn_part.at[:, 0, 0, pl.ds(0, 3)])
        arrivals[1].wait(s.ffn_part.at[:, 0, 0])
        swap = net.send(grads.at[:, :, c], grads.at[:, :, c], me.core())
        yield
        swap.wait_recv()

    ffn_grads = reduce_ffn_grads()
    weight_grads(2)
    step(ffn_grads)
    core_sum(me, s.dxn2_part, swaps[3], s.dxn2_sum, 3)
    step(dxn2)
    weight_grads(1)
    weight_grads(3)
    step(ffn_grads, dxn2, dxn2)
    weight_grads(0)
    step(dxn2)
    swaps = []
    normed_net.drain()
    for k in range(4):
        part = nt(s.ab[k], weight(2)).astype(BF)
        s.xn2[k] = part.reshape(4, 2, 32, 2048)
        swaps.append(net.send(s.xn2.at[k, :, 1 - c], s.out_sum.both.at[k], me.core()))
        if k % 2 == 1:
            step(dxn2)
    finish(dxn2)
    hidden = s.hidden[...]
    r = rows_rms(hidden)
    hat = hidden * r
    d = s.dxn2_sum.total[...]
    s.ffn_gain_grad[...] = jnp.sum(d * hat, axis=0, keepdims=True)
    scaled = d * gain_row(1)
    dh = s.cots[z, x, c].astype(F32)
    dh = dh + r * (scaled - hat * jnp.mean(scaled * hat, axis=-1, keepdims=True))
    s.dh[...] = dh
    s.dhb[odd, rows, :] = dh.astype(BF)
    spread = oct_gather(net, me, s.dhb)
    step(spread)

    def finish_output():
        for k in range(4):
            core_sum(me, s.xn2, swaps[k], s.out_sum, k)
        yield from torus_reduce(net, me, s.out_sum, "zz")
        s.out[rows, :] = (s.hidden[...] + s.out_sum.total[...]).astype(BF)
        yield from quad_gather(net, me, s.out)

    output = finish_output()
    step(spread, output, spread)


    def reduce_att_grads(k):
        start, width = ATT_SLICES[k]
        cols = pl.ds(start, width)
        both_z = s.both_z
        yield from order_reduce(
            net, me, "x", "y", lambda p, i, j: s.att_part.at[p, j, i, :, cols], s.slices[k],
            lambda p: both_z.at[p, odd, :, cols], lambda p: both_z.at[p, 1 - odd, :, cols],
        )
        arrivals = net.group()
        mine_z = both_z.at[zh, :, :, cols]
        theirs = both_z.at[1 - zh, :, :, cols]
        dst = s.from_z.at[zl, 1, :, :, cols]
        net.send(theirs, dst, me.at(zh=1 - zh), arrivals)
        net.send(theirs, dst, me.at(zh=1 - zh, zl=1 - zl), arrivals)
        net.send(mine_z, s.from_z.at[zl, 0, :, :, cols], me.at(zl=1 - zl), arrivals)
        yield
        arrivals.wait(s.slices[k].last)
        add_refs(s.att_grads.at[zl, :, :, cols], [mine_z, s.from_z.at[zl, 1, :, :, cols]])
        add_refs(
            s.att_grads.at[1 - zl, :, :, cols],
            [s.from_z.at[1 - zl, 0, :, :, cols], s.from_z.at[1 - zl, 1, :, :, cols]],
        )

    def attend_back(q):
        at = pl.ds(pl.multiple_of(q * 128, 128), 128)
        do = nn(s.dhb[q], att[:, :, :, :, 384:640].reshape(2048, 256)).astype(BF)
        kv = s.qk[at, 256:384]
        sides = (kv, swap_halves(kv))
        dk = [jnp.zeros((128, 128), F32)] * 2
        dv = [jnp.zeros((128, 128), F32)] * 2
        for block in range(2):
            cols = slice(block * 128, (block + 1) * 128)
            dq = None
            for side in range(2):
                p = s.p[q * 4 + 2 * block + side]
                dob = half_of(do[:, cols], side)
                query = half_of(s.qk[at, cols], side)
                dp = nt(dob, sides[1 - side])
                dv[side] = dv[side] + tn(p.astype(BF), dob)
                ds = (p * (dp - jnp.sum(p * dp, axis=-1, keepdims=True))).astype(BF)
                part = nn(ds, half_of(sides[side], side))
                dq = part if dq is None else dq + part
                dk[side] = dk[side] + tn(ds, query)
            s.d_heads[at, cols] = dq * 0.125
        dkey = (dk[0] + pltpu.roll(dk[1], 64, 1)) * 0.125
        s.d_heads[at, 256:384] = dkey + dv[1] + pltpu.roll(dv[0], 64, 1)

    attend_back(odd)
    step(spread, ffn_grads)
    finish(spread)
    grad = tn(s.dhb[...].reshape(256, 2048), s.o[...]).astype(BF)
    s.att_part[:, :, :, :, 384:640] = grad.reshape(2, 4, 4, 64, 256)
    slices = [reduce_att_grads(k) for k in range(2)]
    step(slices[1], output)
    attend_back(1 - odd)
    step(output, slices[1])
    dout = s.d_heads[...]
    dn = dout * cos - partner(dout) * sin
    z_raw = s.z[...]
    r = lax.rsqrt(head_mean(z_raw * z_raw) + EPS)
    zhat = z_raw * r
    dgain = jnp.sum(dn * zhat, axis=0, keepdims=True)
    q_pairs = dgain[:, 0:128] + dgain[:, 128:256]
    q_pairs = q_pairs + pltpu.roll(q_pairs, 64, 1)
    k_pairs = pltpu.roll(dgain[:, 256:384], 64, 1)
    dz = dn * head_gain
    dz = r * (dz - zhat * head_mean(dz * zhat))
    low_grads = jnp.where(is_value, dout, dz).astype(BF)
    step(slices[1], ffn_grads)
    grad = tn(s.xn[...], low_grads).astype(BF)
    s.att_part[:, :, :, :, 0:384] = grad.reshape(2, 4, 4, 64, 384)
    step(slices[0], slices[1])
    gain_grad = jnp.zeros((1, 2048), F32)
    for q in range(2):
        at = slice(q * 128, (q + 1) * 128)
        back = nt(low_grads[at], att[:, :, :, :, 0:384].reshape(2048, 384))
        s.dxn_part[q] = back.astype(BF)
        t = s.tok[q].astype(F32)
        gain_grad = gain_grad + jnp.sum(back * (t * rows_rms(t)), axis=0, keepdims=True)
    summed = oct_reduce(net, me, s.dxn_part, s.dxn_sum)
    step(summed)

    def gain_grads():
        sums = s.gain_sums
        for k in range(8):
            part = slice(k * 256, (k + 1) * 256)
            sums[k:k + 1, 0:256] = gain_grad[:, part]
            sums[k:k + 1, 256:512] = s.ffn_gain_grad[:, part]
        row = lax.broadcasted_iota(jnp.int32, (8, 128), 0)
        head_grad = jnp.where(lanes((8, 128)) < 64, q_pairs, k_pairs)
        sums[:, 512:640] = jnp.where(row == 0, head_grad, 0.0)

        def total(buf, own, devices):
            group = net.group()
            for device in devices:
                net.send(buf.at[own], buf.at[own], device, group)
            yield
            group.wait(buf.at[pl.ds(0, len(devices))])
            sums[...] = sum(buf[k] for k in range(1, len(devices) + 1)) + buf[0]

        s.gain_quad[c * 2 + zl] = sums[...]
        yield from total(
            s.gain_quad, c * 2 + zl, [me.core(), me.zl_pair(), me.at(c=1 - c, zl=1 - zl)]
        )
        s.gain_y[y] = sums[...]
        yield from total(s.gain_y, y, [me.step("y", k) for k in (1, 2, 3)])
        s.gain_xz[mine] = sums[...]
        yield from total(
            s.gain_xz,
            mine,
            [me.step("x", k) for k in (1, 2, 3)]
            + [me.at(zh=1 - zh, x=lax.rem(x + k, 4)) for k in range(4)],
        )

    gains = gain_grads()
    step(gains, output, slices[1])


    def input_grad():
        yield from summed
        d = oct_total(me, s.dxn_part, s.dxn_sum)
        t = s.tok[odd, rows, :].astype(F32)
        r = rows_rms(t)
        hat = t * r
        scaled = d * gain_row(0)
        total = s.dh[...]
        total = total + r * (scaled - hat * jnp.mean(scaled * hat, axis=-1, keepdims=True))
        s.dx[rows, :] = total.astype(BF)
        yield from quad_gather(net, me, s.dx)

    rest = input_grad()
    finish(rest, gains, slices[1], slices[0], output, ffn_grads)
    net.drain()


def everything(**args):
    in_specs, in_tree = jax.tree.flatten(input_plan())
    out_shapes, out_tree = jax.tree.flatten(output_plan())
    results = pl.pallas_call(
        kernel,
        out_shape=tuple(out_shapes),
        in_specs=in_specs,
        out_specs=[VM] * len(out_shapes),
        scratch_shapes=jax.tree.leaves(scratch_plan()),
        compiler_params=pltpu.CompilerParams(
            vmem_limit_bytes=VMEM_BYTES, collective_id=1, has_side_effects=True
        ),
        name="everything",
    )(*in_tree.flatten_up_to(args))
    return named(jax.tree.unflatten(out_tree, results))


def finish_kernel(
    out_in, dx_in, att, ffn, sums,
    out, dx, gq, gk, gv, go, gate, up, down, attn_gain, ffn_gain, gain_q, gain_k,
):
    out[...] = out_in[...]
    dx[...] = dx_in[...].astype(F32)
    for zl in range(2):
        even, odd = att[zl, 0].astype(F32), att[zl, 1].astype(F32)
        for parity, block in enumerate((even, odd)):
            start = zl * 512 + parity * 256
            gq[:, start:start + 256] = block[:, 0:256]
            go[:, start:start + 256] = block[:, 384:640]
        even, odd = even[:, 256:384], odd[:, 256:384]
        low = lanes(even.shape) < 64
        gk[:, zl * 128:(zl + 1) * 128] = jnp.where(low, even, pltpu.roll(odd, 64, 1))
        gv[:, zl * 128:(zl + 1) * 128] = jnp.where(low, pltpu.roll(even, 64, 1), odd)
    for m, ref in enumerate((gate, up, down)):
        for k in range(8):
            for c in range(2):
                start = k * 512 + c * 256
                ref[:, start:start + 256] = ffn[m, k, c].astype(F32)
    dp = lax.axis_index("dp")
    row = sums[pl.ds(lax.div(dp, 4), 1), :]
    shift = lax.rem(4 - lax.rem(dp, 4), 4) * 64
    attn_gain[...] = pltpu.roll(row[:, 0:256], shift, 1)[:, 0:64]
    ffn_gain[...] = pltpu.roll(row[:, 256:512], shift, 1)[:, 0:64]
    gain_q[...] = sums[0:1, 512:576]
    gain_k[...] = sums[0:1, 576:640]


def rows_block(*shape):
    n = len(shape)
    return pl.BlockSpec(shape, lambda t: (0,) * (n - 2) + (t, 0))


def whole_block(*shape):
    return pl.BlockSpec(shape, lambda t: (0,) * len(shape))


def finished(r):
    tall = rows_block(64, 2048)
    full, half, wide = (rows_block(32, n) for n in (1024, 256, 4096))
    one = whole_block(1, 64)
    sizes = [(64, 1024), (64, 256), (64, 256), (64, 1024)] + [(64, 4096)] * 3 + [(1, 64)] * 4
    return pl.pallas_call(
        finish_kernel,
        grid=(2,),
        out_shape=(
            jax.ShapeDtypeStruct((128, 2048), BF),
            jax.ShapeDtypeStruct((128, 2048), F32),
        )
        + tuple(jax.ShapeDtypeStruct(size, F32) for size in sizes),
        in_specs=[
            tall, tall, rows_block(2, 2, 32, 640), rows_block(3, 8, 2, 32, 256), whole_block(8, 640),
        ],
        out_specs=[tall, tall, full, half, half, full, wide, wide, wide, one, one, one, one],
        name="finished",
    )(r.out, r.dx, r.att_grads, r.ffn_grads, r.gain_sums)


def rotary_tables():
    position = np.arange(128, dtype=np.float64)[:, None]
    lane = np.arange(128)
    angle = position * THETA ** (-2.0 * (lane % 32) / 64.0)[None, :]
    sign = np.where(lane % 64 < 32, -1.0, 1.0)
    return np.cos(angle).astype(np.float32), (np.sin(angle) * sign).astype(np.float32)


def on_device(
    tokens, gain_attn, w_query, w_key, w_value, gain_query, gain_key, w_out, gain_ffn,
    w_gate, w_up, w_down, cotangent,
):
    cos, sin = (jnp.asarray(t) for t in rotary_tables())
    rows = [jnp.pad(v, (0, 64)).reshape(1, 128) for v in (gain_attn, gain_ffn)]
    rows.append(jnp.concatenate([gain_query, gain_key]).reshape(1, 128))
    small = jnp.pad(jnp.concatenate(rows, axis=0), ((0, 13), (0, 0)))
    r = everything(
        tokens=tokens, cot=cotangent, small=small, cos=cos, sin=sin,
        wq=w_query, wk=w_key, wv=w_value, wo=w_out, wg=w_gate, wu=w_up, wd=w_down,
    )
    out, dx, gq, gk, gv, go, gate, up, down, attn, ffn, gain_q, gain_k = finished(r)
    attn, ffn, gain_q, gain_k = (v.reshape(64) for v in (attn, ffn, gain_q, gain_k))
    return out, dx, attn, gq, gk, gv, gain_q, gain_k, go, ffn, gate, up, down


def solution(mesh):
    return jax.shard_map(
        on_device,
        mesh=mesh,
        in_specs=(
            P("dp", None), P("dp"), P("dp", "head"), P("dp", "head"), P("dp", "head"),
            P(), P(), P("dp", "head"), P("dp"),
            P("dp", "tensor"), P("dp", "tensor"), P("dp", "tensor"), P("dp", None),
        ),
        out_specs=(
            P("dp", None), P("dp", None), P("dp"),
            P("dp", "head"), P("dp", "head"), P("dp", "head"),
            P(), P(), P("dp", "head"), P("dp"),
            P("dp", "tensor"), P("dp", "tensor"), P("dp", "tensor"),
        ),
        check_vma=False,
    )
```

```python
import types

import jax
import jax.numpy as jnp
import numpy as np
from jax import lax
from jax.experimental import pallas as pl
from jax.experimental.pallas import tpu as pltpu
from jax.sharding import PartitionSpec as P

BF = jnp.bfloat16
F32 = jnp.float32
MESH = pl.DeviceIdType.MESH
EPS = 1e-05
THETA = 1000000.0
VMEM_BYTES = 62 << 20
ATT_SLICES = ((0, 384), (384, 256))


def nn(a, b):
    return lax.dot_general(a, b, (((1,), (0,)), ((), ())), preferred_element_type=F32)


def nt(a, b):
    return lax.dot_general(a, b, (((1,), (1,)), ((), ())), preferred_element_type=F32)


def tn(a, b):
    return lax.dot_general(a, b, (((0,), (0,)), ((), ())), preferred_element_type=F32)


class Place:
    def __init__(self):
        dp = lax.axis_index("dp")
        self.c = lax.axis_index("head")
        self.zl = lax.axis_index("tensor")
        self.zh = lax.div(dp, 16)
        self.y = lax.rem(lax.div(dp, 4), 4)
        self.x = lax.rem(dp, 4)
        self.odd = lax.rem(self.y, 2)
        self.z = self.zh * 2 + self.zl

    def at(self, zh=None, y=None, x=None, c=None, zl=None):
        zh = self.zh if zh is None else zh
        y = self.y if y is None else y
        x = self.x if x is None else x
        return (zh * 16 + y * 4 + x, self.c if c is None else c, self.zl if zl is None else zl)

    def step(self, axis, by):
        if axis == "x":
            return self.at(x=lax.rem(self.x + by + 4, 4))
        if axis == "y":
            return self.at(y=lax.rem(self.y + by + 4, 4))
        z = lax.rem(self.z + by + 4, 4)
        return self.at(zh=lax.div(z, 2), zl=lax.rem(z, 2))

    def core(self):
        return self.at(c=1 - self.c)

    def zl_pair(self):
        return self.at(zl=1 - self.zl)

    def y_pair(self):
        return self.at(y=self.y + 1 - 2 * self.odd)

    def zh_pair(self):
        return self.at(zh=1 - self.zh)

    def ring(self, axis):
        return {"x": self.x, "y": self.y, "z": self.z}[axis]


class Copy:
    def __init__(self, copy):
        self.copy = copy
        self.left = True

    def wait_recv(self):
        self.copy.wait_recv()

    def wait_send(self):
        if self.left:
            self.copy.wait_send()
            self.left = False


class Group:
    def __init__(self, sem):
        self.sem = sem

    def wait(self, like):
        pltpu.make_async_copy(like, like, self.sem).wait()


class Net:
    def __init__(self, send_sems, recv_sems):
        self.send_sems = send_sems
        self.recv_sems = recv_sems
        self.slots = [None] * send_sems.shape[0]
        self.sends = 0
        self.groups = 0

    def group(self):
        k = self.groups
        assert k < self.recv_sems.shape[0], k
        self.groups += 1
        return Group(self.recv_sems.at[k])

    def send(self, src, dst, device, group=None):
        slot = self.sends % len(self.slots)
        self.sends += 1
        if self.slots[slot] is not None:
            self.slots[slot].wait_send()
        copy = pltpu.make_async_remote_copy(
            src_ref=src,
            dst_ref=dst,
            send_sem=self.send_sems.at[slot],
            recv_sem=(group or self.group()).sem,
            device_id=device,
            device_id_type=MESH,
        )
        copy.start()
        self.slots[slot] = Copy(copy)
        return self.slots[slot]

    def drain(self):
        for copy in self.slots:
            if copy is not None:
                copy.wait_send()


class Tagged:
    def __init__(self, net):
        self.net = net
        self.copies = []

    def group(self):
        return self.net.group()

    def send(self, src, dst, device, group=None):
        self.copies.append(self.net.send(src, dst, device, group))
        return self.copies[-1]

    def drain(self):
        for copy in self.copies:
            copy.wait_send()


def greet(devices):
    barrier = pltpu.get_barrier_semaphore()
    for device in devices:
        pl.semaphore_signal(barrier, inc=1, device_id=device, device_id_type=MESH)
    pl.semaphore_wait(barrier, len(devices))


def together(*pipelines):
    live = list(pipelines)
    while live:
        for pipe in list(live):
            try:
                next(pipe)
            except StopIteration:
                live.remove(pipe)
        yield


def step(*pipelines):
    for pipe in pipelines:
        next(pipe, None)


def finish(*pipelines):
    for _ in together(*pipelines):
        pass


def local(pairs, sems):
    copies = [pltpu.make_async_copy(s, d, sems.at[i]) for i, (s, d) in enumerate(pairs)]
    for copy in copies:
        copy.start()
    for copy in copies:
        copy.wait()


def add_refs(dst, srcs, rows=32):
    lead, height = dst.shape[:-2], dst.shape[-2]
    rows = min(rows, height)
    per = height // rows
    count = int(np.prod(lead, dtype=np.int64)) * per

    def body(t, carry):
        r = lax.rem(t, per)
        rest = lax.div(t, per)
        index = []
        for size in reversed(lead):
            index.insert(0, lax.rem(rest, size))
            rest = lax.div(rest, size)
        at = tuple(index) + (pl.ds(r * rows, rows), slice(None))
        total = srcs[0][at].astype(F32)
        for src in srcs[1:]:
            total = total + src[at].astype(F32)
        dst[at] = total.astype(dst.dtype)
        return carry

    lax.fori_loop(0, count, body, 0)


def ring_gather(net, place, axis, view, like):
    i = place.ring(axis)
    before, after = lax.rem(i + 3, 4), lax.rem(i + 1, 4)
    up, down = place.step(axis, 1), place.step(axis, -1)
    rest = net.group()
    u0 = net.send(view(i, 0), view(i, 0), up)
    d1 = net.send(view(i, 1), view(i, 1), down)
    net.send(view(i, 1), view(i, 1), up, rest)
    net.send(view(i, 0), view(i, 0), down, rest)
    yield
    u0.wait_recv()
    net.send(view(before, 0), view(before, 0), up, rest)
    d1.wait_recv()
    net.send(view(after, 1), view(after, 1), down, rest)
    yield
    rest.wait(like)


def ring_reduce(net, place, axis, view, far, near, out):
    i = place.ring(axis)
    before, after, across = lax.rem(i + 3, 4), lax.rem(i + 1, 4), lax.rem(i + 2, 4)
    up, down = place.step(axis, 1), place.step(axis, -1)
    fars, nears = net.group(), net.group()
    net.send(view(across, 0), far.at[0], up, fars)
    net.send(view(across, 1), far.at[1], down, fars)
    yield
    net.send(view(after, 1), near.at[1], up, nears)
    net.send(view(before, 0), near.at[2], down, nears)
    yield
    fars.wait(far)
    add_refs(far.at[0], [far.at[0], view(after, 0)])
    net.send(far.at[0], near.at[0], up, nears)
    add_refs(far.at[1], [far.at[1], view(before, 1)])
    net.send(far.at[1], near.at[3], down, nears)
    yield
    nears.wait(near)
    add_refs(out(0), [view(i, 0), near.at[0], near.at[2]])
    add_refs(out(1), [view(i, 1), near.at[1], near.at[3]])


def cross_gather(net, place, one, two, view, likes, late=None, also=None, only=None):
    ring = [lax.rem(place.ring(one) + k, 4) for k in range(4)]
    other = [lax.rem(place.ring(two) + k, 4) for k in range(4)]
    up = {one: place.step(one, 1), two: place.step(two, 1)}
    down = {one: place.step(one, -1), two: place.step(two, -1)}
    corners = []
    last = [net.group(), net.group()]
    finals = [[], []]

    def spread(block, axis, group):
        net.send(block, block, up[axis], group)
        net.send(block, block, down[axis], group)

    def arrived(block):
        if also is not None:
            also(block)
        return block

    def along(axis, part, k, half=None):
        if axis == one:
            return view(part, ring[k], other[0], half)
        return view(part, ring[0], other[k], half)

    def turn(axis, part, k):
        across = two if axis == one else one
        half = 1 if axis == one else 0
        if only is not None and half != only:
            return
        group = net.group()
        spread(along(axis, part, k, half), across, group)
        corners.append((axis, part, k, half, across, group))

    def own(part):
        group = net.group()
        block = view(part, ring[0], other[0], None)
        for axis in (one, two):
            spread(block, axis, group)
        return group

    crosses = [own(0)]
    if late is None:
        crosses.append(own(1))
    yield
    if late is not None:
        late.wait_recv()
        crosses.append(own(1))
        yield
    far = net.group()
    for part in (0, 1):
        crosses[part].wait(likes(None, 4))
        order = (3, 1) if part == 0 else (1, 3)
        for n, k in enumerate(order):
            for axis in (one, two):
                block = arrived(along(axis, part, k))
                if n == 0:
                    net.send(block, block, (up, down)[part][axis], far)
                turn(axis, part, k)
        yield
    far.wait(likes(None, 4))
    for part in (0, 1):
        for axis in (one, two):
            arrived(along(axis, part, 2))
            turn(axis, part, 2)
    yield
    for n, (axis, part, k, half, across, group) in enumerate(corners):
        group.wait(likes(half, 2))
        for which, by in ((0, 3), (1, 1)):
            if axis == one:
                block = view(part, ring[k], other[by], half)
                final = view(part, ring[k], other[2], half)
            else:
                block = view(part, ring[by], other[k], half)
                final = view(part, ring[2], other[k], half)
            arrived(block)
            if which == part:
                net.send(block, block, (up, down)[part][across], last[half])
                finals[half].append(final)
        if n % 4 == 3:
            yield
    for half in (0, 1):
        if finals[half]:
            last[half].wait(likes(half, len(finals[half])))
            for final in finals[half]:
                arrived(final)


def order_reduce(net, place, one, two, view, s, out, other_out=None):
    ring = [lax.rem(place.ring(one) + k, 4) for k in range(4)]
    other = [lax.rem(place.ring(two) + k, 4) for k in range(4)]
    up, down = place.step(one, 1), place.step(one, -1)
    order = (2, 1, 3, 0)
    fars = {k: net.group() for k in order}
    nears = {k: net.group() for k in order}
    others = net.group()
    for k in order:
        net.send(view(0, ring[2], other[k]), s.far.at[k, 0], up, fars[k])
        net.send(view(1, ring[2], other[k]), s.far.at[k, 1], down, fars[k])
    for k in order:
        net.send(view(1, ring[1], other[k]), s.near.at[k, 1], up, nears[k])
        net.send(view(0, ring[3], other[k]), s.near.at[k, 2], down, nears[k])
    yield
    for k in order:
        fars[k].wait(s.far.at[k])
        add_refs(s.far.at[k, 0], [s.far.at[k, 0], view(0, ring[1], other[k])])
        net.send(s.far.at[k, 0], s.near.at[k, 0], up, nears[k])
        add_refs(s.far.at[k, 1], [s.far.at[k, 1], view(1, ring[3], other[k])])
        net.send(s.far.at[k, 1], s.near.at[k, 3], down, nears[k])
        if k != 1:
            yield
    for k in order:
        nears[k].wait(s.near.at[k])
        for p in (0, 1):
            add_refs(
                s.mid.at[k, p],
                [view(p, ring[0], other[k]), s.near.at[k, p], s.near.at[k, 2 + p]],
            )
        if k:
            net.send(s.mid.at[k], s.last.at[k - 1], place.step(two, k), others)
        if k != 1:
            yield
    others.wait(s.last)
    for p in (0, 1):
        if other_out is None:
            add_refs(out(p), [s.mid.at[0, p]] + [s.last.at[k, p] for k in range(3)])
        else:
            add_refs(out(p), [s.mid.at[0, p], s.last.at[1, p]])
            add_refs(other_out(p), [s.last.at[0, p], s.last.at[2, p]])


def order_buffers(rows, columns):
    return dict(
        far=pltpu.VMEM((4, 2, rows, columns), BF),
        near=pltpu.VMEM((4, 4, rows, columns), BF),
        mid=pltpu.VMEM((4, 2, rows, columns), BF),
        last=pltpu.VMEM((3, 2, rows, columns), BF),
    )


def torus_gather(net, place, buf, only=None):
    c = place.c
    other = place.core()
    swaps = net.group()

    def also(block):
        net.send(block, block, other, swaps)

    def rows(half):
        return pl.ds(0, 32) if half is None or only is not None else pl.ds(half * 16, 16)

    def view(part, i, j, half):
        return buf.at[i, j, c, rows(half), pl.ds(part * 1024, 1024)]

    def likes(half, n):
        return buf.at[pl.ds(0, 2), pl.ds(0, n // 2), 0, rows(half), pl.ds(0, 1024)]

    also(buf.at[place.z, place.x, c])
    yield from cross_gather(net, place, "z", "x", view, likes, also=also, only=only)
    yield
    swaps.wait(buf.at[:, :, 1 - c])


def torus_buffers():
    return dict(
        both=pltpu.VMEM((4, 4, 32, 2048), BF),
        halves=[order_buffers(16, 1024), order_buffers(16, 1024)],
        total=pltpu.VMEM((32, 2048), F32),
    )


def core_sum(place, src, swap, s, k):
    swap.wait_recv()
    add_refs(s.both.at[k], [s.both.at[k], src.at[k, :, place.c]])


def torus_reduce(net, place, s, orders):
    def half(k):
        def at(part):
            return pl.ds(k * 16, 16), pl.ds(part * 1024, 1024)

        def view(p, i, j):
            zi, xi = (i, j) if orders[k] == "z" else (j, i)
            return s.both.at[(zi, xi) + at(p)]

        second = "x" if orders[k] == "z" else "z"
        return order_reduce(
            net, place, orders[k], second, view, s.halves[k], lambda p: s.total.at[at(p)]
        )

    yield from together(half(0), half(1))


def quad_gather(net, place, buf):
    c, zl = place.c, place.zl
    own = buf.at[pl.ds(c * 64 + zl * 32, 32)]
    one = net.send(own, own, place.zl_pair())
    yield
    one.wait_recv()
    half = buf.at[pl.ds(c * 64, 64)]
    two = net.send(half, half, place.core())
    yield
    two.wait_recv()


def oct_reduce(net, place, src, b):
    c, zl, q = place.c, place.zl, place.odd
    theirs = pl.ds((1 - c) * 64, 64)
    one = net.send(src.at[1 - q, theirs], b.core.at[1 - q], place.core())
    yield
    one.wait_recv()
    b.for_y[...] = (
        src[1 - q, pl.ds(c * 64, 64), :].astype(F32) + b.core[1 - q].astype(F32)
    ).astype(BF)
    far, near = pl.ds((1 - zl) * 32, 32), pl.ds(zl * 32, 32)
    two = [net.send(b.for_y.at[r], b.y.at[r], place.y_pair()) for r in (far, near)]
    yield
    one = net.send(src.at[q, theirs], b.core.at[q], place.core())
    yield
    one.wait_recv()
    two[0].wait_recv()
    theirs = src[q, pl.ds(c * 64 + (1 - zl) * 32, 32), :].astype(F32)
    theirs = theirs + b.core[q, far, :].astype(F32) + b.y[far, :].astype(F32)
    b.for_zl[...] = theirs.astype(BF)
    three = net.send(b.for_zl, b.zl, place.zl_pair())
    yield
    two[1].wait_recv()
    three.wait_recv()


def oct_total(place, src, b):
    c, zl, q = place.c, place.zl, place.odd
    near = pl.ds(zl * 32, 32)
    total = src[q, pl.ds(c * 64 + zl * 32, 32), :].astype(F32) + b.core[q, near, :].astype(F32)
    return total + b.y[near, :].astype(F32) + b.zl[...].astype(F32)


def oct_buffers():
    return dict(
        core=pltpu.VMEM((2, 64, 2048), BF),
        for_y=pltpu.VMEM((64, 2048), BF),
        y=pltpu.VMEM((64, 2048), BF),
        for_zl=pltpu.VMEM((32, 2048), BF),
        zl=pltpu.VMEM((32, 2048), BF),
    )


def quad_gather(net, place, buf):
    c, zl = place.c, place.zl
    own = buf.at[pl.ds(c * 64 + zl * 32, 32)]
    one = net.send(own, own, place.zl_pair())
    yield
    one.wait_recv()
    half = buf.at[pl.ds(c * 64, 64)]
    two = net.send(half, half, place.core())
    yield
    two.wait_recv()


def oct_gather(net, place, buf):
    c, zl, q = place.c, place.zl, place.odd
    own = buf.at[q, pl.ds(c * 64 + zl * 32, 32)]
    from_zl = net.send(own, own, place.zl_pair())
    from_y = [net.send(own, own, place.y_pair())]
    yield
    from_zl.wait_recv()
    other = buf.at[q, pl.ds(c * 64 + (1 - zl) * 32, 32)]
    from_y.append(net.send(other, other, place.y_pair()))
    half = buf.at[q, pl.ds(c * 64, 64)]
    from_core = net.send(half, half, place.core())
    yield
    from_core.wait_recv()
    yield
    for copy in from_y:
        copy.wait_recv()
    half = buf.at[1 - q, pl.ds(c * 64, 64)]
    from_core = net.send(half, half, place.core())
    yield
    from_core.wait_recv()


def sem_scratch(n):
    return [pltpu.SemaphoreType.DMA((n,)), pltpu.SemaphoreType.DMA((n,))]


ANY = pl.BlockSpec(memory_space=pl.ANY)
VM = pl.BlockSpec(memory_space=pltpu.VMEM)


def lanes(shape):
    return lax.broadcasted_iota(jnp.int32, shape, len(shape) - 1)


def partner(v):
    n = v.shape[-1]
    low = lax.rem(lanes(v.shape), 64) < 32
    return jnp.where(low, pltpu.roll(v, n - 32, 1), pltpu.roll(v, 32, 1))


def head_mean(v):
    n = v.shape[-1]
    r = lax.broadcasted_iota(jnp.int32, (n, n), 0)
    same = lax.div(r, 64) == lax.div(lanes((n, n)), 64)
    return lax.dot_general(
        v, jnp.where(same, 1.0 / 64.0, 0.0), (((1,), (0,)), ((), ())),
        precision=lax.Precision.HIGHEST, preferred_element_type=F32,
    )


def half_of(v, which):
    upper = lanes(v.shape) >= 64
    keep = upper if which else jnp.logical_not(upper)
    return jnp.where(keep, v, jnp.zeros_like(v))


def swap_halves(v):
    return pltpu.roll(v.astype(F32), 64, 1).astype(v.dtype)


def rows_rms(v):
    return lax.rsqrt(jnp.mean(v * v, axis=-1, keepdims=True) + EPS)


N_SENDS = 48
N_GROUPS = 149
N_LOCAL = 17


def input_plan():
    return dict(
        tokens=ANY, cot=ANY, small=ANY, cos=ANY, sin=ANY,
        wq=ANY, wk=ANY, wv=ANY, wo=ANY, wg=ANY, wu=ANY, wd=ANY,
    )


def output_plan():
    return dict(
        out=jax.ShapeDtypeStruct((128, 2048), BF),
        dx=jax.ShapeDtypeStruct((128, 2048), BF),
        att_grads=jax.ShapeDtypeStruct((2, 2, 64, 640), BF),
        ffn_grads=jax.ShapeDtypeStruct((3, 8, 2, 64, 256), BF),
        gain_sums=jax.ShapeDtypeStruct((8, 640), F32),
    )


def scratch_plan():
    return dict(
        tok=pltpu.VMEM((2, 128, 2048), BF),
        kv_in=pltpu.VMEM((2, 64, 128), BF),
        shard=pltpu.VMEM((2, 2, 64, 640), BF),
        small_in=pltpu.VMEM((16, 128), BF),
        cos_in=pltpu.VMEM((128, 128), F32),
        sin_in=pltpu.VMEM((128, 128), F32),
        att=pltpu.VMEM((2, 4, 4, 64, 640), BF),
        gains=pltpu.VMEM((2, 4, 4, 16, 128), BF),
        ffn=pltpu.VMEM((3, 2, 4, 4, 64, 256), BF),
        cots=pltpu.VMEM((4, 4, 2, 32, 2048), BF),
        xn2=pltpu.VMEM((4, 4, 2, 32, 2048), BF),
        xn=pltpu.VMEM((256, 2048), BF),
        z=pltpu.VMEM((256, 384), F32),
        qk=pltpu.VMEM((256, 384), BF),
        p=pltpu.VMEM((8, 128, 128), F32),
        o=pltpu.VMEM((256, 256), BF),
        branch=pltpu.VMEM((2, 128, 2048), BF),
        branch_sum=oct_buffers(),
        dxn_sum=oct_buffers(),
        hidden=pltpu.VMEM((32, 2048), F32),
        da=pltpu.VMEM((4, 256, 256), F32),
        ab=pltpu.VMEM((4, 256, 256), BF),
        dg=pltpu.VMEM((4, 256, 256), BF),
        du=pltpu.VMEM((4, 256, 256), BF),
        dxn2_part=pltpu.VMEM((4, 4, 2, 32, 2048), BF),
        ffn_part=pltpu.VMEM((3, 2, 4, 4, 64, 256), BF),
        ffn_far=pltpu.VMEM((4, 2, 3, 64, 256), BF),
        ffn_near=pltpu.VMEM((4, 4, 3, 64, 256), BF),
        ffn_mid=pltpu.VMEM((4, 2, 3, 64, 256), BF),
        dh=pltpu.VMEM((32, 2048), F32),
        dhb=pltpu.VMEM((2, 128, 2048), BF),
        ffn_gain_grad=pltpu.VMEM((1, 2048), F32),
        d_heads=pltpu.VMEM((256, 384), F32),
        att_part=pltpu.VMEM((2, 4, 4, 64, 640), BF),
        dxn_part=pltpu.VMEM((2, 128, 2048), BF),
        both_z=pltpu.VMEM((2, 2, 64, 640), BF),
        from_z=pltpu.VMEM((2, 2, 2, 64, 640), BF),
        gain_quad=pltpu.VMEM((4, 8, 640), F32),
        gain_y=pltpu.VMEM((4, 8, 640), F32),
        gain_xz=pltpu.VMEM((8, 8, 640), F32),
        dxn2_sum=torus_buffers(),
        out_sum=torus_buffers(),
        slices=[order_buffers(64, n) for _, n in ATT_SLICES],
        send_sems=pltpu.SemaphoreType.DMA((N_SENDS,)),
        recv_sems=pltpu.SemaphoreType.DMA((N_GROUPS,)),
        sems=pltpu.SemaphoreType.DMA((N_LOCAL,)),
    )


def named(plan):
    if isinstance(plan, dict):
        return types.SimpleNamespace(**{k: named(v) for k, v in plan.items()})
    if isinstance(plan, list):
        return [named(v) for v in plan]
    return plan


def kernel(*refs):
    s = types.SimpleNamespace()
    for plan in (input_plan(), output_plan(), scratch_plan()):
        leaves, tree = jax.tree.flatten(plan)
        part = jax.tree.unflatten(tree, refs[: len(leaves)])
        refs = refs[len(leaves):]
        vars(s).update(vars(named(part)))
    send_sems, recv_sems, sems = s.send_sems, s.recv_sems, s.sems
    me = Place()
    zh, y, x, c, zl, z, odd = me.zh, me.y, me.x, me.c, me.zl, me.z, me.odd
    net = Net(send_sems, recv_sems)
    att, ffn = s.att, s.ffn
    rows = pl.ds(c * 64 + zl * 32, 32)


    def piece(k):
        return pl.ds(pl.multiple_of(k * 512 + c * 256, 256), 256)

    def load(pairs):
        started = []
        for src, dst in pairs:
            started.append(pltpu.make_async_copy(src, dst, sems.at[len(loads)]))
            loads.append(started[-1])
            started[-1].start()
        return started

    loads = []
    narrow = pl.ds(pl.multiple_of(zl * 128, 128), 128)
    mine = zh * 4 + x
    att_copies = load([(w.at[:, narrow], s.kv_in.at[k]) for k, w in enumerate((s.wk, s.wv))])
    for parity in range(2):
        wide = pl.ds(pl.multiple_of(zl * 512 + parity * 256, 256), 256)
        block = s.shard.at[0, parity]
        att_copies += load(
            [
                (s.wq.at[:, wide], block.at[:, pl.ds(0, 256)]),
                (s.wo.at[:, wide], block.at[:, pl.ds(384, 256)]),
            ]
        )
    (small_copy,) = load([(s.small, s.small_in)])
    (cots_copy,) = load([(s.cot.at[rows], s.cots.at[z, x, c])])
    ffn_copies = load(
        [(w.at[:, piece(mine)], ffn.at[m, zh, y, x]) for m, w in enumerate((s.wg, s.wu, s.wd))]
    )
    (tok_copy,) = load([(s.tokens, s.tok.at[odd])])
    other_copies = load([(s.cos, s.cos_in), (s.sin, s.sin_in)])
    greet(
        [me.step("x", 1), me.step("x", 2), me.step("x", -1)]
        + [me.step("y", 1), me.step("y", 2), me.step("y", -1)]
        + [me.step("z", 1), me.step("z", 2), me.step("z", -1)]
        + [me.core(), me.at(c=1 - c, zl=1 - zl)]
        + [me.at(zh=1 - zh, x=lax.rem(x + k, 4)) for k in (1, 2, 3)]
    )

    def gather_attention():
        shard = s.shard

        def plane(p):
            return 1 - zh if p else zh

        def blocks(n):
            return att.at[0, 0, pl.ds(0, n)]

        rings = {}
        last = net.group()

        def set_off(p, k):
            block = att.at[plane(p), lax.rem(y + k, 4), x]
            rings[p, k] = net.group()
            net.send(block, block, me.step("x", 1), rings[p, k])
            net.send(block, block, me.step("x", -1), rings[p, k])

        def along_y(p):
            group = net.group()
            for k in (1, 3, 2):
                parity = odd if k == 2 else 1 - odd
                dst = att.at[plane(p), y, x]
                net.send(shard.at[p, parity], dst, me.step("y", k), group)
            s.att[plane(p), y, x] = shard[p, odd]
            set_off(p, 0)
            return group

        swap = net.send(shard.at[0], shard.at[1], me.zh_pair())
        groups = [along_y(0)]
        yield
        swap.wait_recv()
        groups.append(along_y(1))
        yield
        for p in (0, 1):
            groups[p].wait(blocks(3))
            for k in (1, 3, 2):
                set_off(p, k)
            yield
        for k in (0, 1, 3, 2):
            for p in (0, 1):
                rings[p, k].wait(blocks(2))
                by = 1 if p else 3
                block = att.at[plane(p), lax.rem(y + k, 4), lax.rem(x + by, 4)]
                net.send(block, block, me.step("x", -1 if p else 1), last)
            yield
        last.wait(att.at[:, 0])

    def gather_tokens():
        half = s.tok.at[odd, pl.ds(c * 64, 64)]
        copy = net.send(half, half, me.y_pair())
        yield
        copy.wait_recv()
        half = s.tok.at[1 - odd, pl.ds(c * 64, 64)]
        copy = net.send(half, half, me.core())
        yield
        copy.wait_recv()

    def gather_ffn():
        arrivals = [net.group(), net.group()]
        for dz in (0, 1):
            for dx in range(4):
                if dz == 0 and dx == 0:
                    continue
                tx = lax.rem(x + dx, 4)
                tz = 1 - zh if dz else zh
                for m, w in enumerate((s.wg, s.wu, s.wd)):
                    net.send(
                        w.at[:, piece(tz * 4 + tx)],
                        ffn.at[m, zh, y, x],
                        me.at(zh=tz, x=tx),
                        arrivals[dz],
                    )
        yield
        arrivals[0].wait(s.ffn_part.at[:, 0, 0, pl.ds(0, 3)])
        arrivals[1].wait(s.ffn_part.at[:, 0, 0])
        for copy in ffn_copies:
            copy.wait()
        yield from ring_gather(
            net, me, "y", lambda i, p: ffn.at[:, p, i], s.ffn_part.at[:, 0]
        )

    def gather_gains():
        own_gain = s.gains.at[zh, y, x]
        near, far = net.group(), net.group()
        for k in range(4):
            device = lax.rem(x + k, 4)
            if k:
                net.send(own_gain, own_gain, me.at(x=device), near)
            net.send(own_gain, own_gain, me.at(zh=1 - zh, x=device), far)
        yield
        near.wait(s.gains.at[0, 0, pl.ds(0, 3)])
        far.wait(s.gains.at[0, 0])
        row = s.gains.at[:, y]
        group = net.group()
        for k in (1, -1, 2):
            net.send(row, row, me.step("y", k), group)
        yield
        group.wait(s.gains.at[:, pl.ds(0, 3)])

    def gain_row(k):
        blocks = []
        for pair in range(16):
            a, b = 2 * pair, 2 * pair + 1
            total = None
            for d in (a, b):
                block = s.gains[d // 16, d // 4 % 4, d % 4].astype(F32)
                total = block if total is None else total + block
            blocks.append(total[k:k + 1, :])
        return jnp.concatenate(blocks, axis=1)

    for copy in att_copies:
        copy.wait()
    key, value = s.kv_in[0], s.kv_in[1]
    low_half = lanes((64, 128)) < 64
    s.shard[0, 0, :, 256:384] = jnp.where(low_half, key, swap_halves(value))
    s.shard[0, 1, :, 256:384] = jnp.where(low_half, swap_halves(key), value)
    attention = gather_attention()
    gains = gather_gains()
    weights = gather_ffn()
    cots = torus_gather(net, me, s.cots, only=0)
    pair_tokens = gather_tokens()
    step(attention)
    small_copy.wait()
    small = s.small_in[...].astype(F32)
    s.gains[zh, y, x] = jnp.where(lax.rem(x, 2) == 1, pltpu.roll(small, 64, 1), small).astype(BF)
    step(gains, weights, attention, attention, gains, attention)
    tok_copy.wait()
    step(pair_tokens, attention)
    finish(gains)
    for copy in other_copies:
        copy.wait()
    step(pair_tokens, attention, weights)
    cots_copy.wait()
    step(attention, cots)
    finish(pair_tokens)
    t = s.tok[...].reshape(256, 2048).astype(F32)
    s.xn[...] = (t * rows_rms(t) * gain_row(0)).astype(BF)
    step(attention, cots)
    finish(attention)


    step(cots)
    raw = nn(s.xn[...], att[:, :, :, :, 0:384].reshape(2048, 384))
    s.z[...] = raw
    step(cots)
    both_gains = small[2:3, :] + pltpu.roll(small[3:4, :], 64, 1)
    turned = pltpu.roll(both_gains, 64, 1)
    low = lanes((1, 128)) < 64
    gain_q = jnp.where(low, both_gains, turned)
    head_gain = jnp.concatenate([gain_q, gain_q, turned], axis=1)
    cos, sin = (
        jnp.concatenate([jnp.concatenate([ref[...]] * 3, axis=1)] * 2, axis=0)
        for ref in (s.cos_in, s.sin_in)
    )
    is_value = lanes((256, 384)) >= 320
    n = raw * lax.rsqrt(head_mean(raw * raw) + EPS) * head_gain
    s.qk[...] = jnp.where(is_value, raw, n * cos + partner(n) * sin).astype(BF)
    step(cots)
    causal = lax.broadcasted_iota(jnp.int32, (128, 128), 0) >= lanes((128, 128))

    def attend(q):
        at = pl.ds(pl.multiple_of(q * 128, 128), 128)
        kv = s.qk[at, 256:384]
        sides = (kv, swap_halves(kv))
        for block in range(2):
            cols = slice(block * 128, (block + 1) * 128)
            out = None
            for side in range(2):
                query = half_of(s.qk[at, cols], side)
                score = jnp.where(causal, nt(query, sides[side]) * 0.125, -1e30)
                e = jnp.exp(score - jnp.max(score, axis=-1, keepdims=True))
                p = e / jnp.sum(e, axis=-1, keepdims=True)
                s.p[q * 4 + 2 * block + side] = p
                part = nn(p.astype(BF), half_of(sides[1 - side], side))
                out = part if out is None else out + part
            s.o[at, cols] = out.astype(BF)

    def project(q):
        at = pl.ds(pl.multiple_of(q * 128, 128), 128)
        branch = nt(s.o[at, :], att[:, :, :, :, 384:640].reshape(2048, 256))
        s.branch[q] = branch.astype(BF)

    attend(1 - odd)
    project(1 - odd)
    summed = oct_reduce(net, me, s.branch, s.branch_sum)
    step(summed)
    attend(odd)
    step(summed)
    project(odd)
    step(summed, cots, weights)
    finish(summed)
    hidden = s.tok[odd, rows, :].astype(F32)
    hidden = hidden + oct_total(me, s.branch, s.branch_sum)
    s.hidden[...] = hidden
    s.xn2[z, x, c] = (hidden * rows_rms(hidden) * gain_row(1)).astype(BF)
    normed_net = Tagged(net)
    normed = torus_gather(normed_net, me, s.xn2)
    step(normed, normed, normed)
    finish(cots, weights)
    step(normed, normed)


    def weight(m):
        return ffn[m].reshape(2048, 256)

    for k in range(4):
        s.da[k] = nn(s.cots[k].reshape(256, 2048), weight(2))
        step(normed)
    finish(normed)
    swaps = []
    for k in range(4):
        xk = s.xn2[k].reshape(256, 2048)
        g, u, da = nn(xk, weight(0)), nn(xk, weight(1)), s.da[k]
        sigma = jax.nn.sigmoid(g)
        swish = g * sigma
        s.ab[k] = (swish * u).astype(BF)
        dg = (da * u * sigma * (1.0 + g * (1.0 - sigma))).astype(BF)
        du = (da * swish).astype(BF)
        s.dg[k] = dg
        s.du[k] = du
        part = (nt(dg, weight(0)) + nt(du, weight(1))).astype(BF)
        s.dxn2_part[k] = part.reshape(4, 2, 32, 2048)
        swaps.append(
            net.send(s.dxn2_part.at[k, :, 1 - c], s.dxn2_sum.both.at[k], me.core())
        )
        if k:
            core_sum(me, s.dxn2_part, swaps[k - 1], s.dxn2_sum, k - 1)


    dxn2 = torus_reduce(net, me, s.dxn2_sum, "zx")

    def weight_grads(k):
        yk = lax.rem(y + k, 4)

        def one(p, carry):
            cols = pl.ds(pl.multiple_of((p * 4 + yk) * 256, 256), 256)
            xd = s.xn2[:, :, :, :, cols].reshape(1024, 256)
            dyd = s.cots[:, :, :, :, cols].reshape(1024, 256)
            for m, left, right in ((0, xd, s.dg), (1, xd, s.du), (2, dyd, s.ab)):
                grad = tn(left, right[...].reshape(1024, 256))
                s.ffn_part[m, p, yk] = grad.astype(BF).reshape(4, 64, 256)
            return carry

        lax.fori_loop(0, 2, one, 0)

    def reduce_ffn_grads():
        part, grads = s.ffn_part, s.ffn_grads
        arrivals = [net.group(), net.group()]
        dst = grads.at[:, mine, c]
        keep = pltpu.make_async_copy(s.ffn_mid.at[0, zh], dst, sems.at[N_LOCAL - 1])

        def block(k):
            xk = lax.rem(x + k, 4)
            far, near, mid = (ref.at[k] for ref in (s.ffn_far, s.ffn_near, s.ffn_mid))
            yield from ring_reduce(
                net, me, "y", lambda i, p: part.at[:, p, i, xk], far, near, lambda p: mid.at[p]
            )
            if k:
                net.send(mid.at[zh], dst, me.at(x=xk), arrivals[0])
            else:
                keep.start()
            net.send(mid.at[1 - zh], dst, me.at(zh=1 - zh, x=xk), arrivals[1])

        yield from together(*[block(k) for k in (2, 1, 3, 0)])
        keep.wait()
        arrivals[0].wait(s.ffn_part.at[:, 0, 0, pl.ds(0, 3)])
        arrivals[1].wait(s.ffn_part.at[:, 0, 0])
        swap = net.send(grads.at[:, :, c], grads.at[:, :, c], me.core())
        yield
        swap.wait_recv()

    ffn_grads = reduce_ffn_grads()
    weight_grads(2)
    step(ffn_grads)
    core_sum(me, s.dxn2_part, swaps[3], s.dxn2_sum, 3)
    step(dxn2)
    weight_grads(1)
    weight_grads(3)
    step(ffn_grads, dxn2, dxn2)
    weight_grads(0)
    step(dxn2)
    swaps = []
    normed_net.drain()
    for k in range(4):
        part = nt(s.ab[k], weight(2)).astype(BF)
        s.xn2[k] = part.reshape(4, 2, 32, 2048)
        swaps.append(net.send(s.xn2.at[k, :, 1 - c], s.out_sum.both.at[k], me.core()))
        if k % 2 == 1:
            step(dxn2)
    finish(dxn2)
    hidden = s.hidden[...]
    r = rows_rms(hidden)
    hat = hidden * r
    d = s.dxn2_sum.total[...]
    s.ffn_gain_grad[...] = jnp.sum(d * hat, axis=0, keepdims=True)
    scaled = d * gain_row(1)
    dh = s.cots[z, x, c].astype(F32)
    dh = dh + r * (scaled - hat * jnp.mean(scaled * hat, axis=-1, keepdims=True))
    s.dh[...] = dh
    s.dhb[odd, rows, :] = dh.astype(BF)
    spread = oct_gather(net, me, s.dhb)
    step(spread)

    def finish_output():
        for k in range(4):
            core_sum(me, s.xn2, swaps[k], s.out_sum, k)
        yield from torus_reduce(net, me, s.out_sum, "zz")
        s.out[rows, :] = (s.hidden[...] + s.out_sum.total[...]).astype(BF)
        yield from quad_gather(net, me, s.out)

    output = finish_output()
    step(spread, output, spread)


    def reduce_att_grads(k):
        start, width = ATT_SLICES[k]
        cols = pl.ds(start, width)
        both_z = s.both_z
        yield from order_reduce(
            net, me, "x", "y", lambda p, i, j: s.att_part.at[p, j, i, :, cols], s.slices[k],
            lambda p: both_z.at[p, odd, :, cols], lambda p: both_z.at[p, 1 - odd, :, cols],
        )
        arrivals = net.group()
        mine_z = both_z.at[zh, :, :, cols]
        theirs = both_z.at[1 - zh, :, :, cols]
        dst = s.from_z.at[zl, 1, :, :, cols]
        net.send(theirs, dst, me.at(zh=1 - zh), arrivals)
        net.send(theirs, dst, me.at(zh=1 - zh, zl=1 - zl), arrivals)
        net.send(mine_z, s.from_z.at[zl, 0, :, :, cols], me.at(zl=1 - zl), arrivals)
        yield
        arrivals.wait(s.slices[k].last)
        add_refs(s.att_grads.at[zl, :, :, cols], [mine_z, s.from_z.at[zl, 1, :, :, cols]])
        add_refs(
            s.att_grads.at[1 - zl, :, :, cols],
            [s.from_z.at[1 - zl, 0, :, :, cols], s.from_z.at[1 - zl, 1, :, :, cols]],
        )

    def attend_back(q):
        at = pl.ds(pl.multiple_of(q * 128, 128), 128)
        do = nn(s.dhb[q], att[:, :, :, :, 384:640].reshape(2048, 256)).astype(BF)
        kv = s.qk[at, 256:384]
        sides = (kv, swap_halves(kv))
        dk = [jnp.zeros((128, 128), F32)] * 2
        dv = [jnp.zeros((128, 128), F32)] * 2
        for block in range(2):
            cols = slice(block * 128, (block + 1) * 128)
            dq = None
            for side in range(2):
                p = s.p[q * 4 + 2 * block + side]
                dob = half_of(do[:, cols], side)
                query = half_of(s.qk[at, cols], side)
                dp = nt(dob, sides[1 - side])
                dv[side] = dv[side] + tn(p.astype(BF), dob)
                ds = (p * (dp - jnp.sum(p * dp, axis=-1, keepdims=True))).astype(BF)
                part = nn(ds, half_of(sides[side], side))
                dq = part if dq is None else dq + part
                dk[side] = dk[side] + tn(ds, query)
            s.d_heads[at, cols] = dq * 0.125
        dkey = (dk[0] + pltpu.roll(dk[1], 64, 1)) * 0.125
        s.d_heads[at, 256:384] = dkey + dv[1] + pltpu.roll(dv[0], 64, 1)

    attend_back(odd)
    step(spread, ffn_grads)
    finish(spread)
    grad = tn(s.dhb[...].reshape(256, 2048), s.o[...]).astype(BF)
    s.att_part[:, :, :, :, 384:640] = grad.reshape(2, 4, 4, 64, 256)
    slices = [reduce_att_grads(k) for k in range(2)]
    step(slices[1], output)
    attend_back(1 - odd)
    step(output, slices[1])
    dout = s.d_heads[...]
    dn = dout * cos - partner(dout) * sin
    z_raw = s.z[...]
    r = lax.rsqrt(head_mean(z_raw * z_raw) + EPS)
    zhat = z_raw * r
    dgain = jnp.sum(dn * zhat, axis=0, keepdims=True)
    q_pairs = dgain[:, 0:128] + dgain[:, 128:256]
    q_pairs = q_pairs + pltpu.roll(q_pairs, 64, 1)
    k_pairs = pltpu.roll(dgain[:, 256:384], 64, 1)
    dz = dn * head_gain
    dz = r * (dz - zhat * head_mean(dz * zhat))
    low_grads = jnp.where(is_value, dout, dz).astype(BF)
    step(slices[1], ffn_grads)
    grad = tn(s.xn[...], low_grads).astype(BF)
    s.att_part[:, :, :, :, 0:384] = grad.reshape(2, 4, 4, 64, 384)
    step(slices[0], slices[1])
    gain_grad = jnp.zeros((1, 2048), F32)
    for q in range(2):
        at = slice(q * 128, (q + 1) * 128)
        back = nt(low_grads[at], att[:, :, :, :, 0:384].reshape(2048, 384))
        s.dxn_part[q] = back.astype(BF)
        t = s.tok[q].astype(F32)
        gain_grad = gain_grad + jnp.sum(back * (t * rows_rms(t)), axis=0, keepdims=True)
    summed = oct_reduce(net, me, s.dxn_part, s.dxn_sum)
    step(summed)

    def gain_grads():
        sums = s.gain_sums
        for k in range(8):
            part = slice(k * 256, (k + 1) * 256)
            sums[k:k + 1, 0:256] = gain_grad[:, part]
            sums[k:k + 1, 256:512] = s.ffn_gain_grad[:, part]
        row = lax.broadcasted_iota(jnp.int32, (8, 128), 0)
        head_grad = jnp.where(lanes((8, 128)) < 64, q_pairs, k_pairs)
        sums[:, 512:640] = jnp.where(row == 0, head_grad, 0.0)

        def total(buf, own, devices):
            group = net.group()
            for device in devices:
                net.send(buf.at[own], buf.at[own], device, group)
            yield
            group.wait(buf.at[pl.ds(0, len(devices))])
            sums[...] = sum(buf[k] for k in range(1, len(devices) + 1)) + buf[0]

        s.gain_quad[c * 2 + zl] = sums[...]
        yield from total(
            s.gain_quad, c * 2 + zl, [me.core(), me.zl_pair(), me.at(c=1 - c, zl=1 - zl)]
        )
        s.gain_y[y] = sums[...]
        yield from total(s.gain_y, y, [me.step("y", k) for k in (1, 2, 3)])
        s.gain_xz[mine] = sums[...]
        yield from total(
            s.gain_xz,
            mine,
            [me.step("x", k) for k in (1, 2, 3)]
            + [me.at(zh=1 - zh, x=lax.rem(x + k, 4)) for k in range(4)],
        )

    gains = gain_grads()
    step(gains, output, slices[1])


    def input_grad():
        yield from summed
        d = oct_total(me, s.dxn_part, s.dxn_sum)
        t = s.tok[odd, rows, :].astype(F32)
        r = rows_rms(t)
        hat = t * r
        scaled = d * gain_row(0)
        total = s.dh[...]
        total = total + r * (scaled - hat * jnp.mean(scaled * hat, axis=-1, keepdims=True))
        s.dx[rows, :] = total.astype(BF)
        yield from quad_gather(net, me, s.dx)

    rest = input_grad()
    finish(rest, gains, slices[1], slices[0], output, ffn_grads)
    net.drain()


def everything(**args):
    in_specs, in_tree = jax.tree.flatten(input_plan())
    out_shapes, out_tree = jax.tree.flatten(output_plan())
    results = pl.pallas_call(
        kernel,
        out_shape=tuple(out_shapes),
        in_specs=in_specs,
        out_specs=[VM] * len(out_shapes),
        scratch_shapes=jax.tree.leaves(scratch_plan()),
        compiler_params=pltpu.CompilerParams(
            vmem_limit_bytes=VMEM_BYTES, collective_id=1, has_side_effects=True
        ),
        name="everything",
    )(*in_tree.flatten_up_to(args))
    return named(jax.tree.unflatten(out_tree, results))


def finish_kernel(
    out_in, dx_in, att, ffn, sums,
    out, dx, gq, gk, gv, go, gate, up, down, attn_gain, ffn_gain, gain_q, gain_k,
):
    out[...] = out_in[...]
    dx[...] = dx_in[...].astype(F32)
    for zl in range(2):
        even, odd = att[zl, 0].astype(F32), att[zl, 1].astype(F32)
        for parity, block in enumerate((even, odd)):
            start = zl * 512 + parity * 256
            gq[:, start:start + 256] = block[:, 0:256]
            go[:, start:start + 256] = block[:, 384:640]
        even, odd = even[:, 256:384], odd[:, 256:384]
        low = lanes(even.shape) < 64
        gk[:, zl * 128:(zl + 1) * 128] = jnp.where(low, even, pltpu.roll(odd, 64, 1))
        gv[:, zl * 128:(zl + 1) * 128] = jnp.where(low, pltpu.roll(even, 64, 1), odd)
    for m, ref in enumerate((gate, up, down)):
        for k in range(8):
            for c in range(2):
                start = k * 512 + c * 256
                ref[:, start:start + 256] = ffn[m, k, c].astype(F32)
    dp = lax.axis_index("dp")
    row = sums[pl.ds(lax.div(dp, 4), 1), :]
    shift = lax.rem(4 - lax.rem(dp, 4), 4) * 64
    attn_gain[...] = pltpu.roll(row[:, 0:256], shift, 1)[:, 0:64]
    ffn_gain[...] = pltpu.roll(row[:, 256:512], shift, 1)[:, 0:64]
    gain_q[...] = sums[0:1, 512:576]
    gain_k[...] = sums[0:1, 576:640]


def rows_block(*shape):
    n = len(shape)
    return pl.BlockSpec(shape, lambda t: (0,) * (n - 2) + (t, 0))


def whole_block(*shape):
    return pl.BlockSpec(shape, lambda t: (0,) * len(shape))


def finished(r):
    tall = rows_block(64, 2048)
    full, half, wide = (rows_block(32, n) for n in (1024, 256, 4096))
    one = whole_block(1, 64)
    sizes = [(64, 1024), (64, 256), (64, 256), (64, 1024)] + [(64, 4096)] * 3 + [(1, 64)] * 4
    return pl.pallas_call(
        finish_kernel,
        grid=(2,),
        out_shape=(
            jax.ShapeDtypeStruct((128, 2048), BF),
            jax.ShapeDtypeStruct((128, 2048), F32),
        )
        + tuple(jax.ShapeDtypeStruct(size, F32) for size in sizes),
        in_specs=[
            tall, tall, rows_block(2, 2, 32, 640), rows_block(3, 8, 2, 32, 256), whole_block(8, 640),
        ],
        out_specs=[tall, tall, full, half, half, full, wide, wide, wide, one, one, one, one],
        name="finished",
    )(r.out, r.dx, r.att_grads, r.ffn_grads, r.gain_sums)


def rotary_tables():
    position = np.arange(128, dtype=np.float64)[:, None]
    lane = np.arange(128)
    angle = position * THETA ** (-2.0 * (lane % 32) / 64.0)[None, :]
    sign = np.where(lane % 64 < 32, -1.0, 1.0)
    return np.cos(angle).astype(np.float32), (np.sin(angle) * sign).astype(np.float32)


def on_device(
    tokens, gain_attn, w_query, w_key, w_value, gain_query, gain_key, w_out, gain_ffn,
    w_gate, w_up, w_down, cotangent,
):
    cos, sin = (jnp.asarray(t) for t in rotary_tables())
    small = jnp.pad(jnp.stack([gain_attn, gain_ffn, gain_query, gain_key]), ((0, 12), (0, 64)))
    r = everything(
        tokens=tokens, cot=cotangent, small=small, cos=cos, sin=sin,
        wq=w_query, wk=w_key, wv=w_value, wo=w_out, wg=w_gate, wu=w_up, wd=w_down,
    )
    out, dx, gq, gk, gv, go, gate, up, down, attn, ffn, gain_q, gain_k = finished(r)
    attn, ffn, gain_q, gain_k = (v.reshape(64) for v in (attn, ffn, gain_q, gain_k))
    return out, dx, attn, gq, gk, gv, gain_q, gain_k, go, ffn, gate, up, down


def solution(mesh):
    return jax.shard_map(
        on_device,
        mesh=mesh,
        in_specs=(
            P("dp", None), P("dp"), P("dp", "head"), P("dp", "head"), P("dp", "head"),
            P(), P(), P("dp", "head"), P("dp"),
            P("dp", "tensor"), P("dp", "tensor"), P("dp", "tensor"), P("dp", None),
        ),
        out_specs=(
            P("dp", None), P("dp", None), P("dp"),
            P("dp", "head"), P("dp", "head"), P("dp", "head"),
            P(), P(), P("dp", "head"), P("dp"),
            P("dp", "tensor"), P("dp", "tensor"), P("dp", "tensor"),
        ),
        check_vma=False,
    )
```
